256 devices in a mesh: gx: 16 (over z, x_hi), gy: 4 (over y), gz: 4 (over x_lo, core).
Axes of the slice: x: 4 (x_hi: 2, x_lo: 2; x = x_hi * 2 + x_lo), y: 4, z: 8, core: 2. Of those that a mesh axis runs over, the one named last changes fastest.
Arguments:
- populations: float32 [19, 128, 32, 512], P(None, 'gx', 'gy', 'gz'), may hold values from 0.005 to 0.6, as said below
- design: float32 [128, 32, 512], P('gx', 'gy', 'gz'), may hold values from 0 to 1
- flags: int32 [128, 32, 512], P('gx', 'gy', 'gz'), may hold values from 0 to 3
- adjoint_seed: float32 [19, 128, 32, 512], P(None, 'gx', 'gy', 'gz'), may hold values from -120 to 120
Outputs:
- design_grad: float32 [128, 32, 512], P('gx', 'gy', 'gz')
- grad_rms: float32 [], replicated
The draws below stay inside these ranges and needn't reach their ends.
Inputs may be any that keep to these rules, and one draw needn't show every extreme that they name: `populations`: every population is positive.
All inputs are finite; a program needn't handle non-finite values.
Results may differ from the reference program's by a relative error of at most 0.0003.
Values sent between devices are 32-bit elements; how exact they have to be, the bound alone decides.
A program may use at most 64 MiB of HBM per device.

```python
import jax
import jax.numpy as jnp
from jax import lax

STEPS = 2
NX = 128
NY = 32
NZ = 512
N_GX = 16


lattice_velocities = [(0, 0, 0), (1, 0, 0), (-1, 0, 0), (0, 1, 0), (0, -1, 0), (0, 0, 1), (0, 0, -1), (1, 1, 0), (-1, -1, 0), (1, -1, 0), (-1, 1, 0), (1, 0, 1), (-1, 0, -1), (1, 0, -1), (-1, 0, 1), (0, 1, 1), (0, -1, -1), (0, 1, -1), (0, -1, 1)]


lattice_weights = [1.0 / 3.0] + [1.0 / 18.0] * 6 + [1.0 / 36.0] * 12


def draw_populations(key, part):
    keys = jax.random.split(jax.random.fold_in(key, 11), 5)
    low, high, reach, rough = (0.9, 1.1, 0.05, 0.2)
    shape = (NX, NY, NZ)
    density = jax.random.uniform(keys[0], shape, jnp.float32, low, high)
    speed_x = jax.random.uniform(keys[1], shape, jnp.float32, -reach, reach)
    speed_y = jax.random.uniform(keys[2], shape, jnp.float32, -reach, reach)
    speed_z = jax.random.uniform(keys[3], shape, jnp.float32, -reach, reach)
    noise = jax.random.uniform(keys[4], (19,) + shape, jnp.float32, -rough, rough)
    square = speed_x * speed_x + speed_y * speed_y + speed_z * speed_z
    layers = []
    for direction in range(19):
        projected = jnp.zeros(shape, jnp.float32)
        for component, speed_value in zip(lattice_velocities[direction], (speed_x, speed_y, speed_z)):
            if component != 0:
                projected = projected + component * speed_value
        layers.append(lattice_weights[direction] * density * (1.0 + 3.0 * projected + 4.5 * projected * projected - 1.5 * square))
    return (jnp.stack(layers) * (1.0 + noise)).astype(jnp.float32)


def draw_flags(key, part):
    ticket = jax.random.randint(jax.random.fold_in(key, 23), (NX, NY, NZ), 0, 100)
    kinds = jnp.where(ticket < 15, 1, jnp.where(ticket < 20, 2, jnp.where(ticket < 25, 3, 0)))
    return kinds.astype(jnp.int32)


def shard_levels(rng, shape, cuts, least, high):
    factor_of = 1.0
    for position, parts in cuts:
        draws = jax.random.uniform(jax.random.fold_in(jax.random.fold_in(rng, 6), position), (parts,), jnp.float32, least / len(cuts), high / len(cuts))
        factor_of = factor_of * jnp.repeat(jnp.exp(draws), shape[position] // parts).reshape((-1,) + (1,) * (len(shape) - 1 - position))
    return factor_of


def bell_draw(rng, extent, spread, limit, shards=(), kind=jnp.bfloat16):
    drawn = jax.random.normal(rng, extent, jnp.float32) * spread
    if len(shards) > 0:
        drawn = shard_levels(rng, extent, shards, -0.22, 0.18) * drawn
    return jnp.clip(drawn, min=-limit, max=limit).astype(kind)


def setup_inputs(seed: int = 0) -> dict:
    streams_of = jax.random.split(jax.random.key(seed), 5)
    return {
        "populations": draw_populations(jax.random.fold_in(streams_of[4], 71), 0),
        "design": jnp.clip(1.0 * jax.random.uniform(streams_of[1], (NX, NY, NZ), jnp.float32) ** shard_levels(streams_of[1], (NX, NY, NZ), ((0, 16), (1, 4), (2, 4)), -0.2, 0.2), 0.0, 1.0),
        "flags": draw_flags(jax.random.fold_in(streams_of[4], 71), 0),
        "adjoint_seed": bell_draw(streams_of[3], (19, NX, NY, NZ), 20.0, 120.0, ((1, 16), (2, 4), (3, 4)), jnp.float32),
    }


lattice_velocities = [(0, 0, 0), (1, 0, 0), (-1, 0, 0), (0, 1, 0), (0, -1, 0), (0, 0, 1), (0, 0, -1), (1, 1, 0), (-1, -1, 0), (1, -1, 0), (-1, 1, 0), (1, 0, 1), (-1, 0, -1), (1, 0, -1), (-1, 0, 1), (0, 1, 1), (0, -1, -1), (0, 1, -1), (0, -1, 1)]
opposite_index = [0, 2, 1, 4, 3, 6, 5, 8, 7, 10, 9, 12, 11, 14, 13, 16, 15, 18, 17]
lattice_weights = [1.0 / 3.0] + [1.0 / 18.0] * 6 + [1.0 / 36.0] * 12
hat_weights = [1.0, 2.0, 3.0, 4.0, 5.0, 4.0, 3.0, 2.0, 1.0]
relax_rate = 1.6
kappa_top = 0.5
inlet_speed = 0.05
norm_eps = 1e-06

def equilibrium(density, speed_x, speed_y, speed_z):
    square = speed_x * speed_x + speed_y * speed_y + speed_z * speed_z
    layers = []
    for direction in range(19):
        projected = 0.0
        for component, speed_value in zip(lattice_velocities[direction], (speed_x, speed_y, speed_z)):
            if component != 0:
                projected = projected + component * speed_value
        layers.append(lattice_weights[direction] * density * (1.0 + 3.0 * projected + 4.5 * projected * projected - 1.5 * square))
    return layers

def moment(state, dimension):
    total = 0.0
    for direction in range(19):
        component = lattice_velocities[direction][dimension]
        if component != 0:
            total = total + component * state[direction]
    return total

def collide(state, kappa, flags):
    density = lax.optimization_barrier(jnp.sum(state, axis=0))
    speed_x = moment(state, 0) / density
    speed_y = moment(state, 1) / density
    speed_z = moment(state, 2) / density
    balance = jnp.stack(equilibrium(density, speed_x, speed_y, speed_z))
    relax = jnp.where(flags == 3, 1.0, relax_rate).astype(state.dtype)
    relaxed = state - relax * (state - balance)
    flipped = jnp.stack([relaxed[other] for other in opposite_index])
    porous = (1.0 - kappa) * relaxed + kappa * flipped
    bounced = jnp.stack([state[other] for other in opposite_index])
    inflow = jnp.asarray(equilibrium(1.0, inlet_speed, 0.0, 0.0), dtype=state.dtype).reshape(19, 1, 1, 1)
    return jnp.where(flags == 1, bounced, jnp.where(flags == 2, inflow, porous))

def collide_slabs(state, kappa, flags):
    count = N_GX
    height = NX // count
    split_state = state.reshape(19, count, height, NY, NZ).transpose(1, 0, 2, 3, 4)
    split_kappa = kappa.reshape(count, height, NY, NZ)
    split_flags = flags.reshape(count, height, NY, NZ)
    single = jax.checkpoint(lambda items: collide(items[0], items[1], items[2]))
    result = lax.map(single, (split_state, split_kappa, split_flags))
    return result.transpose(1, 0, 2, 3, 4).reshape(19, NX, NY, NZ)

def stream(state):
    layers = []
    for direction in range(19):
        layers.append(jnp.roll(state[direction], shift=lattice_velocities[direction], axis=(0, 1, 2)))
    return jnp.stack(layers)

def sweep(padded, dimension):
    length = padded.shape[dimension] - 8
    total = 0.0
    for offset in range(9):
        total = total + hat_weights[offset] * lax.slice_in_dim(padded, offset, offset + length, axis=dimension)
    return total

def smooth(field):
    result = jnp.pad(field, 4)
    for dimension in range(3):
        result = sweep(result, dimension)
    return result

def weight_sums(count, whole):
    positions = jnp.arange(count, dtype=jnp.int32)
    total = jnp.zeros((count,), jnp.float32)
    for offset in range(9):
        moved = positions + (offset - 4)
        inside = jnp.logical_and(moved >= 0, moved < whole)
        total = total + hat_weights[offset] * inside.astype(jnp.float32)
    return total

def reference(populations, design, flags, adjoint_seed):
    totals = weight_sums(NX, NX)[:, None, None] * weight_sums(NY, NY)[None, :, None] * weight_sums(NZ, NZ)[None, None, :]
    totals = totals.astype(design.dtype)

    def objective(field):
        filtered = smooth(field) / totals
        kappa = kappa_top * (1.0 - filtered)
        state = populations
        for number in range(STEPS):
            state = stream(collide_slabs(state, kappa, flags))
        return jnp.sum(adjoint_seed * state)
    raw_grad = jax.grad(objective)(design)
    mean_square = jnp.sum(raw_grad * raw_grad) / (NX * NY * NZ)
    design_grad = raw_grad * lax.rsqrt(mean_square + norm_eps)
    return (design_grad, jnp.sqrt(mean_square))
```

```python
import functools

import jax
import jax.numpy as jnp
import numpy as np
from jax import lax
from jax.experimental import pallas as pl
from jax.experimental.pallas import tpu as pltpu
from jax.sharding import PartitionSpec as P

MESH = pl.DeviceIdType.MESH
F32 = jnp.float32
BF16 = jnp.bfloat16

velocities = [
    (0, 0, 0),
    (1, 0, 0),
    (-1, 0, 0),
    (0, 1, 0),
    (0, -1, 0),
    (0, 0, 1),
    (0, 0, -1),
    (1, 1, 0),
    (-1, -1, 0),
    (1, -1, 0),
    (-1, 1, 0),
    (1, 0, 1),
    (-1, 0, -1),
    (1, 0, -1),
    (-1, 0, 1),
    (0, 1, 1),
    (0, -1, -1),
    (0, 1, -1),
    (0, -1, 1),
]
opposite = [0, 2, 1, 4, 3, 6, 5, 8, 7, 10, 9, 12, 11, 14, 13, 16, 15, 18, 17]
pair_weights = [1.0 / 18.0] * 3 + [1.0 / 36.0] * 6
relax_rate = 1.6
inlet_speed = 0.05
norm_eps = 1e-06
FAR = 4096.0

crossing = {
    (0, 1): [1, 7, 9, 11, 13],
    (0, -1): [2, 8, 10, 12, 14],
    (1, 1): [3, 7, 10, 15, 17],
    (1, -1): [4, 8, 9, 16, 18],
    (2, 1): [5, 11, 14, 15, 18],
    (2, -1): [6, 12, 13, 16, 17],
}
side = {1: 0, -1: 1}
kind = {0: 0, 1: 1, -1: 2}

regions = {(0, 0): (0, 64)}
for order, where_ in enumerate([(-1, 0), (1, 0), (0, -1), (0, 1), (-1, -1), (-1, 1), (1, -1), (1, 1)]):
    regions[where_] = (64 + 40 * order, 40)

flows = [
    (a, b, c) for a in (1, -1, 0) for b in (1, -1, 0) for c in (1, -1, 0) if a or b or c
]
flow_index = {flow: number for number, flow in enumerate(flows)}


def lane_table():
    table = np.zeros((8, 384), np.float32)
    for (a, b), (start, rows) in regions.items():
        for r in range(rows):
            tile, sub = divmod(r, 8)
            if (a, b) == (0, 0):
                x, y = tile, sub
            elif b == 0:
                x, y = (tile - 5 if a < 0 else tile + 8), sub
            else:
                y = tile - 5 if b < 0 else tile + 8
                x = sub + 8 * a
            table[0, start + r] = x
            table[1, start + r] = y
    lanes = np.arange(384)
    table[2] = np.where(lanes < 128, lanes, np.where(lanes < 256, lanes - 129, lanes - 255))
    block = np.arange(256) // 16
    table[3, :256] = np.where(block < 10, block - 1, 3 * FAR)
    table[4, :256] = np.arange(256) % 16
    table[5, :128] = np.where(np.arange(128) < 24, np.arange(128) - 8, 3 * FAR)
    return table


def split(value):
    high = value.astype(BF16)
    return high, (value - high.astype(F32)).astype(BF16)


def left_dot(matrix, value):
    high, low = split(value)
    return jnp.dot(matrix, high, preferred_element_type=F32) + jnp.dot(
        matrix, low, preferred_element_type=F32
    )


def right_dot(value, matrix):
    high, low = split(value)
    return jnp.dot(high, matrix, preferred_element_type=F32) + jnp.dot(
        low, matrix, preferred_element_type=F32
    )


def right_dot_t(value, matrix):
    high, low = split(value)
    dims = (((1,), (1,)), ((), ()))
    return lax.dot_general(high, matrix, dims, preferred_element_type=F32) + lax.dot_general(
        low, matrix, dims, preferred_element_type=F32
    )


def triangle(n):
    return 0.5 * n * (n + 1.0)


def weight_total(position, count):
    position = jnp.where(position < 0, position + count, position)
    position = jnp.where(position > count - 1, position - count, position)
    return (
        25.0
        - triangle(jnp.maximum(0.0, 4.0 - position))
        - triangle(jnp.maximum(0.0, position - (count - 5.0)))
    )


def cut(value, last, low, high):
    return (
        value
        - jnp.where(value < 0, FAR, 0.0) * low
        + jnp.where(value > last, FAR, 0.0) * high
    )


def hat(difference):
    return jnp.maximum(0.0, 5.0 - jnp.abs(difference))


def add_all(terms):
    terms = list(terms)
    while len(terms) > 1:
        terms = [
            terms[n] + terms[n + 1] if n + 1 < len(terms) else terms[n]
            for n in range(0, len(terms), 2)
        ]
    return terms[0]


def project(c, vector):
    total = None
    for component, value in zip(c, vector):
        if component == 1:
            total = value if total is None else total + value
        elif component == -1:
            total = -value if total is None else total - value
    return total


def momentum(t):
    return (
        add_all([t[0], t[3] + t[4], t[5] + t[6]]),
        add_all([t[1], t[3] - t[4], t[7] + t[8]]),
        add_all([t[2], t[5] - t[6], t[7] - t[8]]),
    )


def cell_kinds(flags):
    omega = jnp.where(flags == 3, 1.0, relax_rate)
    solid = flags == 1
    inlet = flags == 2
    blocked = jnp.logical_or(solid, inlet)
    keep = 1.0 - omega
    even = jnp.where(solid, 1.0, jnp.where(inlet, 0.0, keep))
    odd = jnp.where(solid, -1.0, jnp.where(inlet, 0.0, keep))
    fluid_omega = jnp.where(blocked, 0.0, omega)
    return omega, keep, solid, inlet, blocked, even, odd, fluid_omega


def first_collision(f, flags):
    omega, keep, solid, inlet, blocked, even, odd, fluid_omega = cell_kinds(flags)
    rate = jnp.where(inlet, 1.0, fluid_omega)
    s = [f[2 * p + 1] + f[2 * p + 2] for p in range(9)]
    t = [f[2 * p + 1] - f[2 * p + 2] for p in range(9)]
    rho = jnp.where(inlet, 1.0, add_all([f[0]] + s))
    mx, my, mz = momentum(t)
    mx = jnp.where(inlet, inlet_speed, mx)
    my = jnp.where(inlet, 0.0, my)
    mz = jnp.where(inlet, 0.0, mz)
    inverse = 1.0 / rho
    base = rho - 1.5 * (mx * mx + my * my + mz * mz) * inverse
    bend = 4.5 * inverse
    half_even, half_odd = 0.5 * even, 0.5 * odd
    base_a, base_b = rate * pair_weights[0], rate * pair_weights[3]
    first = [even * f[0] + rate * (1.0 / 3.0) * base]
    slope = []
    for p in range(9):
        along = project(velocities[2 * p + 1], (mx, my, mz))
        weight = base_a if p < 3 else base_b
        symmetric = half_even * s[p] + weight * (base + bend * (along * along))
        skew = half_odd * t[p] + (3.0 * weight) * along
        first += [symmetric + skew, symmetric - skew]
        slope.append(jnp.where(blocked, 0.0, -2.0 * skew))
    return first, slope


def adjoint_collision(f, a, kappa, flags):
    omega, keep, solid, inlet, blocked, even, odd, fluid_omega = cell_kinds(flags)
    pass_back = 1.0 - 2.0 * kappa
    s = [f[2 * p + 1] + f[2 * p + 2] for p in range(9)]
    t = [f[2 * p + 1] - f[2 * p + 2] for p in range(9)]
    rho = add_all([f[0]] + s)
    mx, my, mz = momentum(t)
    inverse = 1.0 / rho
    ux, uy, uz = mx * inverse, my * inverse, mz * inverse
    even_a = [a[2 * p + 1] + a[2 * p + 2] for p in range(9)]
    odd_a = [a[2 * p + 1] - a[2 * p + 2] for p in range(9)]
    ws = [pair_weights[p] * even_a[p] for p in range(9)]
    wt = [pair_weights[p] * odd_a[p] for p in range(9)]
    b0 = add_all([(1.0 / 3.0) * a[0]] + ws)
    b1x, b1y, b1z = momentum(wt)
    bxx = add_all([ws[0], ws[3] + ws[4], ws[5] + ws[6]])
    byy = add_all([ws[1], ws[3] + ws[4], ws[7] + ws[8]])
    bzz = add_all([ws[2], ws[5] + ws[6], ws[7] + ws[8]])
    bxy, bxz, byz = ws[3] - ws[4], ws[5] - ws[6], ws[7] - ws[8]
    vx = bxx * ux + bxy * uy + bxz * uz
    vy = bxy * ux + byy * uy + byz * uz
    vz = bxz * ux + byz * uy + bzz * uz
    moved = 3.0 * (mx * b1x + my * b1y + mz * b1z)
    kept = add_all([odd_a[p] * t[p] for p in range(9)])
    slope = jnp.where(blocked, 0.0, -(keep * kept + 2.0 * omega * moved))
    usq = ux * ux + uy * uy + uz * uz
    to_rho = fluid_omega * (b0 * (1.0 + 1.5 * usq) - 4.5 * (ux * vx + uy * vy + uz * vz))
    back = 3.0 * pass_back
    gx = fluid_omega * (back * b1x + 9.0 * vx - 3.0 * ux * b0)
    gy = fluid_omega * (back * b1y + 9.0 * vy - 3.0 * uy * b0)
    gz = fluid_omega * (back * b1z + 9.0 * vz - 3.0 * uz * b0)
    half_even = 0.5 * even
    half_odd = 0.5 * jnp.where(blocked, odd, odd * pass_back)
    result = [even * a[0] + to_rho]
    for p in range(9):
        along = project(velocities[2 * p + 1], (gx, gy, gz))
        symmetric = half_even * even_a[p] + to_rho
        skew = half_odd * odd_a[p] + along
        result += [symmetric + skew, symmetric - skew]
    return result, slope


def aligned(index):
    return pl.multiple_of(index * 8, 8)


def kernel(
    sizes,
    pop_in,
    design_in,
    flags_in,
    seed_in,
    table_in,
    out_ref,
    rms_ref,
    pops,
    flags_v,
    table,
    first_v,
    slope_v,
    seed_v,
    field,
    x_send,
    x_recv,
    y_field,
    y_send,
    y_rows,
    xy_send,
    z_send,
    z_recv,
    z_pack,
    kappa_v,
    grad_v,
    spread,
    spread_recv,
    q_out,
    q_recv,
    ring_a,
    ring_b,
    big_l,
    big_l_wide,
    big_lt,
    rep_l,
    rep_l_wide,
    rep_lt,
    cross_x,
    cross_z,
    block_mask,
    row_scale,
    local_sem,
    send_sem,
    recv_sem,
):
    nx, ny, nz = sizes
    gx, gy, gz = lax.axis_index("gx"), lax.axis_index("gy"), lax.axis_index("gz")

    def device(move):
        return (
            lax.rem(gx + move[0] % nx, nx),
            lax.rem(gy + move[1] % ny, ny),
            lax.rem(gz + move[2] % nz, nz),
        )

    slab_moves = [(0, b, c) for b in range(ny) for c in range(nz) if b or c]
    slab_moves.sort(key=lambda m: -(min(m[1], ny - m[1]) + min(m[2], nz - m[2])))
    line_moves = [(a, 0, 2 * (a % 2)) for a in range(1, nx)]
    line_moves.sort(key=lambda m: -(min(m[0], nx - m[0]) + 2 * (m[0] % 2)))

    def key(move):
        return (move[0] % nx, move[1] % ny, move[2] % nz)

    partners = []
    for move in line_moves + flows + slab_moves:
        if key(move) not in partners:
            partners.append(key(move))
    barrier = pltpu.get_barrier_semaphore()
    for move in partners:
        pl.semaphore_signal(barrier, inc=1, device_id=device(move), device_id_type=MESH)

    loads = [
        pltpu.make_async_copy(table_in, table, local_sem.at[0]),
        pltpu.make_async_copy(pop_in, pops, local_sem.at[1]),
        pltpu.make_async_copy(flags_in, flags_v, local_sem.at[2]),
        pltpu.make_async_copy(seed_in, seed_v.at[:, pl.ds(8, 64), :], local_sem.at[3]),
        pltpu.make_async_copy(design_in, field.at[pl.ds(0, 64)], local_sem.at[4]),
    ]
    for load in loads:
        load.start()
    for load in loads:
        load.wait()

    lane = lax.broadcasted_iota(jnp.int32, (8, 128), 1)
    row = lax.broadcasted_iota(jnp.int32, (8, 128), 0)

    def own(k, j, rows):
        if k == 0:
            return first_v[j, rows, :]
        if k == 1:
            return slope_v[(j - 1) // 2, rows, :]
        return seed_v[opposite[j], rows, :]

    def start_step(x, carry):
        rows = pl.ds(aligned(x), 8)
        inner = pl.ds(aligned(x + 1), 8)
        first, slope = first_collision([pops[i, rows, :] for i in range(19)], flags_v[rows, :])
        for i in range(19):
            first_v[i, inner, :] = first[i]
        for p in range(9):
            slope_v[p, inner, :] = slope[p]
        packs = list(carry[:2])
        for n, sign in enumerate((1, -1)):
            edge = 127 if sign == 1 else 0
            for k in range(3):
                for s, j in enumerate(crossing[2, sign]):
                    tile = (
                        first[j]
                        if k == 0
                        else slope[(j - 1) // 2]
                        if k == 1
                        else seed_v[opposite[j], inner, :]
                    )
                    place = k * 40 + s * 8 + x
                    moved = pltpu.roll(tile, jnp.bitwise_and(place + 128 - edge, 127), 1)
                    packs[n] = jnp.where(lane == place, moved, packs[n])
        tile = field[rows, :]
        quad = carry[2]
        here = lax.shift_right_logical(lane, 4) == x
        part = jnp.bitwise_and(lane, 15)
        high = pltpu.roll(tile, jnp.bitwise_and(16 * x + 5, 127), 1)
        low = pltpu.roll(tile, jnp.bitwise_and(16 * x + 8, 127), 1)
        quad = jnp.where(jnp.logical_and(here, part < 5), high, quad)
        quad = jnp.where(
            jnp.logical_and(here, jnp.logical_and(part >= 8, part < 13)), low, quad
        )
        return packs[0], packs[1], quad

    blank = jnp.zeros((8, 128), F32)
    pack_up, pack_down, quad = lax.fori_loop(0, 8, start_step, (blank, blank, blank))
    z_send[0, 0] = quad
    z_send[1, 0] = quad
    z_send[0, 1] = pack_up
    z_send[1, 1] = pack_down
    for sign in (1, -1):
        n = side[sign]
        edge = 7 if sign == 1 else 0
        for k in range(3):
            for s, j in enumerate(crossing[0, sign]):
                x_send[n, 5 * k + s] = own(k, j, pl.ds(8 * (edge + 1), 8))
            for s, j in enumerate(crossing[1, sign]):
                y_send[n, 5 * k + s] = own(k, j, pl.ds(8 + edge, 8, stride=8))
        for r in range(5):
            y_field[n, pl.ds(8 * r, 8), :] = field[
                pl.ds(3 + r if sign == 1 else r, 8, stride=8), :
            ]
    diagonals = [(a, b) for a in (1, -1) for b in (1, -1)]
    for n, (a, b) in enumerate(diagonals):
        j = velocities.index((a, b, 0))
        xy_send[n] = y_field[side[b]]
        for k in range(3):
            at = (8 if a == 1 else 1) * 8 + (7 if b == 1 else 0)
            xy_send[n, pl.ds(k if a == 1 else 5 + k, 1), :] = own(k, j, pl.ds(at, 1))

    def one_if(condition):
        return jnp.where(condition, 1.0, 0.0).astype(F32)

    x_low, x_high = one_if(gx == 0), one_if(gx == nx - 1)
    y_low, y_high = one_if(gy == 0), one_if(gy == ny - 1)
    z_low, z_high = one_if(gz == 0), one_if(gz == nz - 1)
    lanes_x = cut(table[0:1, :], 7.0, x_low, x_high)
    lanes_y = cut(table[1:2, :], 7.0, y_low, y_high)
    lanes_z = cut(table[2:3, :], 127.0, z_low, z_high)
    blocks_x = cut(table[3:4, 0:256], 7.0, x_low, x_high)
    blocks_part = table[4:5, 0:256]
    stack_y = cut(table[5:6, 0:128], 7.0, y_low, y_high)
    lane_scale = 1.0 / weight_total(
        table[2:3, :] + (gz * 128).astype(F32), 128.0 * nz
    )

    def build_rows(t, carry):
        rows = pl.ds(pl.multiple_of(t * 16, 16), 16)
        index = lax.broadcasted_iota(jnp.int32, (16, 128), 0) + t * 16
        tile = lax.shift_right_logical(index, 3)
        late = jnp.where(tile >= 20, 2, jnp.where(tile >= 10, 1, 0))
        plane = tile - 10 * late
        x = (plane - 1).astype(F32)
        y = (jnp.bitwise_and(index, 7) - jnp.where(late == 1, 1, jnp.where(late == 2, -1, 0))).astype(F32)
        row_scale[rows, :] = 1.0 / (
            weight_total(x + (gx * 8).astype(F32), 8.0 * nx)
            * weight_total(y + (gy * 8).astype(F32), 8.0 * ny)
        )
        cut_x = cut(x, 7.0, x_low, x_high)
        cut_y = cut(y, 7.0, y_low, y_high)
        wide_x = jnp.concatenate([cut_x] * 3, axis=1)
        wide_y = jnp.concatenate([cut_y] * 3, axis=1)
        weights = hat(wide_x - lanes_x) * hat(wide_y - lanes_y)
        big_l_wide[rows, :] = weights
        big_l[rows, :] = weights.astype(BF16)
        repeated = hat(cut_y - stack_y)
        rep_l_wide[rows, :] = repeated
        rep_l[rows, :] = repeated.astype(BF16)
        block = lax.shift_right_logical(lax.broadcasted_iota(jnp.int32, (16, 256), 1), 4)
        block_mask[rows, :] = jnp.where(
            block == jnp.concatenate([plane] * 2, axis=1), 1.0, 0.0
        )
        return carry

    lax.fori_loop(0, 16, build_rows, 0)
    big_lt[...] = big_l_wide[...].T.astype(BF16)
    rep_lt[...] = rep_l_wide[...].T[0:32, :].astype(BF16)

    def build_cross(t, carry):
        rows = pl.ds(pl.multiple_of(t * 16, 16), 16)
        x = cut((t - 8).astype(F32), 7.0, x_low, x_high)
        same = lax.broadcasted_iota(jnp.int32, (16, 256), 0).astype(F32) == blocks_part
        cross_x[rows, :] = jnp.where(same, hat(x - blocks_x), 0.0).astype(BF16)
        return carry

    lax.fori_loop(0, 24, build_cross, 0)

    def build_z(t, carry):
        rows = pl.ds(pl.multiple_of(t * 16, 16), 16)
        index = lax.broadcasted_iota(jnp.int32, (16, 384), 0)
        inside = index + t * 16
        halo = jnp.where(
            index < 5,
            index - 5,
            jnp.where(jnp.logical_and(index >= 8, index < 13), index + 120, 100000),
        )
        z = cut(jnp.where(t < 8, inside, halo).astype(F32), 127.0, z_low, z_high)
        cross_z[rows, :] = hat(z - lanes_z).astype(BF16)
        return carry

    lax.fori_loop(0, 24, build_z, 0)
    grad_v[...] = jnp.zeros_like(grad_v)

    pl.semaphore_wait(barrier, len(partners))
    count = [0]
    started = []

    def send(source, target, move):
        n = count[0]
        count[0] += 1
        copy = pltpu.make_async_remote_copy(
            src_ref=source,
            dst_ref=target,
            send_sem=send_sem.at[n],
            recv_sem=recv_sem.at[n],
            device_id=device(move),
            device_id_type=MESH,
        )
        copy.start()
        started.append(copy)
        return copy

    def region(a, b):
        start, rows = regions[a, b]
        return pl.ds(start, rows)

    field_copies, fill_copies = [], []
    for n, (a, b) in enumerate(diagonals):
        field_copies.append(send(xy_send.at[n], field.at[region(-a, -b)], (a, b, 0)))
    for a in (1, -1):
        source = pl.ds(24, 40) if a == 1 else pl.ds(0, 40)
        field_copies.append(send(field.at[source], field.at[region(-a, 0)], (a, 0, 0)))
    for flow in flows:
        if flow[2] != 0:
            n = flow_index[flow]
            if flow[0] != 0 and flow[1] != 0:
                source, target = z_send.at[side[flow[2]], 0], z_recv.at[n, 0]
            else:
                source, target = z_send.at[side[flow[2]]], z_recv.at[n]
            field_copies.append(send(source, target, flow))
    for b in (1, -1):
        field_copies.append(send(y_field.at[side[b]], field.at[region(0, -b)], (0, b, 0)))
    for a in (1, -1):
        fill_copies.append(send(x_send.at[side[a]], x_recv.at[side[a]], (a, 0, 0)))
    for b in (1, -1):
        fill_copies.append(
            send(y_send.at[side[b]], y_rows.at[side[b], :, pl.ds(8, 8), :], (0, b, 0))
        )

    for copy in field_copies:
        copy.wait_recv()
    inner_xy = left_dot(big_l[...], field[...])
    part = jnp.bitwise_and(lane, 15)
    stacked = []
    for b in (-1, 0, 1):
        tiles = []
        for a in (-1, 0, 1):
            below = z_recv[flow_index[-a, -b, 1], 0]
            above = z_recv[flow_index[-a, -b, -1], 0]
            tiles.append(jnp.where(part < 8, below, above))
        stacked.append(jnp.concatenate(tiles, axis=1))
    stacked.append(jnp.zeros((8, 384), F32))
    halo_x = right_dot(jnp.concatenate(stacked, axis=0), cross_x[...])
    halo_x = jnp.concatenate([halo_x, jnp.zeros((96, 256), F32)], axis=0)
    halo_xy = left_dot(rep_l[...], halo_x) * block_mask[...]
    summed = right_dot(jnp.concatenate([inner_xy, halo_xy], axis=1), cross_z[...])
    scale_rows = jnp.concatenate([row_scale[...]] * 3, axis=1)
    kappa_v[...] = 0.5 * (1.0 - summed * scale_rows * lane_scale)

    for copy in fill_copies:
        copy.wait_recv()
    for sign in (1, -1):
        n = side[sign]
        rows = pl.ds(0, 8) if sign == 1 else pl.ds(72, 8)
        for s, j in enumerate(crossing[0, sign]):
            first_v[j, rows, :] = x_recv[n, s]
            slope_v[(j - 1) // 2, rows, :] = x_recv[n, 5 + s]
            seed_v[opposite[j], rows, :] = x_recv[n, 10 + s]
    for a, b in diagonals:
        j = velocities.index((a, b, 0))
        s = crossing[1, b].index(j)
        start = regions[-a, -b][0]
        for k in range(3):
            y_rows[side[b], 5 * k + s, pl.ds(7 if a == 1 else 16, 1), :] = field[
                pl.ds(start + (k if a == 1 else 5 + k), 1), :
            ]
    eighth = lax.shift_right_logical(lane, 3)
    slot = eighth - jnp.where(eighth >= 10, 10, jnp.where(eighth >= 5, 5, 0))
    step = jnp.bitwise_and(lane, 7)
    for sign in (1, -1):
        base = z_recv[flow_index[0, 0, sign], 1]
        total = base
        for s, j in enumerate(crossing[2, sign]):
            a, b, _ = velocities[j]
            if a != 0:
                corner = z_recv[flow_index[a, 0, sign], 1]
                if a == 1:
                    moved = jnp.where(step == 0, pltpu.roll(corner, 121, 1), pltpu.roll(base, 1, 1))
                else:
                    moved = jnp.where(step == 7, pltpu.roll(corner, 7, 1), pltpu.roll(base, 127, 1))
            elif b != 0:
                corner = z_recv[flow_index[0, b, sign], 1]
                if b == 1:
                    moved = pltpu.roll(jnp.where(row == 7, corner, base), 1, 0)
                else:
                    moved = pltpu.roll(jnp.where(row == 0, corner, base), 7, 0)
            else:
                continue
            total = jnp.where(slot == s, moved, total)
        z_pack[side[sign]] = total

    def plane_step(x, carry):
        def stream(k, j):
            a, b, c = velocities[j]
            tile = own(k, j, pl.ds(aligned(x + 1 - a), 8))
            if b != 0:
                s = crossing[1, b].index(j)
                line = y_rows[side[b], 5 * k + s, pl.ds(8 + x - a, 1), :]
                tile = jnp.where(
                    row == (0 if b == 1 else 7), line, pltpu.roll(tile, b % 8, 0)
                )
            if c != 0:
                s = crossing[2, c].index(j)
                edge = 0 if c == 1 else 127
                place = k * 40 + s * 8 + x
                column = pltpu.roll(
                    z_pack[side[c]], jnp.bitwise_and(256 + edge - place, 127), 1
                )
                tile = jnp.where(lane == edge, column, pltpu.roll(tile, c % 128, 1))
            return tile

        def spot(j):
            a, b, c = velocities[j]
            return (
                pl.ds(aligned(kind[b] * 10 + x + 1 - a), 8),
                pl.ds(128 * kind[c], 128),
            )

        center = pl.ds(aligned(x + 1), 8)
        flags = flags_v[pl.ds(aligned(x), 8), :]
        state, slopes = [first_v[0, center, :]], [None]
        weights = [seed_v[0, center, :]] + [None] * 18
        for j in range(1, 19):
            slope = stream(1, j)
            rows, lanes = spot(j)
            change = kappa_v[rows, lanes] * slope
            before = stream(0, j)
            state.append(before + change if j % 2 == 1 else before - change)
            slopes.append(slope)
            weights[opposite[j]] = stream(2, j)
        kappa = kappa_v[center, 0:128]
        back, here = adjoint_collision(state, weights, kappa, flags)
        grad_v[center, 0:128] += here
        for j in range(1, 19):
            rows, lanes = spot(j)
            if j % 2 == 1:
                grad_v[rows, lanes] += slopes[j] * back[j]
            else:
                grad_v[rows, lanes] -= slopes[j] * back[j]
        return carry

    lax.fori_loop(0, 8, plane_step, 0)

    scaled = grad_v[...] * (scale_rows * (-0.5 * lane_scale))
    summed = right_dot_t(scaled, cross_z[...])
    spread[...] = left_dot(big_lt[...], summed[:, 0:128])
    halo_x = left_dot(rep_lt[...], summed[:, 128:384] * block_mask[...])
    halo = right_dot_t(halo_x, cross_x[...])
    for b in range(3):
        for a in range(3):
            q_out[3 * b + a] = halo[8 * b : 8 * b + 8, 128 * a : 128 * a + 128]
    spread_copies = []
    for flow in flows:
        a, b, c = flow
        if c == 0:
            spread_copies.append(
                send(spread.at[region(a, b)], spread_recv.at[region(a, b)], flow)
            )
        else:
            spread_copies.append(
                send(q_out.at[3 * (b + 1) + a + 1], q_recv.at[flow_index[flow]], flow)
            )
    for copy in spread_copies:
        copy.wait_recv()
    spread[pl.ds(24, 40), :] += spread_recv[region(-1, 0), :]
    spread[pl.ds(0, 40), :] += spread_recv[region(1, 0), :]
    for b in (1, -1):
        lines = (
            spread_recv[region(0, b), :]
            + spread_recv[region(-1, b), :]
            + spread_recv[region(1, b), :]
        )
        for r in range(5):
            at = pl.ds(r if b == 1 else 3 + r, 8, stride=8)
            spread[at, :] += lines[8 * r : 8 * r + 8, :]
    up = add_all([q_recv[flow_index[a, b, 1]] for a in (-1, 0, 1) for b in (-1, 0, 1)])
    down = add_all([q_recv[flow_index[a, b, -1]] for a in (-1, 0, 1) for b in (-1, 0, 1)])
    squares = blank
    for x in range(8):
        first = pltpu.roll(up, (128 - 16 * x - 8) % 128, 1)
        last = pltpu.roll(down, (123 - 16 * x) % 128, 1)
        tile = spread[pl.ds(8 * x, 8), :]
        tile = tile + jnp.where(lane < 5, first, jnp.where(lane >= 123, last, 0.0))
        spread[pl.ds(8 * x, 8), :] = tile
        squares = squares + tile * tile

    mine = gy * nz + gz
    ring_a[mine] = jnp.sum(squares, axis=0, keepdims=True)
    ring_copies = [send(ring_a.at[mine], ring_a.at[mine], move) for move in slab_moves]
    for copy in ring_copies:
        copy.wait_recv()
    ring_b[gx] = jnp.sum(ring_a[...], axis=0)
    ring_copies = [send(ring_b.at[gx], ring_b.at[gx], move) for move in line_moves]
    for copy in ring_copies:
        copy.wait_recv()
    total = jnp.sum(jnp.sum(ring_b[...], axis=0), axis=1, keepdims=True)
    mean_square = total / (8192.0 * nx * ny * nz)
    out_ref[...] = spread[pl.ds(0, 64), :] * lax.rsqrt(mean_square + norm_eps)
    rms_ref[...] = jnp.sqrt(mean_square)
    for copy in started:
        copy.wait_send()


def solution(mesh):
    sizes = tuple(mesh.shape[name] for name in ("gx", "gy", "gz"))
    table = lane_table()
    copies = 4 + 2 + 18 + 2 + 2 + 2 + 26 + (sizes[1] * sizes[2] - 1) + (sizes[0] - 1)

    def body(populations, design, flags, adjoint_seed):
        anywhere = pl.BlockSpec(memory_space=pl.ANY)
        inside = pl.BlockSpec(memory_space=pltpu.VMEM)
        scratch = [
            pltpu.VMEM((19, 64, 128), F32),
            pltpu.VMEM((64, 128), jnp.int32),
            pltpu.VMEM((8, 384), F32),
            pltpu.VMEM((19, 80, 128), F32),
            pltpu.VMEM((9, 80, 128), F32),
            pltpu.VMEM((19, 80, 128), F32),
            pltpu.VMEM((384, 128), F32),
            pltpu.VMEM((2, 15, 8, 128), F32),
            pltpu.VMEM((2, 15, 8, 128), F32),
            pltpu.VMEM((2, 40, 128), F32),
            pltpu.VMEM((2, 15, 8, 128), F32),
            pltpu.VMEM((2, 15, 24, 128), F32),
            pltpu.VMEM((4, 40, 128), F32),
            pltpu.VMEM((2, 2, 8, 128), F32),
            pltpu.VMEM((26, 2, 8, 128), F32),
            pltpu.VMEM((2, 8, 128), F32),
            pltpu.VMEM((256, 384), F32),
            pltpu.VMEM((256, 384), F32),
            pltpu.VMEM((384, 128), F32),
            pltpu.VMEM((384, 128), F32),
            pltpu.VMEM((9, 8, 128), F32),
            pltpu.VMEM((26, 8, 128), F32),
            pltpu.VMEM((sizes[1] * sizes[2], 1, 128), F32),
            pltpu.VMEM((sizes[0], 1, 128), F32),
            pltpu.VMEM((256, 384), BF16),
            pltpu.VMEM((256, 384), F32),
            pltpu.VMEM((384, 256), BF16),
            pltpu.VMEM((256, 128), BF16),
            pltpu.VMEM((256, 128), F32),
            pltpu.VMEM((32, 256), BF16),
            pltpu.VMEM((384, 256), BF16),
            pltpu.VMEM((384, 384), BF16),
            pltpu.VMEM((256, 256), F32),
            pltpu.VMEM((256, 128), F32),
            pltpu.SemaphoreType.DMA((5,)),
            pltpu.SemaphoreType.DMA((copies,)),
            pltpu.SemaphoreType.DMA((copies,)),
        ]
        grad, rms = pl.pallas_call(
            functools.partial(kernel, sizes),
            out_shape=(
                jax.ShapeDtypeStruct((64, 128), F32),
                jax.ShapeDtypeStruct((1, 1), F32),
            ),
            in_specs=[anywhere] * 5,
            out_specs=(inside, inside),
            scratch_shapes=scratch,
            compiler_params=pltpu.CompilerParams(
                collective_id=0, has_side_effects=True, vmem_limit_bytes=56 * 1024 * 1024
            ),
        )(
            populations.reshape(19, 64, 128),
            design.reshape(64, 128),
            flags.reshape(64, 128),
            adjoint_seed.reshape(19, 64, 128),
            jnp.asarray(table),
        )
        return grad.reshape(8, 8, 128), rms.reshape(())

    return jax.shard_map(
        body,
        mesh=mesh,
        in_specs=(
            P(None, "gx", "gy", "gz"),
            P("gx", "gy", "gz"),
            P("gx", "gy", "gz"),
            P(None, "gx", "gy", "gz"),
        ),
        out_specs=(P("gx", "gy", "gz"), P()),
        check_vma=False,
    )
```

```python
import functools

import jax
import jax.numpy as jnp
from jax import lax
from jax.experimental import pallas as pl
from jax.experimental.pallas import tpu as pltpu
from jax.sharding import PartitionSpec as P

MESH = pl.DeviceIdType.MESH
F32 = jnp.float32
BF16 = jnp.bfloat16

velocities = [
    (0, 0, 0),
    (1, 0, 0),
    (-1, 0, 0),
    (0, 1, 0),
    (0, -1, 0),
    (0, 0, 1),
    (0, 0, -1),
    (1, 1, 0),
    (-1, -1, 0),
    (1, -1, 0),
    (-1, 1, 0),
    (1, 0, 1),
    (-1, 0, -1),
    (1, 0, -1),
    (-1, 0, 1),
    (0, 1, 1),
    (0, -1, -1),
    (0, 1, -1),
    (0, -1, 1),
]
opposite = [0, 2, 1, 4, 3, 6, 5, 8, 7, 10, 9, 12, 11, 14, 13, 16, 15, 18, 17]
pair_weights = [1.0 / 18.0] * 3 + [1.0 / 36.0] * 6
relax_rate = 1.6
inlet_speed = 0.05
norm_eps = 1e-06
FAR = 4096.0

crossing = {
    (0, 1): [1, 7, 9, 11, 13],
    (0, -1): [2, 8, 10, 12, 14],
    (1, 1): [3, 7, 10, 15, 17],
    (1, -1): [4, 8, 9, 16, 18],
    (2, 1): [5, 11, 14, 15, 18],
    (2, -1): [6, 12, 13, 16, 17],
}
side = {1: 0, -1: 1}
kind = {0: 0, 1: 1, -1: 2}

regions = {(0, 0): (0, 64)}
for order, where_ in enumerate([(-1, 0), (1, 0), (0, -1), (0, 1), (-1, -1), (-1, 1), (1, -1), (1, 1)]):
    regions[where_] = (64 + 40 * order, 40) if order < 4 else (96 + 32 * order, 32)

flows = [
    (a, b, c) for a in (1, -1, 0) for b in (1, -1, 0) for c in (1, -1, 0) if a or b or c
]
flow_index = {flow: number for number, flow in enumerate(flows)}


def outer_cells():
    r = lax.broadcasted_iota(jnp.int32, (1, 384), 1)
    low = jnp.bitwise_and(r, 7)
    tile = lax.shift_right_logical(r, 3)
    x = jnp.where(r < 64, tile, jnp.where(r < 104, tile - 13, jnp.where(r < 144, tile - 5, low)))
    y = jnp.where(r < 144, low, jnp.where(r < 184, tile - 23, tile - 15))
    k = jnp.bitwise_and(r, 31)
    edge = lax.shift_right_logical(r, 5) - 7
    part_y = lax.shift_right_logical(k * 13, 6)
    part_x = k - 5 * part_y
    edge_x = jnp.where(edge < 2, part_x - 5, part_x + 8)
    edge_y = jnp.where(jnp.bitwise_and(edge, 1) == 0, part_y - 5, part_y + 8)
    used = jnp.logical_and(k < 25, edge < 4)
    x = jnp.where(r < 224, x, jnp.where(used, edge_x, 12288))
    y = jnp.where(r < 224, y, jnp.where(used, edge_y, 12288))
    return x.astype(F32), y.astype(F32)


def split(value):
    high = value.astype(BF16)
    return high, (value - high.astype(F32)).astype(BF16)


def left_dot(matrix, value):
    high, low = split(value)
    return jnp.dot(matrix, high, preferred_element_type=F32) + jnp.dot(
        matrix, low, preferred_element_type=F32
    )


def right_dot(value, matrix):
    high, low = split(value)
    return jnp.dot(high, matrix, preferred_element_type=F32) + jnp.dot(
        low, matrix, preferred_element_type=F32
    )


def right_dot_t(value, matrix):
    high, low = split(value)
    dims = (((1,), (1,)), ((), ()))
    return lax.dot_general(high, matrix, dims, preferred_element_type=F32) + lax.dot_general(
        low, matrix, dims, preferred_element_type=F32
    )


def triangle(n):
    return 0.5 * n * (n + 1.0)


def weight_total(position, count):
    position = jnp.where(position < 0, position + count, position)
    position = jnp.where(position > count - 1, position - count, position)
    return (
        25.0
        - triangle(jnp.maximum(0.0, 4.0 - position))
        - triangle(jnp.maximum(0.0, position - (count - 5.0)))
    )


def cut(value, last, low, high):
    return (
        value
        - jnp.where(value < 0, FAR, 0.0) * low
        + jnp.where(value > last, FAR, 0.0) * high
    )


def hat(difference):
    return jnp.maximum(0.0, 5.0 - jnp.abs(difference))


def add_all(terms):
    terms = list(terms)
    while len(terms) > 1:
        terms = [
            terms[n] + terms[n + 1] if n + 1 < len(terms) else terms[n]
            for n in range(0, len(terms), 2)
        ]
    return terms[0]


def project(c, vector):
    total = None
    for component, value in zip(c, vector):
        if component == 1:
            total = value if total is None else total + value
        elif component == -1:
            total = -value if total is None else total - value
    return total


def momentum(t):
    return (
        add_all([t[0], t[3] + t[4], t[5] + t[6]]),
        add_all([t[1], t[3] - t[4], t[7] + t[8]]),
        add_all([t[2], t[5] - t[6], t[7] - t[8]]),
    )


def cell_kinds(flags):
    omega = jnp.where(flags == 3, 1.0, relax_rate)
    solid = flags == 1
    inlet = flags == 2
    blocked = jnp.logical_or(solid, inlet)
    keep = 1.0 - omega
    even = jnp.where(solid, 1.0, jnp.where(inlet, 0.0, keep))
    odd = jnp.where(solid, -1.0, jnp.where(inlet, 0.0, keep))
    fluid_omega = jnp.where(blocked, 0.0, omega)
    return omega, keep, solid, inlet, blocked, even, odd, fluid_omega


def first_collision(f, flags):
    omega, keep, solid, inlet, blocked, even, odd, fluid_omega = cell_kinds(flags)
    rate = jnp.where(inlet, 1.0, fluid_omega)
    s = [f[2 * p + 1] + f[2 * p + 2] for p in range(9)]
    t = [f[2 * p + 1] - f[2 * p + 2] for p in range(9)]
    rho = jnp.where(inlet, 1.0, add_all([f[0]] + s))
    mx, my, mz = momentum(t)
    mx = jnp.where(inlet, inlet_speed, mx)
    my = jnp.where(inlet, 0.0, my)
    mz = jnp.where(inlet, 0.0, mz)
    inverse = 1.0 / rho
    base = rho - 1.5 * (mx * mx + my * my + mz * mz) * inverse
    bend = 4.5 * inverse
    half_even, half_odd = 0.5 * even, 0.5 * odd
    base_a, base_b = rate * pair_weights[0], rate * pair_weights[3]
    first = [even * f[0] + rate * (1.0 / 3.0) * base]
    slope = []
    for p in range(9):
        along = project(velocities[2 * p + 1], (mx, my, mz))
        weight = base_a if p < 3 else base_b
        symmetric = half_even * s[p] + weight * (base + bend * (along * along))
        skew = half_odd * t[p] + (3.0 * weight) * along
        first += [symmetric + skew, symmetric - skew]
        slope.append(jnp.where(blocked, 0.0, -2.0 * skew))
    return first, slope


def adjoint_collision(f, a, kappa, flags):
    omega, keep, solid, inlet, blocked, even, odd, fluid_omega = cell_kinds(flags)
    pass_back = 1.0 - 2.0 * kappa
    s = [f[2 * p + 1] + f[2 * p + 2] for p in range(9)]
    t = [f[2 * p + 1] - f[2 * p + 2] for p in range(9)]
    rho = add_all([f[0]] + s)
    mx, my, mz = momentum(t)
    inverse = 1.0 / rho
    ux, uy, uz = mx * inverse, my * inverse, mz * inverse
    even_a = [a[2 * p + 1] + a[2 * p + 2] for p in range(9)]
    odd_a = [a[2 * p + 1] - a[2 * p + 2] for p in range(9)]
    ws = [pair_weights[p] * even_a[p] for p in range(9)]
    wt = [pair_weights[p] * odd_a[p] for p in range(9)]
    b0 = add_all([(1.0 / 3.0) * a[0]] + ws)
    b1x, b1y, b1z = momentum(wt)
    bxx = add_all([ws[0], ws[3] + ws[4], ws[5] + ws[6]])
    byy = add_all([ws[1], ws[3] + ws[4], ws[7] + ws[8]])
    bzz = add_all([ws[2], ws[5] + ws[6], ws[7] + ws[8]])
    bxy, bxz, byz = ws[3] - ws[4], ws[5] - ws[6], ws[7] - ws[8]
    vx = bxx * ux + bxy * uy + bxz * uz
    vy = bxy * ux + byy * uy + byz * uz
    vz = bxz * ux + byz * uy + bzz * uz
    moved = 3.0 * (mx * b1x + my * b1y + mz * b1z)
    kept = add_all([odd_a[p] * t[p] for p in range(9)])
    slope = jnp.where(blocked, 0.0, -(keep * kept + 2.0 * omega * moved))
    usq = ux * ux + uy * uy + uz * uz
    to_rho = fluid_omega * (b0 * (1.0 + 1.5 * usq) - 4.5 * (ux * vx + uy * vy + uz * vz))
    back = 3.0 * pass_back
    gx = fluid_omega * (back * b1x + 9.0 * vx - 3.0 * ux * b0)
    gy = fluid_omega * (back * b1y + 9.0 * vy - 3.0 * uy * b0)
    gz = fluid_omega * (back * b1z + 9.0 * vz - 3.0 * uz * b0)
    half_even = 0.5 * even
    half_odd = 0.5 * jnp.where(blocked, odd, odd * pass_back)
    result = [even * a[0] + to_rho]
    for p in range(9):
        along = project(velocities[2 * p + 1], (gx, gy, gz))
        symmetric = half_even * even_a[p] + to_rho
        skew = half_odd * odd_a[p] + along
        result += [symmetric + skew, symmetric - skew]
    return result, slope


def aligned(index):
    return pl.multiple_of(index * 8, 8)


def kernel(
    sizes,
    pop_in,
    design_in,
    flags_in,
    seed_in,
    out_ref,
    rms_ref,
    pops,
    flags_v,
    first_v,
    slope_v,
    seed_v,
    field,
    x_send,
    x_recv,
    y_field,
    y_send,
    y_rows,
    xy_send,
    mixed_send,
    z_send,
    z_recv,
    z_pack,
    kappa_v,
    grad_v,
    spread,
    spread_recv,
    q_out,
    q_recv,
    ring_a,
    ring_b,
    big_l,
    big_l_wide,
    big_lt,
    rep_l,
    rep_l_wide,
    rep_lt,
    cross_x,
    cross_z,
    block_mask,
    row_scale,
    local_sem,
    send_sem,
    recv_sem,
):
    nx, ny, nz = sizes
    gx, gy, gz = lax.axis_index("gx"), lax.axis_index("gy"), lax.axis_index("gz")

    def device(move):
        return (
            lax.rem(gx + move[0] % nx, nx),
            lax.rem(gy + move[1] % ny, ny),
            lax.rem(gz + move[2] % nz, nz),
        )

    slab_moves = [(0, b, c) for b in range(ny) for c in range(nz) if b or c]
    slab_moves.sort(key=lambda m: -(min(m[1], ny - m[1]) + min(m[2], nz - m[2])))
    line_moves = [(a, 0, 2 * (a % 2)) for a in range(1, nx)]
    line_moves.sort(key=lambda m: -(min(m[0], nx - m[0]) + 2 * (m[0] % 2)))

    def key(move):
        return (move[0] % nx, move[1] % ny, move[2] % nz)

    partners = []
    for move in line_moves + flows + slab_moves:
        if key(move) not in partners:
            partners.append(key(move))
    barrier = pltpu.get_barrier_semaphore()
    for move in partners:
        pl.semaphore_signal(barrier, inc=1, device_id=device(move), device_id_type=MESH)

    loads = [
        pltpu.make_async_copy(pop_in, pops, local_sem.at[1]),
        pltpu.make_async_copy(flags_in, flags_v, local_sem.at[2]),
        pltpu.make_async_copy(seed_in, seed_v.at[:, pl.ds(8, 64), :], local_sem.at[3]),
        pltpu.make_async_copy(design_in, field.at[pl.ds(0, 64)], local_sem.at[4]),
    ]
    for load in loads:
        load.start()
    for load in loads:
        load.wait()

    lane = lax.broadcasted_iota(jnp.int32, (8, 128), 1)
    row = lax.broadcasted_iota(jnp.int32, (8, 128), 0)

    def own(k, j, rows):
        if k == 0:
            return first_v[j, rows, :]
        if k == 1:
            return slope_v[(j - 1) // 2, rows, :]
        return seed_v[opposite[j], rows, :]

    def start_step(x, carry):
        rows = pl.ds(aligned(x), 8)
        inner = pl.ds(aligned(x + 1), 8)
        first, slope = first_collision([pops[i, rows, :] for i in range(19)], flags_v[rows, :])
        for i in range(19):
            first_v[i, inner, :] = first[i]
        for p in range(9):
            slope_v[p, inner, :] = slope[p]
        packs = list(carry[:2])
        for n, sign in enumerate((1, -1)):
            edge = 127 if sign == 1 else 0
            for k in range(3):
                for s, j in enumerate(crossing[2, sign]):
                    tile = (
                        first[j]
                        if k == 0
                        else slope[(j - 1) // 2]
                        if k == 1
                        else seed_v[opposite[j], inner, :]
                    )
                    place = k * 40 + s * 8 + x
                    moved = pltpu.roll(tile, jnp.bitwise_and(place + 128 - edge, 127), 1)
                    packs[n] = jnp.where(lane == place, moved, packs[n])
        tile = field[rows, :]
        quad = carry[2]
        here = lax.shift_right_logical(lane, 4) == x
        part = jnp.bitwise_and(lane, 15)
        high = pltpu.roll(tile, jnp.bitwise_and(16 * x + 5, 127), 1)
        low = pltpu.roll(tile, jnp.bitwise_and(16 * x + 8, 127), 1)
        quad = jnp.where(jnp.logical_and(here, part < 5), high, quad)
        quad = jnp.where(
            jnp.logical_and(here, jnp.logical_and(part >= 8, part < 13)), low, quad
        )
        return packs[0], packs[1], quad

    blank = jnp.zeros((8, 128), F32)
    pack_up, pack_down, quad = lax.fori_loop(0, 8, start_step, (blank, blank, blank))
    z_send[0, 0] = quad
    z_send[1, 0] = quad
    z_send[0, 1] = pack_up
    z_send[1, 1] = pack_down
    for sign in (1, -1):
        n = side[sign]
        edge = 7 if sign == 1 else 0
        for k in range(3):
            for s, j in enumerate(crossing[0, sign]):
                x_send[n, 5 * k + s] = own(k, j, pl.ds(8 * (edge + 1), 8))
            for s, j in enumerate(crossing[1, sign]):
                y_send[n, 5 * k + s] = own(k, j, pl.ds(8 + edge, 8, stride=8))
        for r in range(5):
            y_field[n, pl.ds(8 * r, 8), :] = field[
                pl.ds(3 + r if sign == 1 else r, 8, stride=8), :
            ]
    packs = {1: pack_up, -1: pack_down}
    mixed = [flow for flow in flows if flow[2] and (flow[0] == 0) != (flow[1] == 0)]
    for n, (a, b, c) in enumerate(mixed):
        if a:
            s = crossing[2, c].index(velocities.index((a, b, c)))
            tile = quad
            for k in range(3):
                free = k if a == 1 else 112 + k
                place = 40 * k + 8 * s + (7 if a == 1 else 0)
                tile = jnp.where(
                    lane == free, pltpu.roll(packs[c], (free - place) % 128, 1), tile
                )
        elif b == 1:
            tile = jnp.where(row == 0, pltpu.roll(packs[c], 1, 0), quad)
        else:
            tile = jnp.where(row == 7, pltpu.roll(packs[c], 7, 0), quad)
        mixed_send[n] = tile
    diagonals = [(a, b) for a in (1, -1) for b in (1, -1)]
    for n, (a, b) in enumerate(diagonals):
        j = velocities.index((a, b, 0))
        for r in range(5):
            at = (24 if a == 1 else 0) + (3 + r if b == 1 else r)
            xy_send[n, pl.ds(5 * r, 5), :] = field[pl.ds(at, 5, stride=8), :]
        for k in range(3):
            at = (8 if a == 1 else 1) * 8 + (7 if b == 1 else 0)
            xy_send[n, pl.ds(25 + k, 1), :] = own(k, j, pl.ds(at, 1))
        xy_send[n, pl.ds(28, 4), :] = jnp.zeros((4, 128), F32)

    pl.semaphore_wait(barrier, len(partners))
    count = [0]
    started = []

    def send(source, target, move):
        n = count[0]
        count[0] += 1
        copy = pltpu.make_async_remote_copy(
            src_ref=source,
            dst_ref=target,
            send_sem=send_sem.at[n],
            recv_sem=recv_sem.at[n],
            device_id=device(move),
            device_id_type=MESH,
        )
        copy.start()
        started.append(copy)
        return copy

    def region(a, b):
        start, rows = regions[a, b]
        return pl.ds(start, rows)

    field_copies, fill_copies = [], []
    for n, (a, b) in enumerate(diagonals):
        field_copies.append(send(xy_send.at[n], field.at[region(-a, -b)], (a, b, 0)))
    for a in (1, -1):
        source = pl.ds(24, 40) if a == 1 else pl.ds(0, 40)
        field_copies.append(send(field.at[source], field.at[region(-a, 0)], (a, 0, 0)))
    for flow in flows:
        if flow[2] != 0:
            n = flow_index[flow]
            if flow[0] != 0 and flow[1] != 0:
                source, target = z_send.at[side[flow[2]], 0], z_recv.at[n, 0]
            elif flow in mixed:
                source, target = mixed_send.at[mixed.index(flow)], z_recv.at[n, 0]
            else:
                source, target = z_send.at[side[flow[2]]], z_recv.at[n]
            field_copies.append(send(source, target, flow))
    for b in (1, -1):
        field_copies.append(send(y_field.at[side[b]], field.at[region(0, -b)], (0, b, 0)))
    for a in (1, -1):
        fill_copies.append(send(x_send.at[side[a]], x_recv.at[side[a]], (a, 0, 0)))
    for b in (1, -1):
        fill_copies.append(
            send(y_send.at[side[b]], y_rows.at[side[b], :, pl.ds(8, 8), :], (0, b, 0))
        )

    def one_if(condition):
        return jnp.where(condition, 1.0, 0.0).astype(F32)

    x_low, x_high = one_if(gx == 0), one_if(gx == nx - 1)
    y_low, y_high = one_if(gy == 0), one_if(gy == ny - 1)
    z_low, z_high = one_if(gz == 0), one_if(gz == nz - 1)
    lanes_x, lanes_y = outer_cells()
    lanes_x = cut(lanes_x, 7.0, x_low, x_high)
    lanes_y = cut(lanes_y, 7.0, y_low, y_high)
    wide = lax.broadcasted_iota(jnp.int32, (1, 384), 1)
    plain_z = jnp.where(wide < 128, wide, jnp.where(wide < 256, wide - 129, wide - 255)).astype(F32)
    lanes_z = cut(plain_z, 127.0, z_low, z_high)
    line = lax.broadcasted_iota(jnp.int32, (1, 128), 1)
    tenth = lax.shift_right_logical(line * 205, 11)
    part_ten = line - 10 * tenth
    blocks_x = cut(jnp.where(tenth < 10, tenth - 1, 12288).astype(F32), 7.0, x_low, x_high)
    blocks_part = jnp.where(part_ten < 5, part_ten, part_ten + 3)
    stack_y = cut(jnp.where(line < 24, line - 8, 12288).astype(F32), 7.0, y_low, y_high)
    lane_scale = 1.0 / weight_total(plain_z + (gz * 128).astype(F32), 128.0 * nz)

    def build_rows(t, carry):
        rows = pl.ds(pl.multiple_of(t * 16, 16), 16)
        index = lax.broadcasted_iota(jnp.int32, (16, 128), 0) + t * 16
        tile = lax.shift_right_logical(index, 3)
        late = jnp.where(tile >= 20, 2, jnp.where(tile >= 10, 1, 0))
        plane = tile - 10 * late
        x = (plane - 1).astype(F32)
        y = (jnp.bitwise_and(index, 7) - jnp.where(late == 1, 1, jnp.where(late == 2, -1, 0))).astype(F32)
        row_scale[rows, :] = 1.0 / (
            weight_total(x + (gx * 8).astype(F32), 8.0 * nx)
            * weight_total(y + (gy * 8).astype(F32), 8.0 * ny)
        )
        cut_x = cut(x, 7.0, x_low, x_high)
        cut_y = cut(y, 7.0, y_low, y_high)
        wide_x = jnp.concatenate([cut_x] * 3, axis=1)
        wide_y = jnp.concatenate([cut_y] * 3, axis=1)
        weights = hat(wide_x - lanes_x) * hat(wide_y - lanes_y)
        big_l_wide[rows, :] = weights
        big_l[rows, :] = weights.astype(BF16)
        repeated = hat(cut_y - stack_y)
        rep_l_wide[rows, :] = repeated
        rep_l[rows, :] = repeated.astype(BF16)
        block_mask[rows, :] = jnp.where(tenth == plane, 1.0, 0.0)
        return carry

    lax.fori_loop(0, 16, build_rows, 0)
    big_lt[...] = big_l_wide[...].T.astype(BF16)
    rep_lt[...] = rep_l_wide[...].T[0:32, :].astype(BF16)

    def build_cross(t, carry):
        rows = pl.ds(pl.multiple_of(t * 16, 16), 16)
        x = cut((t - 8).astype(F32), 7.0, x_low, x_high)
        same = lax.broadcasted_iota(jnp.int32, (16, 128), 0) == blocks_part
        cross_x[rows, :] = jnp.where(same, hat(x - blocks_x), 0.0).astype(BF16)
        return carry

    lax.fori_loop(0, 24, build_cross, 0)

    def build_z(t, carry):
        rows = pl.ds(pl.multiple_of(t * 16, 16), 16)
        index = lax.broadcasted_iota(jnp.int32, (16, 384), 0) + t * 16
        halo = index - 128
        halo = halo - 10 * lax.shift_right_logical(halo * 205, 11)
        halo = jnp.where(halo < 5, halo - 5, halo + 123)
        z = cut(jnp.where(index < 128, index, halo).astype(F32), 127.0, z_low, z_high)
        cross_z[rows, :] = hat(z - lanes_z).astype(BF16)
        return carry

    lax.fori_loop(0, 16, build_z, 0)
    grad_v[...] = jnp.zeros_like(grad_v)

    for copy in field_copies:
        copy.wait_recv()
    inner_xy = left_dot(big_l[...], field[...])
    part = jnp.bitwise_and(lane, 15)
    stacked = []
    for b in (-1, 0, 1):
        tiles = []
        for a in (-1, 0, 1):
            below = z_recv[flow_index[-a, -b, 1], 0]
            above = z_recv[flow_index[-a, -b, -1], 0]
            tiles.append(jnp.where(part < 8, below, above))
        stacked.append(jnp.concatenate(tiles, axis=1))
    stacked.append(jnp.zeros((8, 384), F32))
    halo_x = right_dot(jnp.concatenate(stacked, axis=0), cross_x[...])
    halo_x = jnp.concatenate([halo_x, jnp.zeros((96, 128), F32)], axis=0)
    halo_xy = left_dot(rep_l[...], halo_x) * block_mask[...]
    summed = right_dot(jnp.concatenate([inner_xy, halo_xy], axis=1), cross_z[...])
    scale_rows = jnp.concatenate([row_scale[...]] * 3, axis=1)
    kappa_v[...] = 0.5 * (1.0 - summed * scale_rows * lane_scale)

    for copy in fill_copies:
        copy.wait_recv()
    for sign in (1, -1):
        n = side[sign]
        rows = pl.ds(0, 8) if sign == 1 else pl.ds(72, 8)
        for s, j in enumerate(crossing[0, sign]):
            first_v[j, rows, :] = x_recv[n, s]
            slope_v[(j - 1) // 2, rows, :] = x_recv[n, 5 + s]
            seed_v[opposite[j], rows, :] = x_recv[n, 10 + s]
    for a, b in diagonals:
        j = velocities.index((a, b, 0))
        s = crossing[1, b].index(j)
        start = regions[-a, -b][0]
        for k in range(3):
            y_rows[side[b], 5 * k + s, pl.ds(7 if a == 1 else 16, 1), :] = field[
                pl.ds(start + 25 + k, 1), :
            ]
    eighth = lax.shift_right_logical(lane, 3)
    slot = eighth - jnp.where(eighth >= 10, 10, jnp.where(eighth >= 5, 5, 0))
    for sign in (1, -1):
        base = z_recv[flow_index[0, 0, sign], 1]
        total = base
        for s, j in enumerate(crossing[2, sign]):
            a, b, _ = velocities[j]
            if a != 0:
                corner = z_recv[flow_index[a, 0, sign], 0]
                moved = pltpu.roll(base, a % 128, 1)
                for k in range(3):
                    free = k if a == 1 else 112 + k
                    place = 40 * k + 8 * s + (0 if a == 1 else 7)
                    moved = jnp.where(
                        lane == place, pltpu.roll(corner, (place - free) % 128, 1), moved
                    )
            elif b != 0:
                corner = z_recv[flow_index[0, b, sign], 0]
                moved = jnp.where(row == (0 if b == 1 else 7), corner, pltpu.roll(base, b % 8, 0))
            else:
                continue
            total = jnp.where(slot == s, moved, total)
        z_pack[side[sign]] = total

    def plane_step(x, carry):
        def stream(k, j):
            a, b, c = velocities[j]
            tile = own(k, j, pl.ds(aligned(x + 1 - a), 8))
            if b != 0:
                s = crossing[1, b].index(j)
                line = y_rows[side[b], 5 * k + s, pl.ds(8 + x - a, 1), :]
                tile = jnp.where(
                    row == (0 if b == 1 else 7), line, pltpu.roll(tile, b % 8, 0)
                )
            if c != 0:
                s = crossing[2, c].index(j)
                edge = 0 if c == 1 else 127
                place = k * 40 + s * 8 + x
                column = pltpu.roll(
                    z_pack[side[c]], jnp.bitwise_and(256 + edge - place, 127), 1
                )
                tile = jnp.where(lane == edge, column, pltpu.roll(tile, c % 128, 1))
            return tile

        def spot(j):
            a, b, c = velocities[j]
            return (
                pl.ds(aligned(kind[b] * 10 + x + 1 - a), 8),
                pl.ds(128 * kind[c], 128),
            )

        center = pl.ds(aligned(x + 1), 8)
        flags = flags_v[pl.ds(aligned(x), 8), :]
        state, slopes = [first_v[0, center, :]], [None]
        weights = [seed_v[0, center, :]] + [None] * 18
        for j in range(1, 19):
            slope = stream(1, j)
            rows, lanes = spot(j)
            change = kappa_v[rows, lanes] * slope
            before = stream(0, j)
            state.append(before + change if j % 2 == 1 else before - change)
            slopes.append(slope)
            weights[opposite[j]] = stream(2, j)
        kappa = kappa_v[center, 0:128]
        back, here = adjoint_collision(state, weights, kappa, flags)
        grad_v[center, 0:128] += here
        for j in range(1, 19):
            rows, lanes = spot(j)
            if j % 2 == 1:
                grad_v[rows, lanes] += slopes[j] * back[j]
            else:
                grad_v[rows, lanes] -= slopes[j] * back[j]
        return carry

    lax.fori_loop(0, 8, plane_step, 0)

    scaled = grad_v[...] * (scale_rows * (-0.5 * lane_scale))
    summed = right_dot_t(scaled, cross_z[...])
    spread[...] = left_dot(big_lt[...], summed[:, 0:128])
    halo_x = left_dot(rep_lt[...], summed[:, 128:256] * block_mask[...])
    halo = right_dot_t(halo_x, cross_x[...])
    for b in range(3):
        for a in range(3):
            q_out[3 * b + a] = halo[8 * b : 8 * b + 8, 128 * a : 128 * a + 128]
    spread_copies = []
    for flow in flows:
        a, b, c = flow
        if c == 0:
            spread_copies.append(
                send(spread.at[region(a, b)], spread_recv.at[region(a, b)], flow)
            )
        else:
            spread_copies.append(
                send(q_out.at[3 * (b + 1) + a + 1], q_recv.at[flow_index[flow]], flow)
            )
    for copy in spread_copies:
        copy.wait_recv()
    spread[pl.ds(24, 40), :] += spread_recv[region(-1, 0), :]
    spread[pl.ds(0, 40), :] += spread_recv[region(1, 0), :]
    for b in (1, -1):
        for r in range(5):
            y = r if b == 1 else 3 + r
            spread[pl.ds(y, 8, stride=8), :] += spread_recv[
                pl.ds(regions[0, b][0] + 8 * r, 8), :
            ]
            for a in (1, -1):
                spread[pl.ds(y + (0 if a == 1 else 24), 5, stride=8), :] += spread_recv[
                    pl.ds(regions[a, b][0] + 5 * r, 5), :
                ]
    up = add_all([q_recv[flow_index[a, b, 1]] for a in (-1, 0, 1) for b in (-1, 0, 1)])
    down = add_all([q_recv[flow_index[a, b, -1]] for a in (-1, 0, 1) for b in (-1, 0, 1)])
    squares = blank
    for x in range(8):
        first = pltpu.roll(up, (128 - 16 * x - 8) % 128, 1)
        last = pltpu.roll(down, (123 - 16 * x) % 128, 1)
        tile = spread[pl.ds(8 * x, 8), :]
        tile = tile + jnp.where(lane < 5, first, jnp.where(lane >= 123, last, 0.0))
        spread[pl.ds(8 * x, 8), :] = tile
        squares = squares + tile * tile

    mine = gy * nz + gz
    ring_a[mine] = jnp.sum(squares, axis=0, keepdims=True)
    ring_copies = [send(ring_a.at[mine], ring_a.at[mine], move) for move in slab_moves]
    for copy in ring_copies:
        copy.wait_recv()
    ring_b[gx] = jnp.sum(ring_a[...], axis=0)
    ring_copies = [send(ring_b.at[gx], ring_b.at[gx], move) for move in line_moves]
    for copy in ring_copies:
        copy.wait_recv()
    total = jnp.sum(jnp.sum(ring_b[...], axis=0), axis=1, keepdims=True)
    mean_square = total / (8192.0 * nx * ny * nz)
    out_ref[...] = spread[pl.ds(0, 64), :] * lax.rsqrt(mean_square + norm_eps)
    rms_ref[...] = jnp.sqrt(mean_square)
    for copy in started:
        copy.wait_send()


def solution(mesh):
    sizes = tuple(mesh.shape[name] for name in ("gx", "gy", "gz"))
    copies = 4 + 2 + 18 + 2 + 2 + 2 + 26 + (sizes[1] * sizes[2] - 1) + (sizes[0] - 1)

    def body(populations, design, flags, adjoint_seed):
        anywhere = pl.BlockSpec(memory_space=pl.ANY)
        inside = pl.BlockSpec(memory_space=pltpu.VMEM)
        scratch = [
            pltpu.VMEM((19, 64, 128), F32),
            pltpu.VMEM((64, 128), jnp.int32),
            pltpu.VMEM((19, 80, 128), F32),
            pltpu.VMEM((9, 80, 128), F32),
            pltpu.VMEM((19, 80, 128), F32),
            pltpu.VMEM((384, 128), F32),
            pltpu.VMEM((2, 15, 8, 128), F32),
            pltpu.VMEM((2, 15, 8, 128), F32),
            pltpu.VMEM((2, 40, 128), F32),
            pltpu.VMEM((2, 15, 8, 128), F32),
            pltpu.VMEM((2, 15, 24, 128), F32),
            pltpu.VMEM((4, 32, 128), F32),
            pltpu.VMEM((8, 8, 128), F32),
            pltpu.VMEM((2, 2, 8, 128), F32),
            pltpu.VMEM((26, 2, 8, 128), F32),
            pltpu.VMEM((2, 8, 128), F32),
            pltpu.VMEM((256, 384), F32),
            pltpu.VMEM((256, 384), F32),
            pltpu.VMEM((384, 128), F32),
            pltpu.VMEM((384, 128), F32),
            pltpu.VMEM((9, 8, 128), F32),
            pltpu.VMEM((26, 8, 128), F32),
            pltpu.VMEM((sizes[1] * sizes[2], 1, 128), F32),
            pltpu.VMEM((sizes[0], 1, 128), F32),
            pltpu.VMEM((256, 384), BF16),
            pltpu.VMEM((256, 384), F32),
            pltpu.VMEM((384, 256), BF16),
            pltpu.VMEM((256, 128), BF16),
            pltpu.VMEM((256, 128), F32),
            pltpu.VMEM((32, 256), BF16),
            pltpu.VMEM((384, 128), BF16),
            pltpu.VMEM((256, 384), BF16),
            pltpu.VMEM((256, 128), F32),
            pltpu.VMEM((256, 128), F32),
            pltpu.SemaphoreType.DMA((5,)),
            pltpu.SemaphoreType.DMA((copies,)),
            pltpu.SemaphoreType.DMA((copies,)),
        ]
        grad, rms = pl.pallas_call(
            functools.partial(kernel, sizes),
            out_shape=(
                jax.ShapeDtypeStruct((64, 128), F32),
                jax.ShapeDtypeStruct((1, 1), F32),
            ),
            in_specs=[anywhere] * 4,
            out_specs=(inside, inside),
            scratch_shapes=scratch,
            compiler_params=pltpu.CompilerParams(
                collective_id=0, has_side_effects=True, vmem_limit_bytes=56491008
            ),
        )(
            populations.reshape(19, 64, 128),
            design.reshape(64, 128),
            flags.reshape(64, 128),
            adjoint_seed.reshape(19, 64, 128),
        )
        return grad.reshape(8, 8, 128), rms.reshape(())

    return jax.shard_map(
        body,
        mesh=mesh,
        in_specs=(
            P(None, "gx", "gy", "gz"),
            P("gx", "gy", "gz"),
            P("gx", "gy", "gz"),
            P(None, "gx", "gy", "gz"),
        ),
        out_specs=(P("gx", "gy", "gz"), P()),
        check_vma=False,
    )
```

```python
import functools

import jax
import jax.numpy as jnp
from jax import lax
from jax.experimental import pallas as pl
from jax.experimental.pallas import tpu as pltpu
from jax.sharding import PartitionSpec as P

MESH = pl.DeviceIdType.MESH
F32 = jnp.float32
BF16 = jnp.bfloat16

velocities = [
    (0, 0, 0),
    (1, 0, 0),
    (-1, 0, 0),
    (0, 1, 0),
    (0, -1, 0),
    (0, 0, 1),
    (0, 0, -1),
    (1, 1, 0),
    (-1, -1, 0),
    (1, -1, 0),
    (-1, 1, 0),
    (1, 0, 1),
    (-1, 0, -1),
    (1, 0, -1),
    (-1, 0, 1),
    (0, 1, 1),
    (0, -1, -1),
    (0, 1, -1),
    (0, -1, 1),
]
opposite = [0, 2, 1, 4, 3, 6, 5, 8, 7, 10, 9, 12, 11, 14, 13, 16, 15, 18, 17]
pair_weights = [1.0 / 18.0] * 3 + [1.0 / 36.0] * 6
relax_rate = 1.6
inlet_speed = 0.05
norm_eps = 1e-06
FAR = 4096.0

crossing = {
    (0, 1): [1, 7, 9, 11, 13],
    (0, -1): [2, 8, 10, 12, 14],
    (1, 1): [3, 7, 10, 15, 17],
    (1, -1): [4, 8, 9, 16, 18],
    (2, 1): [5, 11, 14, 15, 18],
    (2, -1): [6, 12, 13, 16, 17],
}
side = {1: 0, -1: 1}
kind = {0: 0, 1: 1, -1: 2}

regions = {(0, 0): (0, 64)}
for order, where_ in enumerate([(-1, 0), (1, 0), (0, -1), (0, 1), (-1, -1), (-1, 1), (1, -1), (1, 1)]):
    regions[where_] = (64 + 40 * order, 40) if order < 4 else (96 + 32 * order, 32)

flows = [
    (a, b, c) for a in (1, -1, 0) for b in (1, -1, 0) for c in (1, -1, 0) if a or b or c
]
flow_index = {flow: number for number, flow in enumerate(flows)}


def outer_cells():
    r = lax.broadcasted_iota(jnp.int32, (1, 384), 1)
    low = jnp.bitwise_and(r, 7)
    tile = lax.shift_right_logical(r, 3)
    x = jnp.where(r < 64, tile, jnp.where(r < 104, tile - 13, jnp.where(r < 144, tile - 5, low)))
    y = jnp.where(r < 144, low, jnp.where(r < 184, tile - 23, tile - 15))
    k = jnp.bitwise_and(r, 31)
    edge = lax.shift_right_logical(r, 5) - 7
    part_y = lax.shift_right_logical(k * 13, 6)
    part_x = k - 5 * part_y
    edge_x = jnp.where(edge < 2, part_x - 5, part_x + 8)
    edge_y = jnp.where(jnp.bitwise_and(edge, 1) == 0, part_y - 5, part_y + 8)
    used = jnp.logical_and(k < 25, edge < 4)
    x = jnp.where(r < 224, x, jnp.where(used, edge_x, 12288))
    y = jnp.where(r < 224, y, jnp.where(used, edge_y, 12288))
    return x.astype(F32), y.astype(F32)


def split(value):
    high = value.astype(BF16)
    return high, (value - high.astype(F32)).astype(BF16)


def left_dot(matrix, value):
    both = jnp.dot(
        matrix, jnp.concatenate(split(value), axis=1), preferred_element_type=F32
    )
    width = value.shape[1]
    return both[:, :width] + both[:, width:]


def right_dot(value, matrix):
    high, low = split(value)
    return jnp.dot(high, matrix, preferred_element_type=F32) + jnp.dot(
        low, matrix, preferred_element_type=F32
    )


def right_dot_t(value, matrix):
    high, low = split(value)
    dims = (((1,), (1,)), ((), ()))
    return lax.dot_general(high, matrix, dims, preferred_element_type=F32) + lax.dot_general(
        low, matrix, dims, preferred_element_type=F32
    )


def triangle(n):
    return 0.5 * n * (n + 1.0)


def weight_total(position, count):
    position = jnp.where(position < 0, position + count, position)
    position = jnp.where(position > count - 1, position - count, position)
    return (
        25.0
        - triangle(jnp.maximum(0.0, 4.0 - position))
        - triangle(jnp.maximum(0.0, position - (count - 5.0)))
    )


def cut(value, last, low, high):
    return (
        value
        - jnp.where(value < 0, FAR, 0.0) * low
        + jnp.where(value > last, FAR, 0.0) * high
    )


def hat(difference):
    return jnp.maximum(0.0, 5.0 - jnp.abs(difference))


def add_all(terms):
    terms = list(terms)
    while len(terms) > 1:
        terms = [
            terms[n] + terms[n + 1] if n + 1 < len(terms) else terms[n]
            for n in range(0, len(terms), 2)
        ]
    return terms[0]


def project(c, vector):
    total = None
    for component, value in zip(c, vector):
        if component == 1:
            total = value if total is None else total + value
        elif component == -1:
            total = -value if total is None else total - value
    return total


def momentum(t):
    return (
        add_all([t[0], t[3] + t[4], t[5] + t[6]]),
        add_all([t[1], t[3] - t[4], t[7] + t[8]]),
        add_all([t[2], t[5] - t[6], t[7] - t[8]]),
    )


def cell_kinds(flags):
    omega = jnp.where(flags == 3, 1.0, relax_rate)
    solid = flags == 1
    inlet = flags == 2
    blocked = jnp.logical_or(solid, inlet)
    keep = 1.0 - omega
    even = jnp.where(solid, 1.0, jnp.where(inlet, 0.0, keep))
    odd = jnp.where(solid, -1.0, jnp.where(inlet, 0.0, keep))
    fluid_omega = jnp.where(blocked, 0.0, omega)
    return omega, keep, solid, inlet, blocked, even, odd, fluid_omega


def first_collision(f, flags):
    omega, keep, solid, inlet, blocked, even, odd, fluid_omega = cell_kinds(flags)
    rate = jnp.where(inlet, 1.0, fluid_omega)
    s = [f[2 * p + 1] + f[2 * p + 2] for p in range(9)]
    t = [f[2 * p + 1] - f[2 * p + 2] for p in range(9)]
    rho = jnp.where(inlet, 1.0, add_all([f[0]] + s))
    mx, my, mz = momentum(t)
    mx = jnp.where(inlet, inlet_speed, mx)
    my = jnp.where(inlet, 0.0, my)
    mz = jnp.where(inlet, 0.0, mz)
    inverse = 1.0 / rho
    base = rho - 1.5 * (mx * mx + my * my + mz * mz) * inverse
    bend = 4.5 * inverse
    half_even, half_odd = 0.5 * even, 0.5 * odd
    base_a, base_b = rate * pair_weights[0], rate * pair_weights[3]
    first = [even * f[0] + rate * (1.0 / 3.0) * base]
    slope = []
    for p in range(9):
        along = project(velocities[2 * p + 1], (mx, my, mz))
        weight = base_a if p < 3 else base_b
        symmetric = half_even * s[p] + weight * (base + bend * (along * along))
        skew = half_odd * t[p] + (3.0 * weight) * along
        first += [symmetric + skew, symmetric - skew]
        slope.append(jnp.where(blocked, 0.0, -2.0 * skew))
    return first, slope


def adjoint_collision(f, a, kappa, flags):
    omega, keep, solid, inlet, blocked, even, odd, fluid_omega = cell_kinds(flags)
    pass_back = 1.0 - 2.0 * kappa
    s = [f[2 * p + 1] + f[2 * p + 2] for p in range(9)]
    t = [f[2 * p + 1] - f[2 * p + 2] for p in range(9)]
    rho = add_all([f[0]] + s)
    mx, my, mz = momentum(t)
    inverse = 1.0 / rho
    ux, uy, uz = mx * inverse, my * inverse, mz * inverse
    even_a = [a[2 * p + 1] + a[2 * p + 2] for p in range(9)]
    odd_a = [a[2 * p + 1] - a[2 * p + 2] for p in range(9)]
    ws = [pair_weights[p] * even_a[p] for p in range(9)]
    wt = [pair_weights[p] * odd_a[p] for p in range(9)]
    b0 = add_all([(1.0 / 3.0) * a[0]] + ws)
    b1x, b1y, b1z = momentum(wt)
    bxx = add_all([ws[0], ws[3] + ws[4], ws[5] + ws[6]])
    byy = add_all([ws[1], ws[3] + ws[4], ws[7] + ws[8]])
    bzz = add_all([ws[2], ws[5] + ws[6], ws[7] + ws[8]])
    bxy, bxz, byz = ws[3] - ws[4], ws[5] - ws[6], ws[7] - ws[8]
    vx = bxx * ux + bxy * uy + bxz * uz
    vy = bxy * ux + byy * uy + byz * uz
    vz = bxz * ux + byz * uy + bzz * uz
    moved = 3.0 * (mx * b1x + my * b1y + mz * b1z)
    kept = add_all([odd_a[p] * t[p] for p in range(9)])
    slope = jnp.where(blocked, 0.0, -(keep * kept + 2.0 * omega * moved))
    usq = ux * ux + uy * uy + uz * uz
    to_rho = fluid_omega * (b0 * (1.0 + 1.5 * usq) - 4.5 * (ux * vx + uy * vy + uz * vz))
    back = 3.0 * pass_back
    gx = fluid_omega * (back * b1x + 9.0 * vx - 3.0 * ux * b0)
    gy = fluid_omega * (back * b1y + 9.0 * vy - 3.0 * uy * b0)
    gz = fluid_omega * (back * b1z + 9.0 * vz - 3.0 * uz * b0)
    half_even = 0.5 * even
    half_odd = 0.5 * jnp.where(blocked, odd, odd * pass_back)
    result = [even * a[0] + to_rho]
    for p in range(9):
        along = project(velocities[2 * p + 1], (gx, gy, gz))
        symmetric = half_even * even_a[p] + to_rho
        skew = half_odd * odd_a[p] + along
        result += [symmetric + skew, symmetric - skew]
    return result, slope


def aligned(index):
    return pl.multiple_of(index * 8, 8)


def kernel(
    sizes,
    pop_in,
    design_in,
    flags_in,
    seed_in,
    out_ref,
    rms_ref,
    pops,
    flags_v,
    first_v,
    slope_v,
    seed_v,
    field,
    x_send,
    x_recv,
    y_field,
    y_send,
    y_rows,
    xy_send,
    mixed_send,
    z_send,
    z_recv,
    z_pack,
    kappa_v,
    grad_v,
    spread,
    spread_recv,
    q_out,
    q_recv,
    ring_a,
    ring_b,
    big_l,
    big_l_wide,
    big_lt,
    rep_l,
    rep_l_wide,
    rep_lt,
    cross_x,
    cross_z,
    block_mask,
    row_scale,
    local_sem,
    send_sem,
    recv_sem,
):
    nx, ny, nz = sizes
    gx, gy, gz = lax.axis_index("gx"), lax.axis_index("gy"), lax.axis_index("gz")

    def around(start, length):
        if length & (length - 1) == 0:
            return [jnp.bitwise_and(start + n, length - 1) for n in range(length)]
        return [lax.rem(start + n, length) for n in range(length)]

    place_x, place_y, place_z = around(gx, nx), around(gy, ny), around(gz, nz)

    def device(move):
        return place_x[move[0] % nx], place_y[move[1] % ny], place_z[move[2] % nz]

    slab_moves = [(0, b, c) for b in range(ny) for c in range(nz) if b or c]
    slab_moves.sort(key=lambda m: -(min(m[1], ny - m[1]) + min(m[2], nz - m[2])))
    line_moves = [(a, 0, 2 * (a % 2)) for a in range(1, nx)]
    line_moves.sort(key=lambda m: -(min(m[0], nx - m[0]) + 2 * (m[0] % 2)))

    def key(move):
        return (move[0] % nx, move[1] % ny, move[2] % nz)

    partners = []
    for move in line_moves + flows + slab_moves:
        if key(move) not in partners:
            partners.append(key(move))
    barrier = pltpu.get_barrier_semaphore()
    for move in partners:
        pl.semaphore_signal(barrier, inc=1, device_id=device(move), device_id_type=MESH)

    loads = [
        pltpu.make_async_copy(pop_in, pops, local_sem.at[1]),
        pltpu.make_async_copy(flags_in, flags_v, local_sem.at[2]),
        pltpu.make_async_copy(seed_in, seed_v.at[:, pl.ds(8, 64), :], local_sem.at[3]),
        pltpu.make_async_copy(design_in, field.at[pl.ds(0, 64)], local_sem.at[4]),
    ]
    for load in loads:
        load.start()
    for load in loads:
        load.wait()

    lane = lax.broadcasted_iota(jnp.int32, (8, 128), 1)
    row = lax.broadcasted_iota(jnp.int32, (8, 128), 0)

    def own(k, j, rows):
        if k == 0:
            return first_v[j, rows, :]
        if k == 1:
            return slope_v[(j - 1) // 2, rows, :]
        return seed_v[opposite[j], rows, :]

    def start_step(x, carry):
        rows = pl.ds(aligned(x), 8)
        inner = pl.ds(aligned(x + 1), 8)
        first, slope = first_collision([pops[i, rows, :] for i in range(19)], flags_v[rows, :])
        for i in range(19):
            first_v[i, inner, :] = first[i]
        for p in range(9):
            slope_v[p, inner, :] = slope[p]
        packs = list(carry[:2])
        for n, sign in enumerate((1, -1)):
            edge = 127 if sign == 1 else 0
            for k in range(3):
                for s, j in enumerate(crossing[2, sign]):
                    tile = (
                        first[j]
                        if k == 0
                        else slope[(j - 1) // 2]
                        if k == 1
                        else seed_v[opposite[j], inner, :]
                    )
                    place = k * 40 + s * 8 + x
                    moved = pltpu.roll(tile, jnp.bitwise_and(place + 128 - edge, 127), 1)
                    packs[n] = jnp.where(lane == place, moved, packs[n])
        tile = field[rows, :]
        quad = carry[2]
        here = lax.shift_right_logical(lane, 4) == x
        part = jnp.bitwise_and(lane, 15)
        high = pltpu.roll(tile, jnp.bitwise_and(16 * x + 5, 127), 1)
        low = pltpu.roll(tile, jnp.bitwise_and(16 * x + 8, 127), 1)
        quad = jnp.where(jnp.logical_and(here, part < 5), high, quad)
        quad = jnp.where(
            jnp.logical_and(here, jnp.logical_and(part >= 8, part < 13)), low, quad
        )
        return packs[0], packs[1], quad

    blank = jnp.zeros((8, 128), F32)
    pack_up, pack_down, quad = lax.fori_loop(0, 8, start_step, (blank, blank, blank), unroll=2)
    z_send[0, 0] = quad
    z_send[1, 0] = quad
    z_send[0, 1] = pack_up
    z_send[1, 1] = pack_down
    for sign in (1, -1):
        n = side[sign]
        edge = 7 if sign == 1 else 0
        for k in range(3):
            for s, j in enumerate(crossing[0, sign]):
                x_send[n, 5 * k + s] = own(k, j, pl.ds(8 * (edge + 1), 8))
            for s, j in enumerate(crossing[1, sign]):
                y_send[n, 5 * k + s] = own(k, j, pl.ds(8 + edge, 8, stride=8))
        for r in range(5):
            y_field[n, pl.ds(8 * r, 8), :] = field[
                pl.ds(3 + r if sign == 1 else r, 8, stride=8), :
            ]
    packs = {1: pack_up, -1: pack_down}
    mixed = [flow for flow in flows if flow[2] and (flow[0] == 0) != (flow[1] == 0)]
    for n, (a, b, c) in enumerate(mixed):
        if a:
            s = crossing[2, c].index(velocities.index((a, b, c)))
            tile = quad
            for k in range(3):
                free = k if a == 1 else 112 + k
                place = 40 * k + 8 * s + (7 if a == 1 else 0)
                tile = jnp.where(
                    lane == free, pltpu.roll(packs[c], (free - place) % 128, 1), tile
                )
        elif b == 1:
            tile = jnp.where(row == 0, pltpu.roll(packs[c], 1, 0), quad)
        else:
            tile = jnp.where(row == 7, pltpu.roll(packs[c], 7, 0), quad)
        mixed_send[n] = tile
    diagonals = [(a, b) for a in (1, -1) for b in (1, -1)]
    for n, (a, b) in enumerate(diagonals):
        j = velocities.index((a, b, 0))
        for r in range(5):
            at = (24 if a == 1 else 0) + (3 + r if b == 1 else r)
            xy_send[n, pl.ds(5 * r, 5), :] = field[pl.ds(at, 5, stride=8), :]
        for k in range(3):
            at = (8 if a == 1 else 1) * 8 + (7 if b == 1 else 0)
            xy_send[n, pl.ds(25 + k, 1), :] = own(k, j, pl.ds(at, 1))
        xy_send[n, pl.ds(28, 4), :] = jnp.zeros((4, 128), F32)

    pl.semaphore_wait(barrier, len(partners))
    count = [0]
    started = []

    def send(source, target, move):
        n = count[0]
        count[0] += 1
        copy = pltpu.make_async_remote_copy(
            src_ref=source,
            dst_ref=target,
            send_sem=send_sem.at[n],
            recv_sem=recv_sem.at[n],
            device_id=device(move),
            device_id_type=MESH,
        )
        copy.start()
        started.append(copy)
        return copy

    def region(a, b):
        start, rows = regions[a, b]
        return pl.ds(start, rows)

    field_copies, fill_copies = [], []
    for n, (a, b) in enumerate(diagonals):
        field_copies.append(send(xy_send.at[n], field.at[region(-a, -b)], (a, b, 0)))
    for a in (1, -1):
        source = pl.ds(24, 40) if a == 1 else pl.ds(0, 40)
        field_copies.append(send(field.at[source], field.at[region(-a, 0)], (a, 0, 0)))
    for flow in flows:
        if flow[2] != 0:
            n = flow_index[flow]
            if flow[0] != 0 and flow[1] != 0:
                source, target = z_send.at[side[flow[2]], 0], z_recv.at[n, 0]
            elif flow in mixed:
                source, target = mixed_send.at[mixed.index(flow)], z_recv.at[n, 0]
            else:
                source, target = z_send.at[side[flow[2]]], z_recv.at[n]
            field_copies.append(send(source, target, flow))
    for b in (1, -1):
        field_copies.append(send(y_field.at[side[b]], field.at[region(0, -b)], (0, b, 0)))
    for a in (1, -1):
        fill_copies.append(send(x_send.at[side[a]], x_recv.at[side[a]], (a, 0, 0)))
    for b in (1, -1):
        fill_copies.append(
            send(y_send.at[side[b]], y_rows.at[side[b], :, pl.ds(8, 8), :], (0, b, 0))
        )

    def one_if(condition):
        return jnp.where(condition, 1.0, 0.0).astype(F32)

    x_low, x_high = one_if(gx == 0), one_if(gx == nx - 1)
    y_low, y_high = one_if(gy == 0), one_if(gy == ny - 1)
    z_low, z_high = one_if(gz == 0), one_if(gz == nz - 1)
    lanes_x, lanes_y = outer_cells()
    lanes_x = cut(lanes_x, 7.0, x_low, x_high)
    lanes_y = cut(lanes_y, 7.0, y_low, y_high)
    wide = lax.broadcasted_iota(jnp.int32, (1, 384), 1)
    plain_z = jnp.where(wide < 128, wide, jnp.where(wide < 256, wide - 129, wide - 255)).astype(F32)
    lanes_z = cut(plain_z, 127.0, z_low, z_high)
    line = lax.broadcasted_iota(jnp.int32, (1, 128), 1)
    tenth = lax.shift_right_logical(line * 205, 11)
    part_ten = line - 10 * tenth
    blocks_x = cut(jnp.where(tenth < 10, tenth - 1, 12288).astype(F32), 7.0, x_low, x_high)
    blocks_part = jnp.where(part_ten < 5, part_ten, part_ten + 3)
    stack_y = cut(jnp.where(line < 24, line - 8, 12288).astype(F32), 7.0, y_low, y_high)
    lane_scale = 1.0 / weight_total(plain_z + (gz * 128).astype(F32), 128.0 * nz)

    def build_rows(t, carry):
        rows = pl.ds(pl.multiple_of(t * 16, 16), 16)
        index = lax.broadcasted_iota(jnp.int32, (16, 128), 0) + t * 16
        tile = lax.shift_right_logical(index, 3)
        late = jnp.where(tile >= 20, 2, jnp.where(tile >= 10, 1, 0))
        plane = tile - 10 * late
        x = (plane - 1).astype(F32)
        y = (jnp.bitwise_and(index, 7) - jnp.where(late == 1, 1, jnp.where(late == 2, -1, 0))).astype(F32)
        row_scale[rows, :] = 1.0 / (
            weight_total(x + (gx * 8).astype(F32), 8.0 * nx)
            * weight_total(y + (gy * 8).astype(F32), 8.0 * ny)
        )
        cut_x = cut(x, 7.0, x_low, x_high)
        cut_y = cut(y, 7.0, y_low, y_high)
        wide_x = jnp.concatenate([cut_x] * 3, axis=1)
        wide_y = jnp.concatenate([cut_y] * 3, axis=1)
        weights = hat(wide_x - lanes_x) * hat(wide_y - lanes_y)
        big_l_wide[rows, :] = weights
        big_l[rows, :] = weights.astype(BF16)
        repeated = hat(cut_y - stack_y)
        rep_l_wide[rows, :] = repeated
        rep_l[rows, :] = repeated.astype(BF16)
        block_mask[rows, :] = jnp.where(tenth == plane, 1.0, 0.0)
        return carry

    lax.fori_loop(0, 16, build_rows, 0)
    big_lt[...] = big_l_wide[...].T.astype(BF16)
    rep_lt[...] = rep_l_wide[...].T[0:32, :].astype(BF16)

    def build_cross(t, carry):
        rows = pl.ds(pl.multiple_of(t * 16, 16), 16)
        x = cut((t - 8).astype(F32), 7.0, x_low, x_high)
        same = lax.broadcasted_iota(jnp.int32, (16, 128), 0) == blocks_part
        cross_x[rows, :] = jnp.where(same, hat(x - blocks_x), 0.0).astype(BF16)
        return carry

    lax.fori_loop(0, 24, build_cross, 0)

    def build_z(t, carry):
        rows = pl.ds(pl.multiple_of(t * 16, 16), 16)
        index = lax.broadcasted_iota(jnp.int32, (16, 384), 0) + t * 16
        halo = index - 128
        halo = halo - 10 * lax.shift_right_logical(halo * 205, 11)
        halo = jnp.where(halo < 5, halo - 5, halo + 123)
        z = cut(jnp.where(index < 128, index, halo).astype(F32), 127.0, z_low, z_high)
        cross_z[rows, :] = hat(z - lanes_z).astype(BF16)
        return carry

    lax.fori_loop(0, 16, build_z, 0)
    grad_v[...] = jnp.zeros_like(grad_v)

    for copy in field_copies:
        copy.wait_recv()
    inner_xy = left_dot(big_l[...], field[...])
    part = jnp.bitwise_and(lane, 15)
    stacked = []
    for b in (-1, 0, 1):
        tiles = []
        for a in (-1, 0, 1):
            below = z_recv[flow_index[-a, -b, 1], 0]
            above = z_recv[flow_index[-a, -b, -1], 0]
            tiles.append(jnp.where(part < 8, below, above))
        stacked.append(jnp.concatenate(tiles, axis=1))
    stacked.append(jnp.zeros((8, 384), F32))
    halo_x = right_dot(jnp.concatenate(stacked, axis=0), cross_x[...])
    halo_x = jnp.concatenate([halo_x, jnp.zeros((96, 128), F32)], axis=0)
    halo_xy = left_dot(rep_l[...], halo_x) * block_mask[...]
    summed = right_dot(jnp.concatenate([inner_xy, halo_xy], axis=1), cross_z[...])
    scale_rows = jnp.concatenate([row_scale[...]] * 3, axis=1)
    kappa_v[...] = 0.5 * (1.0 - summed * scale_rows * lane_scale)

    for copy in fill_copies[2:]:
        copy.wait_recv()
    eighth = lax.shift_right_logical(lane, 3)
    slot = eighth - jnp.where(eighth >= 10, 10, jnp.where(eighth >= 5, 5, 0))
    for sign in (1, -1):
        base = z_recv[flow_index[0, 0, sign], 1]
        total = base
        for s, j in enumerate(crossing[2, sign]):
            a, b, _ = velocities[j]
            if a != 0:
                corner = z_recv[flow_index[a, 0, sign], 0]
                moved = pltpu.roll(base, a % 128, 1)
                for k in range(3):
                    free = k if a == 1 else 112 + k
                    place = 40 * k + 8 * s + (0 if a == 1 else 7)
                    moved = jnp.where(
                        lane == place, pltpu.roll(corner, (place - free) % 128, 1), moved
                    )
            elif b != 0:
                corner = z_recv[flow_index[0, b, sign], 0]
                moved = jnp.where(row == (0 if b == 1 else 7), corner, pltpu.roll(base, b % 8, 0))
            else:
                continue
            total = jnp.where(slot == s, moved, total)
        z_pack[side[sign]] = total

    def plane_step(x, carry):
        def stream(k, j):
            a, b, c = velocities[j]
            tile = own(k, j, pl.ds(aligned(x + 1 - a), 8))
            if b != 0:
                s = crossing[1, b].index(j)
                line = y_rows[side[b], 5 * k + s, pl.ds(8 + x - a, 1), :]
                tile = jnp.where(
                    row == (0 if b == 1 else 7), line, pltpu.roll(tile, b % 8, 0)
                )
            if c != 0:
                s = crossing[2, c].index(j)
                edge = 0 if c == 1 else 127
                place = k * 40 + s * 8 + x
                column = pltpu.roll(
                    z_pack[side[c]], jnp.bitwise_and(256 + edge - place, 127), 1
                )
                tile = jnp.where(lane == edge, column, pltpu.roll(tile, c % 128, 1))
            return tile

        def spot(j):
            a, b, c = velocities[j]
            return (
                pl.ds(aligned(kind[b] * 10 + x + 1 - a), 8),
                pl.ds(128 * kind[c], 128),
            )

        center = pl.ds(aligned(x + 1), 8)
        flags = flags_v[pl.ds(aligned(x), 8), :]
        state, slopes = [first_v[0, center, :]], [None]
        weights = [seed_v[0, center, :]] + [None] * 18
        for j in range(1, 19):
            slope = stream(1, j)
            rows, lanes = spot(j)
            change = kappa_v[rows, lanes] * slope
            before = stream(0, j)
            state.append(before + change if j % 2 == 1 else before - change)
            slopes.append(slope)
            weights[opposite[j]] = stream(2, j)
        kappa = kappa_v[center, 0:128]
        back, here = adjoint_collision(state, weights, kappa, flags)
        grad_v[center, 0:128] += here
        for j in range(1, 19):
            rows, lanes = spot(j)
            if j % 2 == 1:
                grad_v[rows, lanes] += slopes[j] * back[j]
            else:
                grad_v[rows, lanes] -= slopes[j] * back[j]
        return carry

    lax.fori_loop(1, 7, plane_step, 0, unroll=6)
    for copy in fill_copies[:2]:
        copy.wait_recv()
    for sign in (1, -1):
        n = side[sign]
        rows = pl.ds(0, 8) if sign == 1 else pl.ds(72, 8)
        for s, j in enumerate(crossing[0, sign]):
            first_v[j, rows, :] = x_recv[n, s]
            slope_v[(j - 1) // 2, rows, :] = x_recv[n, 5 + s]
            seed_v[opposite[j], rows, :] = x_recv[n, 10 + s]
    for a, b in diagonals:
        j = velocities.index((a, b, 0))
        s = crossing[1, b].index(j)
        start = regions[-a, -b][0]
        for k in range(3):
            y_rows[side[b], 5 * k + s, pl.ds(7 if a == 1 else 16, 1), :] = field[
                pl.ds(start + 25 + k, 1), :
            ]
    lax.fori_loop(0, 2, lambda n, carry: plane_step(7 * n, carry), 0, unroll=2)

    scaled = grad_v[...] * (scale_rows * (-0.5 * lane_scale))
    summed = right_dot_t(scaled, cross_z[...])
    spread[...] = left_dot(big_lt[...], summed[:, 0:128])
    halo_x = left_dot(rep_lt[...], summed[:, 128:256] * block_mask[...])
    halo = right_dot_t(halo_x, cross_x[...])
    for b in range(3):
        for a in range(3):
            q_out[3 * b + a] = halo[8 * b : 8 * b + 8, 128 * a : 128 * a + 128]
    spread_copies = []
    for flow in flows:
        a, b, c = flow
        if c == 0:
            spread_copies.append(
                send(spread.at[region(a, b)], spread_recv.at[region(a, b)], flow)
            )
        else:
            spread_copies.append(
                send(q_out.at[3 * (b + 1) + a + 1], q_recv.at[flow_index[flow]], flow)
            )
    for copy in spread_copies:
        copy.wait_recv()
    spread[pl.ds(24, 40), :] += spread_recv[region(-1, 0), :]
    spread[pl.ds(0, 40), :] += spread_recv[region(1, 0), :]
    for b in (1, -1):
        for r in range(5):
            y = r if b == 1 else 3 + r
            spread[pl.ds(y, 8, stride=8), :] += spread_recv[
                pl.ds(regions[0, b][0] + 8 * r, 8), :
            ]
            for a in (1, -1):
                spread[pl.ds(y + (0 if a == 1 else 24), 5, stride=8), :] += spread_recv[
                    pl.ds(regions[a, b][0] + 5 * r, 5), :
                ]
    up = add_all([q_recv[flow_index[a, b, 1]] for a in (-1, 0, 1) for b in (-1, 0, 1)])
    down = add_all([q_recv[flow_index[a, b, -1]] for a in (-1, 0, 1) for b in (-1, 0, 1)])
    squares = blank
    for x in range(8):
        first = pltpu.roll(up, (128 - 16 * x - 8) % 128, 1)
        last = pltpu.roll(down, (123 - 16 * x) % 128, 1)
        tile = spread[pl.ds(8 * x, 8), :]
        tile = tile + jnp.where(lane < 5, first, jnp.where(lane >= 123, last, 0.0))
        spread[pl.ds(8 * x, 8), :] = tile
        squares = squares + tile * tile

    mine = gy * nz + gz
    ring_a[mine] = jnp.sum(squares, axis=0, keepdims=True)
    ring_copies = [send(ring_a.at[mine], ring_a.at[mine], move) for move in slab_moves]
    for copy in ring_copies:
        copy.wait_recv()
    ring_b[gx] = jnp.sum(ring_a[...], axis=0)
    ring_copies = [send(ring_b.at[gx], ring_b.at[gx], move) for move in line_moves]
    for copy in ring_copies:
        copy.wait_recv()
    total = jnp.sum(jnp.sum(ring_b[...], axis=0), axis=1, keepdims=True)
    mean_square = total / (8192.0 * nx * ny * nz)
    out_ref[...] = spread[pl.ds(0, 64), :]
    rms_ref[...] = jnp.broadcast_to(jnp.sqrt(mean_square), (64, 128))
    for copy in started:
        copy.wait_send()


def solution(mesh):
    sizes = tuple(mesh.shape[name] for name in ("gx", "gy", "gz"))
    copies = 4 + 2 + 18 + 2 + 2 + 2 + 26 + (sizes[1] * sizes[2] - 1) + (sizes[0] - 1)

    def body(populations, design, flags, adjoint_seed):
        anywhere = pl.BlockSpec(memory_space=pl.ANY)
        inside = pl.BlockSpec(memory_space=pltpu.VMEM)
        scratch = [
            pltpu.VMEM((19, 64, 128), F32),
            pltpu.VMEM((64, 128), jnp.int32),
            pltpu.VMEM((19, 80, 128), F32),
            pltpu.VMEM((9, 80, 128), F32),
            pltpu.VMEM((19, 80, 128), F32),
            pltpu.VMEM((384, 128), F32),
            pltpu.VMEM((2, 15, 8, 128), F32),
            pltpu.VMEM((2, 15, 8, 128), F32),
            pltpu.VMEM((2, 40, 128), F32),
            pltpu.VMEM((2, 15, 8, 128), F32),
            pltpu.VMEM((2, 15, 24, 128), F32),
            pltpu.VMEM((4, 32, 128), F32),
            pltpu.VMEM((8, 8, 128), F32),
            pltpu.VMEM((2, 2, 8, 128), F32),
            pltpu.VMEM((26, 2, 8, 128), F32),
            pltpu.VMEM((2, 8, 128), F32),
            pltpu.VMEM((256, 384), F32),
            pltpu.VMEM((256, 384), F32),
            pltpu.VMEM((384, 128), F32),
            pltpu.VMEM((384, 128), F32),
            pltpu.VMEM((9, 8, 128), F32),
            pltpu.VMEM((26, 8, 128), F32),
            pltpu.VMEM((sizes[1] * sizes[2], 1, 128), F32),
            pltpu.VMEM((sizes[0], 1, 128), F32),
            pltpu.VMEM((256, 384), BF16),
            pltpu.VMEM((256, 384), F32),
            pltpu.VMEM((384, 256), BF16),
            pltpu.VMEM((256, 128), BF16),
            pltpu.VMEM((256, 128), F32),
            pltpu.VMEM((32, 256), BF16),
            pltpu.VMEM((384, 128), BF16),
            pltpu.VMEM((256, 384), BF16),
            pltpu.VMEM((256, 128), F32),
            pltpu.VMEM((256, 128), F32),
            pltpu.SemaphoreType.DMA((5,)),
            pltpu.SemaphoreType.DMA((copies,)),
            pltpu.SemaphoreType.DMA((copies,)),
        ]
        grad, rms = pl.pallas_call(
            functools.partial(kernel, sizes),
            out_shape=(
                jax.ShapeDtypeStruct((64, 128), F32),
                jax.ShapeDtypeStruct((64, 128), F32),
            ),
            in_specs=[anywhere] * 4,
            out_specs=(inside, inside),
            scratch_shapes=scratch,
            compiler_params=pltpu.CompilerParams(
                collective_id=0, has_side_effects=True, vmem_limit_bytes=56470528
            ),
        )(
            populations.reshape(19, 64, 128),
            design.reshape(64, 128),
            flags.reshape(64, 128),
            adjoint_seed.reshape(19, 64, 128),
        )
        return grad.reshape(8, 8, 128) * lax.rsqrt(rms.reshape(8, 8, 128) * rms.reshape(8, 8, 128) + norm_eps), jnp.max(rms.reshape(8, 8, 128))

    return jax.shard_map(
        body,
        mesh=mesh,
        in_specs=(
            P(None, "gx", "gy", "gz"),
            P("gx", "gy", "gz"),
            P("gx", "gy", "gz"),
            P(None, "gx", "gy", "gz"),
        ),
        out_specs=(P("gx", "gy", "gz"), P()),
        check_vma=False,
    )
```

```python
import functools

import jax
import jax.numpy as jnp
from jax import lax
from jax.experimental import pallas as pl
from jax.experimental.pallas import tpu as pltpu
from jax.sharding import PartitionSpec as P

MESH = pl.DeviceIdType.MESH
F32 = jnp.float32
BF16 = jnp.bfloat16

velocities = [
    (0, 0, 0),
    (1, 0, 0),
    (-1, 0, 0),
    (0, 1, 0),
    (0, -1, 0),
    (0, 0, 1),
    (0, 0, -1),
    (1, 1, 0),
    (-1, -1, 0),
    (1, -1, 0),
    (-1, 1, 0),
    (1, 0, 1),
    (-1, 0, -1),
    (1, 0, -1),
    (-1, 0, 1),
    (0, 1, 1),
    (0, -1, -1),
    (0, 1, -1),
    (0, -1, 1),
]
opposite = [0, 2, 1, 4, 3, 6, 5, 8, 7, 10, 9, 12, 11, 14, 13, 16, 15, 18, 17]
pair_weights = [1.0 / 18.0] * 3 + [1.0 / 36.0] * 6
relax_rate = 1.6
inlet_speed = 0.05
norm_eps = 1e-06
FAR = 4096.0

crossing = {
    (0, 1): [1, 7, 9, 11, 13],
    (0, -1): [2, 8, 10, 12, 14],
    (1, 1): [3, 7, 10, 15, 17],
    (1, -1): [4, 8, 9, 16, 18],
    (2, 1): [5, 11, 14, 15, 18],
    (2, -1): [6, 12, 13, 16, 17],
}
side = {1: 0, -1: 1}
kind = {0: 0, 1: 1, -1: 2}

regions = {(0, 0): (0, 64)}
for order, where_ in enumerate([(-1, 0), (1, 0), (0, -1), (0, 1), (-1, -1), (-1, 1), (1, -1), (1, 1)]):
    regions[where_] = (64 + 40 * order, 40) if order < 4 else (96 + 32 * order, 32)

flows = [
    (a, b, c) for a in (1, -1, 0) for b in (1, -1, 0) for c in (1, -1, 0) if a or b or c
]
flow_index = {flow: number for number, flow in enumerate(flows)}


def outer_cells():
    r = lax.broadcasted_iota(jnp.int32, (1, 384), 1)
    low = jnp.bitwise_and(r, 7)
    tile = lax.shift_right_logical(r, 3)
    x = jnp.where(r < 64, tile, jnp.where(r < 104, tile - 13, jnp.where(r < 144, tile - 5, low)))
    y = jnp.where(r < 144, low, jnp.where(r < 184, tile - 23, tile - 15))
    k = jnp.bitwise_and(r, 31)
    edge = lax.shift_right_logical(r, 5) - 7
    part_y = lax.shift_right_logical(k * 13, 6)
    part_x = k - 5 * part_y
    edge_x = jnp.where(edge < 2, part_x - 5, part_x + 8)
    edge_y = jnp.where(jnp.bitwise_and(edge, 1) == 0, part_y - 5, part_y + 8)
    used = jnp.logical_and(k < 25, edge < 4)
    x = jnp.where(r < 224, x, jnp.where(used, edge_x, 12288))
    y = jnp.where(r < 224, y, jnp.where(used, edge_y, 12288))
    return x.astype(F32), y.astype(F32)


def split(value):
    high = value.astype(BF16)
    return high, (value - high.astype(F32)).astype(BF16)


def left_dot(matrix, value):
    both = jnp.dot(
        matrix, jnp.concatenate(split(value), axis=1), preferred_element_type=F32
    )
    width = value.shape[1]
    return both[:, :width] + both[:, width:]


def right_dot(value, matrix):
    high, low = split(value)
    return jnp.dot(high, matrix, preferred_element_type=F32) + jnp.dot(
        low, matrix, preferred_element_type=F32
    )


def right_dot_t(value, matrix):
    high, low = split(value)
    dims = (((1,), (1,)), ((), ()))
    return lax.dot_general(high, matrix, dims, preferred_element_type=F32) + lax.dot_general(
        low, matrix, dims, preferred_element_type=F32
    )


def triangle(n):
    return 0.5 * n * (n + 1.0)


def weight_total(position, count):
    position = jnp.where(position < 0, position + count, position)
    position = jnp.where(position > count - 1, position - count, position)
    return (
        25.0
        - triangle(jnp.maximum(0.0, 4.0 - position))
        - triangle(jnp.maximum(0.0, position - (count - 5.0)))
    )


def cut(value, last, low, high):
    return (
        value
        - jnp.where(value < 0, FAR, 0.0) * low
        + jnp.where(value > last, FAR, 0.0) * high
    )


def hat(difference):
    return jnp.maximum(0.0, 5.0 - jnp.abs(difference))


def add_all(terms):
    terms = list(terms)
    while len(terms) > 1:
        terms = [
            terms[n] + terms[n + 1] if n + 1 < len(terms) else terms[n]
            for n in range(0, len(terms), 2)
        ]
    return terms[0]


def project(c, vector):
    total = None
    for component, value in zip(c, vector):
        if component == 1:
            total = value if total is None else total + value
        elif component == -1:
            total = -value if total is None else total - value
    return total


def momentum(t):
    return (
        add_all([t[0], t[3] + t[4], t[5] + t[6]]),
        add_all([t[1], t[3] - t[4], t[7] + t[8]]),
        add_all([t[2], t[5] - t[6], t[7] - t[8]]),
    )


def cell_kinds(flags):
    omega = jnp.where(flags == 3, 1.0, relax_rate)
    solid = flags == 1
    inlet = flags == 2
    blocked = jnp.logical_or(solid, inlet)
    keep = 1.0 - omega
    even = jnp.where(solid, 1.0, jnp.where(inlet, 0.0, keep))
    odd = jnp.where(solid, -1.0, jnp.where(inlet, 0.0, keep))
    fluid_omega = jnp.where(blocked, 0.0, omega)
    return omega, keep, solid, inlet, blocked, even, odd, fluid_omega


def first_collision(f, flags):
    omega, keep, solid, inlet, blocked, even, odd, fluid_omega = cell_kinds(flags)
    rate = jnp.where(inlet, 1.0, fluid_omega)
    s = [f[2 * p + 1] + f[2 * p + 2] for p in range(9)]
    t = [f[2 * p + 1] - f[2 * p + 2] for p in range(9)]
    rho = jnp.where(inlet, 1.0, add_all([f[0]] + s))
    mx, my, mz = momentum(t)
    mx = jnp.where(inlet, inlet_speed, mx)
    my = jnp.where(inlet, 0.0, my)
    mz = jnp.where(inlet, 0.0, mz)
    inverse = 1.0 / rho
    base = rho - 1.5 * (mx * mx + my * my + mz * mz) * inverse
    bend = 4.5 * inverse
    half_even, half_odd = 0.5 * even, 0.5 * odd
    base_a, base_b = rate * pair_weights[0], rate * pair_weights[3]
    first = [even * f[0] + rate * (1.0 / 3.0) * base]
    slope = []
    for p in range(9):
        along = project(velocities[2 * p + 1], (mx, my, mz))
        weight = base_a if p < 3 else base_b
        symmetric = half_even * s[p] + weight * (base + bend * (along * along))
        skew = half_odd * t[p] + (3.0 * weight) * along
        first += [symmetric + skew, symmetric - skew]
        slope.append(jnp.where(blocked, 0.0, -2.0 * skew))
    return first, slope


def adjoint_collision(f, a, kappa, flags):
    omega, keep, solid, inlet, blocked, even, odd, fluid_omega = cell_kinds(flags)
    pass_back = 1.0 - 2.0 * kappa
    s = [f[2 * p + 1] + f[2 * p + 2] for p in range(9)]
    t = [f[2 * p + 1] - f[2 * p + 2] for p in range(9)]
    rho = add_all([f[0]] + s)
    mx, my, mz = momentum(t)
    inverse = 1.0 / rho
    ux, uy, uz = mx * inverse, my * inverse, mz * inverse
    even_a = [a[2 * p + 1] + a[2 * p + 2] for p in range(9)]
    odd_a = [a[2 * p + 1] - a[2 * p + 2] for p in range(9)]
    ws = [pair_weights[p] * even_a[p] for p in range(9)]
    wt = [pair_weights[p] * odd_a[p] for p in range(9)]
    b0 = add_all([(1.0 / 3.0) * a[0]] + ws)
    b1x, b1y, b1z = momentum(wt)
    bxx = add_all([ws[0], ws[3] + ws[4], ws[5] + ws[6]])
    byy = add_all([ws[1], ws[3] + ws[4], ws[7] + ws[8]])
    bzz = add_all([ws[2], ws[5] + ws[6], ws[7] + ws[8]])
    bxy, bxz, byz = ws[3] - ws[4], ws[5] - ws[6], ws[7] - ws[8]
    vx = bxx * ux + bxy * uy + bxz * uz
    vy = bxy * ux + byy * uy + byz * uz
    vz = bxz * ux + byz * uy + bzz * uz
    moved = 3.0 * (mx * b1x + my * b1y + mz * b1z)
    kept = add_all([odd_a[p] * t[p] for p in range(9)])
    slope = jnp.where(blocked, 0.0, -(keep * kept + 2.0 * omega * moved))
    usq = ux * ux + uy * uy + uz * uz
    to_rho = fluid_omega * (b0 * (1.0 + 1.5 * usq) - 4.5 * (ux * vx + uy * vy + uz * vz))
    back = 3.0 * pass_back
    gx = fluid_omega * (back * b1x + 9.0 * vx - 3.0 * ux * b0)
    gy = fluid_omega * (back * b1y + 9.0 * vy - 3.0 * uy * b0)
    gz = fluid_omega * (back * b1z + 9.0 * vz - 3.0 * uz * b0)
    half_even = 0.5 * even
    half_odd = 0.5 * jnp.where(blocked, odd, odd * pass_back)
    result = [even * a[0] + to_rho]
    for p in range(9):
        along = project(velocities[2 * p + 1], (gx, gy, gz))
        symmetric = half_even * even_a[p] + to_rho
        skew = half_odd * odd_a[p] + along
        result += [symmetric + skew, symmetric - skew]
    return result, slope


def aligned(index):
    return pl.multiple_of(index * 8, 8)


def kernel(
    sizes,
    pop_in,
    design_in,
    flags_in,
    seed_in,
    out_ref,
    rms_ref,
    pops,
    flags_v,
    first_v,
    slope_v,
    seed_v,
    field,
    x_send,
    x_recv,
    y_field,
    y_send,
    y_rows,
    xy_send,
    mixed_send,
    z_send,
    z_recv,
    z_pack,
    kappa_v,
    grad_v,
    spread,
    spread_recv,
    q_out,
    q_recv,
    ring_a,
    ring_b,
    big_l,
    big_l_wide,
    big_lt,
    rep_l,
    rep_l_wide,
    rep_lt,
    cross_x,
    cross_z,
    cross_xt,
    cross_zt,
    wide_x_v,
    wide_z_v,
    block_mask,
    row_scale,
    local_sem,
    send_sem,
    recv_sem,
):
    nx, ny, nz = sizes
    gx, gy, gz = lax.axis_index("gx"), lax.axis_index("gy"), lax.axis_index("gz")

    def around(start, length):
        if length & (length - 1) == 0:
            return [jnp.bitwise_and(start + n, length - 1) for n in range(length)]
        return [lax.rem(start + n, length) for n in range(length)]

    place_x, place_y, place_z = around(gx, nx), around(gy, ny), around(gz, nz)

    def device(move):
        return place_x[move[0] % nx], place_y[move[1] % ny], place_z[move[2] % nz]

    slab_moves = [(0, b, c) for b in range(ny) for c in range(nz) if b or c]
    slab_moves.sort(key=lambda m: -(min(m[1], ny - m[1]) + min(m[2], nz - m[2])))
    line_moves = [(a, 0, 2 * (a % 2)) for a in range(1, nx)]
    line_moves.sort(key=lambda m: -(min(m[0], nx - m[0]) + 2 * (m[0] % 2)))

    def key(move):
        return (move[0] % nx, move[1] % ny, move[2] % nz)

    partners = []
    for move in line_moves + flows + slab_moves:
        if key(move) not in partners:
            partners.append(key(move))
    barrier = pltpu.get_barrier_semaphore()
    for move in partners:
        pl.semaphore_signal(barrier, inc=1, device_id=device(move), device_id_type=MESH)

    loads = [
        pltpu.make_async_copy(pop_in, pops, local_sem.at[1]),
        pltpu.make_async_copy(flags_in, flags_v, local_sem.at[2]),
        pltpu.make_async_copy(seed_in, seed_v.at[:, pl.ds(8, 64), :], local_sem.at[3]),
        pltpu.make_async_copy(design_in, field.at[pl.ds(0, 64)], local_sem.at[4]),
    ]
    for load in loads:
        load.start()
    for load in loads:
        load.wait()

    lane = lax.broadcasted_iota(jnp.int32, (8, 128), 1)
    row = lax.broadcasted_iota(jnp.int32, (8, 128), 0)

    def own(k, j, rows):
        if k == 0:
            return first_v[j, rows, :]
        if k == 1:
            return slope_v[(j - 1) // 2, rows, :]
        return seed_v[opposite[j], rows, :]

    def start_step(x, carry):
        rows = pl.ds(aligned(x), 8)
        inner = pl.ds(aligned(x + 1), 8)
        first, slope = first_collision([pops[i, rows, :] for i in range(19)], flags_v[rows, :])
        for i in range(19):
            first_v[i, inner, :] = first[i]
        for p in range(9):
            slope_v[p, inner, :] = slope[p]
        packs = list(carry[:2])
        for n, sign in enumerate((1, -1)):
            edge = 127 if sign == 1 else 0
            for k in range(3):
                for s, j in enumerate(crossing[2, sign]):
                    tile = (
                        first[j]
                        if k == 0
                        else slope[(j - 1) // 2]
                        if k == 1
                        else seed_v[opposite[j], inner, :]
                    )
                    place = k * 40 + s * 8 + x
                    moved = pltpu.roll(tile, jnp.bitwise_and(place + 128 - edge, 127), 1)
                    packs[n] = jnp.where(lane == place, moved, packs[n])
        tile = field[rows, :]
        quad = carry[2]
        here = lax.shift_right_logical(lane, 4) == x
        part = jnp.bitwise_and(lane, 15)
        high = pltpu.roll(tile, jnp.bitwise_and(16 * x + 5, 127), 1)
        low = pltpu.roll(tile, jnp.bitwise_and(16 * x + 8, 127), 1)
        quad = jnp.where(jnp.logical_and(here, part < 5), high, quad)
        quad = jnp.where(
            jnp.logical_and(here, jnp.logical_and(part >= 8, part < 13)), low, quad
        )
        return packs[0], packs[1], quad

    blank = jnp.zeros((8, 128), F32)
    pack_up, pack_down, quad = lax.fori_loop(0, 8, start_step, (blank, blank, blank), unroll=2)
    z_send[0, 0] = quad
    z_send[1, 0] = quad
    z_send[0, 1] = pack_up
    z_send[1, 1] = pack_down
    for sign in (1, -1):
        n = side[sign]
        edge = 7 if sign == 1 else 0
        for k in range(3):
            for s, j in enumerate(crossing[0, sign]):
                x_send[n, 5 * k + s] = own(k, j, pl.ds(8 * (edge + 1), 8))
            for s, j in enumerate(crossing[1, sign]):
                y_send[n, 5 * k + s] = own(k, j, pl.ds(8 + edge, 8, stride=8))
        for r in range(5):
            y_field[n, pl.ds(8 * r, 8), :] = field[
                pl.ds(3 + r if sign == 1 else r, 8, stride=8), :
            ]
    packs = {1: pack_up, -1: pack_down}
    mixed = [flow for flow in flows if flow[2] and (flow[0] == 0) != (flow[1] == 0)]
    for n, (a, b, c) in enumerate(mixed):
        if a:
            s = crossing[2, c].index(velocities.index((a, b, c)))
            tile = quad
            for k in range(3):
                free = k if a == 1 else 112 + k
                place = 40 * k + 8 * s + (7 if a == 1 else 0)
                tile = jnp.where(
                    lane == free, pltpu.roll(packs[c], (free - place) % 128, 1), tile
                )
        elif b == 1:
            tile = jnp.where(row == 0, pltpu.roll(packs[c], 1, 0), quad)
        else:
            tile = jnp.where(row == 7, pltpu.roll(packs[c], 7, 0), quad)
        mixed_send[n] = tile
    diagonals = [(a, b) for a in (1, -1) for b in (1, -1)]
    for n, (a, b) in enumerate(diagonals):
        j = velocities.index((a, b, 0))
        for r in range(5):
            at = (24 if a == 1 else 0) + (3 + r if b == 1 else r)
            xy_send[n, pl.ds(5 * r, 5), :] = field[pl.ds(at, 5, stride=8), :]
        for k in range(3):
            at = (8 if a == 1 else 1) * 8 + (7 if b == 1 else 0)
            xy_send[n, pl.ds(25 + k, 1), :] = own(k, j, pl.ds(at, 1))
        xy_send[n, pl.ds(28, 4), :] = jnp.zeros((4, 128), F32)

    pl.semaphore_wait(barrier, len(partners))
    count = [0]
    started = []

    def send(source, target, move):
        n = count[0]
        count[0] += 1
        copy = pltpu.make_async_remote_copy(
            src_ref=source,
            dst_ref=target,
            send_sem=send_sem.at[n],
            recv_sem=recv_sem.at[n],
            device_id=device(move),
            device_id_type=MESH,
        )
        copy.start()
        started.append(copy)
        return copy

    def region(a, b):
        start, rows = regions[a, b]
        return pl.ds(start, rows)

    field_copies, fill_copies = [], []
    for n, (a, b) in enumerate(diagonals):
        field_copies.append(send(xy_send.at[n], field.at[region(-a, -b)], (a, b, 0)))
    for a in (1, -1):
        source = pl.ds(24, 40) if a == 1 else pl.ds(0, 40)
        field_copies.append(send(field.at[source], field.at[region(-a, 0)], (a, 0, 0)))
    for flow in flows:
        if flow[2] != 0:
            n = flow_index[flow]
            if flow[0] != 0 and flow[1] != 0:
                source, target = z_send.at[side[flow[2]], 0], z_recv.at[n, 0]
            elif flow in mixed:
                source, target = mixed_send.at[mixed.index(flow)], z_recv.at[n, 0]
            else:
                source, target = z_send.at[side[flow[2]]], z_recv.at[n]
            field_copies.append(send(source, target, flow))
    for b in (1, -1):
        field_copies.append(send(y_field.at[side[b]], field.at[region(0, -b)], (0, b, 0)))
    for a in (1, -1):
        fill_copies.append(send(x_send.at[side[a]], x_recv.at[side[a]], (a, 0, 0)))
    for b in (1, -1):
        fill_copies.append(
            send(y_send.at[side[b]], y_rows.at[side[b], :, pl.ds(8, 8), :], (0, b, 0))
        )

    def one_if(condition):
        return jnp.where(condition, 1.0, 0.0).astype(F32)

    x_low, x_high = one_if(gx == 0), one_if(gx == nx - 1)
    y_low, y_high = one_if(gy == 0), one_if(gy == ny - 1)
    z_low, z_high = one_if(gz == 0), one_if(gz == nz - 1)
    lanes_x, lanes_y = outer_cells()
    lanes_x = cut(lanes_x, 7.0, x_low, x_high)
    lanes_y = cut(lanes_y, 7.0, y_low, y_high)
    wide = lax.broadcasted_iota(jnp.int32, (1, 384), 1)
    plain_z = jnp.where(wide < 128, wide, jnp.where(wide < 256, wide - 129, wide - 255)).astype(F32)
    lanes_z = cut(plain_z, 127.0, z_low, z_high)
    line = lax.broadcasted_iota(jnp.int32, (1, 128), 1)
    tenth = lax.shift_right_logical(line * 205, 11)
    part_ten = line - 10 * tenth
    blocks_x = cut(jnp.where(tenth < 10, tenth - 1, 12288).astype(F32), 7.0, x_low, x_high)
    blocks_part = jnp.where(part_ten < 5, part_ten, part_ten + 3)
    stack_y = cut(jnp.where(line < 24, line - 8, 12288).astype(F32), 7.0, y_low, y_high)
    lane_scale = 1.0 / weight_total(plain_z + (gz * 128).astype(F32), 128.0 * nz)

    def build_rows(t, carry):
        rows = pl.ds(pl.multiple_of(t * 16, 16), 16)
        index = lax.broadcasted_iota(jnp.int32, (16, 128), 0) + t * 16
        tile = lax.shift_right_logical(index, 3)
        late = jnp.where(tile >= 20, 2, jnp.where(tile >= 10, 1, 0))
        plane = tile - 10 * late
        x = (plane - 1).astype(F32)
        y = (jnp.bitwise_and(index, 7) - jnp.where(late == 1, 1, jnp.where(late == 2, -1, 0))).astype(F32)
        row_scale[rows, :] = 1.0 / (
            weight_total(x + (gx * 8).astype(F32), 8.0 * nx)
            * weight_total(y + (gy * 8).astype(F32), 8.0 * ny)
        )
        cut_x = cut(x, 7.0, x_low, x_high)
        cut_y = cut(y, 7.0, y_low, y_high)
        wide_x = jnp.concatenate([cut_x] * 3, axis=1)
        wide_y = jnp.concatenate([cut_y] * 3, axis=1)
        weights = hat(wide_x - lanes_x) * hat(wide_y - lanes_y)
        big_l_wide[rows, :] = weights
        big_l[rows, :] = weights.astype(BF16)
        repeated = hat(cut_y - stack_y)
        rep_l_wide[rows, :] = repeated
        rep_l[rows, :] = repeated.astype(BF16)
        block_mask[rows, :] = jnp.where(tenth == plane, 1.0, 0.0)
        return carry

    lax.fori_loop(0, 16, build_rows, 0)
    big_lt[...] = big_l_wide[...].T.astype(BF16)
    rep_lt[...] = rep_l_wide[...].T[0:32, :].astype(BF16)

    def build_cross(t, carry):
        rows = pl.ds(pl.multiple_of(t * 16, 16), 16)
        x = cut((t - 8).astype(F32), 7.0, x_low, x_high)
        same = lax.broadcasted_iota(jnp.int32, (16, 128), 0) == blocks_part
        weights = jnp.where(same, hat(x - blocks_x), 0.0)
        wide_x_v[rows, :] = weights
        cross_x[rows, :] = weights.astype(BF16)
        return carry

    lax.fori_loop(0, 24, build_cross, 0)

    def build_z(t, carry):
        rows = pl.ds(pl.multiple_of(t * 16, 16), 16)
        index = lax.broadcasted_iota(jnp.int32, (16, 384), 0) + t * 16
        halo = index - 128
        halo = halo - 10 * lax.shift_right_logical(halo * 205, 11)
        halo = jnp.where(halo < 5, halo - 5, halo + 123)
        z = cut(jnp.where(index < 128, index, halo).astype(F32), 127.0, z_low, z_high)
        weights = hat(z - lanes_z)
        wide_z_v[rows, :] = weights
        cross_z[rows, :] = weights.astype(BF16)
        return carry

    lax.fori_loop(0, 16, build_z, 0)
    cross_xt[...] = wide_x_v[...].T.astype(BF16)
    cross_zt[...] = wide_z_v[...].T.astype(BF16)
    grad_v[...] = jnp.zeros_like(grad_v)

    for copy in field_copies[:6] + field_copies[-2:]:
        copy.wait_recv()
    inner_xy = left_dot(big_l[...], field[...])
    for copy in field_copies[6:-2]:
        copy.wait_recv()
    part = jnp.bitwise_and(lane, 15)
    stacked = []
    for b in (-1, 0, 1):
        tiles = []
        for a in (-1, 0, 1):
            below = z_recv[flow_index[-a, -b, 1], 0]
            above = z_recv[flow_index[-a, -b, -1], 0]
            tiles.append(jnp.where(part < 8, below, above))
        stacked.append(jnp.concatenate(tiles, axis=1))
    stacked.append(jnp.zeros((8, 384), F32))
    halo_x = right_dot(jnp.concatenate(stacked, axis=0), cross_x[...])
    halo_x = jnp.concatenate([halo_x, jnp.zeros((96, 128), F32)], axis=0)
    halo_xy = left_dot(rep_l[...], halo_x) * block_mask[...]
    summed = right_dot(jnp.concatenate([inner_xy, halo_xy], axis=1), cross_z[...])
    scale_rows = jnp.concatenate([row_scale[...]] * 3, axis=1)
    kappa_v[...] = 0.5 * (1.0 - summed * scale_rows * lane_scale)

    for copy in fill_copies[2:]:
        copy.wait_recv()
    eighth = lax.shift_right_logical(lane, 3)
    slot = eighth - jnp.where(eighth >= 10, 10, jnp.where(eighth >= 5, 5, 0))
    for sign in (1, -1):
        base = z_recv[flow_index[0, 0, sign], 1]
        total = base
        for s, j in enumerate(crossing[2, sign]):
            a, b, _ = velocities[j]
            if a != 0:
                corner = z_recv[flow_index[a, 0, sign], 0]
                moved = pltpu.roll(base, a % 128, 1)
                for k in range(3):
                    free = k if a == 1 else 112 + k
                    place = 40 * k + 8 * s + (0 if a == 1 else 7)
                    moved = jnp.where(
                        lane == place, pltpu.roll(corner, (place - free) % 128, 1), moved
                    )
            elif b != 0:
                corner = z_recv[flow_index[0, b, sign], 0]
                moved = jnp.where(row == (0 if b == 1 else 7), corner, pltpu.roll(base, b % 8, 0))
            else:
                continue
            total = jnp.where(slot == s, moved, total)
        z_pack[side[sign]] = total

    def plane_step(x, carry):
        def stream(k, j):
            a, b, c = velocities[j]
            tile = own(k, j, pl.ds(aligned(x + 1 - a), 8))
            if b != 0:
                s = crossing[1, b].index(j)
                line = y_rows[side[b], 5 * k + s, pl.ds(8 + x - a, 1), :]
                tile = jnp.where(
                    row == (0 if b == 1 else 7), line, pltpu.roll(tile, b % 8, 0)
                )
            if c != 0:
                s = crossing[2, c].index(j)
                edge = 0 if c == 1 else 127
                place = k * 40 + s * 8 + x
                column = pltpu.roll(
                    z_pack[side[c]], jnp.bitwise_and(256 + edge - place, 127), 1
                )
                tile = jnp.where(lane == edge, column, pltpu.roll(tile, c % 128, 1))
            return tile

        def spot(j):
            a, b, c = velocities[j]
            return (
                pl.ds(aligned(kind[b] * 10 + x + 1 - a), 8),
                pl.ds(128 * kind[c], 128),
            )

        center = pl.ds(aligned(x + 1), 8)
        flags = flags_v[pl.ds(aligned(x), 8), :]
        state, slopes = [first_v[0, center, :]], [None]
        weights = [seed_v[0, center, :]] + [None] * 18
        for j in range(1, 19):
            slope = stream(1, j)
            rows, lanes = spot(j)
            change = kappa_v[rows, lanes] * slope
            before = stream(0, j)
            state.append(before + change if j % 2 == 1 else before - change)
            slopes.append(slope)
            weights[opposite[j]] = stream(2, j)
        kappa = kappa_v[center, 0:128]
        back, here = adjoint_collision(state, weights, kappa, flags)
        grad_v[center, 0:128] += here
        for j in range(1, 19):
            rows, lanes = spot(j)
            if j % 2 == 1:
                grad_v[rows, lanes] += slopes[j] * back[j]
            else:
                grad_v[rows, lanes] -= slopes[j] * back[j]
        return carry

    lax.fori_loop(1, 7, plane_step, 0, unroll=6)
    for copy in fill_copies[:2]:
        copy.wait_recv()
    for sign in (1, -1):
        n = side[sign]
        rows = pl.ds(0, 8) if sign == 1 else pl.ds(72, 8)
        for s, j in enumerate(crossing[0, sign]):
            first_v[j, rows, :] = x_recv[n, s]
            slope_v[(j - 1) // 2, rows, :] = x_recv[n, 5 + s]
            seed_v[opposite[j], rows, :] = x_recv[n, 10 + s]
    for a, b in diagonals:
        j = velocities.index((a, b, 0))
        s = crossing[1, b].index(j)
        start = regions[-a, -b][0]
        for k in range(3):
            y_rows[side[b], 5 * k + s, pl.ds(7 if a == 1 else 16, 1), :] = field[
                pl.ds(start + 25 + k, 1), :
            ]
    lax.fori_loop(0, 2, lambda n, carry: plane_step(7 * n, carry), 0, unroll=2)

    scaled = grad_v[...] * (scale_rows * (-0.5 * lane_scale))
    summed = right_dot(scaled, cross_zt[...])
    spread[...] = left_dot(big_lt[...], summed[:, 0:128])
    spread_copies = []
    for flow in flows:
        a, b, c = flow
        if c == 0:
            spread_copies.append(
                send(spread.at[region(a, b)], spread_recv.at[region(a, b)], flow)
            )
    halo_x = left_dot(rep_lt[...], summed[:, 128:256] * block_mask[...])
    halo = right_dot(halo_x, cross_xt[...])
    for b in range(3):
        for a in range(3):
            q_out[3 * b + a] = halo[8 * b : 8 * b + 8, 128 * a : 128 * a + 128]
    for flow in flows:
        a, b, c = flow
        if c != 0:
            spread_copies.append(
                send(q_out.at[3 * (b + 1) + a + 1], q_recv.at[flow_index[flow]], flow)
            )
    arrived = dict(zip([f for f in flows if f[2] == 0] + [f for f in flows if f[2] != 0], spread_copies))
    for b in (1, -1):
        arrived[0, b, 0].wait_recv()
        for r in range(5):
            y = r if b == 1 else 3 + r
            spread[pl.ds(y, 8, stride=8), :] += spread_recv[
                pl.ds(regions[0, b][0] + 8 * r, 8), :
            ]
    for flow in reversed(flows):
        if flow[2] != 0:
            arrived[flow].wait_recv()
    up = add_all([q_recv[flow_index[a, b, 1]] for a in (-1, 0, 1) for b in (-1, 0, 1)])
    down = add_all([q_recv[flow_index[a, b, -1]] for a in (-1, 0, 1) for b in (-1, 0, 1)])
    for x in range(8):
        first = pltpu.roll(up, (128 - 16 * x - 8) % 128, 1)
        last = pltpu.roll(down, (123 - 16 * x) % 128, 1)
        spread[pl.ds(8 * x, 8), :] += jnp.where(
            lane < 5, first, jnp.where(lane >= 123, last, 0.0)
        )
    arrived[-1, 0, 0].wait_recv()
    spread[pl.ds(24, 40), :] += spread_recv[region(-1, 0), :]
    arrived[1, 0, 0].wait_recv()
    spread[pl.ds(0, 40), :] += spread_recv[region(1, 0), :]
    for a, b in diagonals:
        arrived[a, b, 0].wait_recv()
        for r in range(5):
            y = r if b == 1 else 3 + r
            spread[pl.ds(y + (0 if a == 1 else 24), 5, stride=8), :] += spread_recv[
                pl.ds(regions[a, b][0] + 5 * r, 5), :
            ]
    squares = blank
    for x in range(8):
        tile = spread[pl.ds(8 * x, 8), :]
        squares = squares + tile * tile

    mine = gy * nz + gz
    ring_a[mine] = jnp.sum(squares, axis=0, keepdims=True)
    ring_copies = [send(ring_a.at[mine], ring_a.at[mine], move) for move in slab_moves]
    for copy in reversed(ring_copies):
        copy.wait_recv()
    ring_b[gx] = jnp.sum(ring_a[...], axis=0)
    ring_copies = [send(ring_b.at[gx], ring_b.at[gx], move) for move in line_moves]
    for copy in reversed(ring_copies):
        copy.wait_recv()
    total = jnp.sum(jnp.sum(ring_b[...], axis=0), axis=1, keepdims=True)
    mean_square = total / (8192.0 * nx * ny * nz)
    out_ref[...] = spread[pl.ds(0, 64), :]
    rms_ref[...] = jnp.broadcast_to(mean_square, (8, 128))
    for copy in started:
        copy.wait_send()


def finish(raw_ref, mean_ref, out_ref, rms_ref):
    mean_square = mean_ref[0:1, 0:1]
    out_ref[...] = raw_ref[...] * lax.rsqrt(mean_square + norm_eps)
    rms_ref[...] = jnp.sqrt(mean_square)


def solution(mesh):
    sizes = tuple(mesh.shape[name] for name in ("gx", "gy", "gz"))
    copies = 4 + 2 + 18 + 2 + 2 + 2 + 26 + (sizes[1] * sizes[2] - 1) + (sizes[0] - 1)

    def body(populations, design, flags, adjoint_seed):
        anywhere = pl.BlockSpec(memory_space=pl.ANY)
        inside = pl.BlockSpec(memory_space=pltpu.VMEM)
        scratch = [
            pltpu.VMEM((19, 64, 128), F32),
            pltpu.VMEM((64, 128), jnp.int32),
            pltpu.VMEM((19, 80, 128), F32),
            pltpu.VMEM((9, 80, 128), F32),
            pltpu.VMEM((19, 80, 128), F32),
            pltpu.VMEM((384, 128), F32),
            pltpu.VMEM((2, 15, 8, 128), F32),
            pltpu.VMEM((2, 15, 8, 128), F32),
            pltpu.VMEM((2, 40, 128), F32),
            pltpu.VMEM((2, 15, 8, 128), F32),
            pltpu.VMEM((2, 15, 24, 128), F32),
            pltpu.VMEM((4, 32, 128), F32),
            pltpu.VMEM((8, 8, 128), F32),
            pltpu.VMEM((2, 2, 8, 128), F32),
            pltpu.VMEM((26, 2, 8, 128), F32),
            pltpu.VMEM((2, 8, 128), F32),
            pltpu.VMEM((256, 384), F32),
            pltpu.VMEM((256, 384), F32),
            pltpu.VMEM((384, 128), F32),
            pltpu.VMEM((384, 128), F32),
            pltpu.VMEM((9, 8, 128), F32),
            pltpu.VMEM((26, 8, 128), F32),
            pltpu.VMEM((sizes[1] * sizes[2], 1, 128), F32),
            pltpu.VMEM((sizes[0], 1, 128), F32),
            pltpu.VMEM((256, 384), BF16),
            pltpu.VMEM((256, 384), F32),
            pltpu.VMEM((384, 256), BF16),
            pltpu.VMEM((256, 128), BF16),
            pltpu.VMEM((256, 128), F32),
            pltpu.VMEM((32, 256), BF16),
            pltpu.VMEM((384, 128), BF16),
            pltpu.VMEM((256, 384), BF16),
            pltpu.VMEM((128, 384), BF16),
            pltpu.VMEM((384, 256), BF16),
            pltpu.VMEM((384, 128), F32),
            pltpu.VMEM((256, 384), F32),
            pltpu.VMEM((256, 128), F32),
            pltpu.VMEM((256, 128), F32),
            pltpu.SemaphoreType.DMA((5,)),
            pltpu.SemaphoreType.DMA((copies,)),
            pltpu.SemaphoreType.DMA((copies,)),
        ]
        grad, rms = pl.pallas_call(
            functools.partial(kernel, sizes),
            out_shape=(
                jax.ShapeDtypeStruct((64, 128), F32),
                jax.ShapeDtypeStruct((8, 128), F32),
            ),
            in_specs=[anywhere] * 4,
            out_specs=(inside, inside),
            scratch_shapes=scratch,
            compiler_params=pltpu.CompilerParams(
                collective_id=0, has_side_effects=True, vmem_limit_bytes=56491008
            ),
        )(
            populations.reshape(19, 64, 128),
            design.reshape(64, 128),
            flags.reshape(64, 128),
            adjoint_seed.reshape(19, 64, 128),
        )
        grad, rms = pl.pallas_call(
            finish,
            out_shape=(
                jax.ShapeDtypeStruct((64, 128), F32),
                jax.ShapeDtypeStruct((1, 1), F32),
            ),
            in_specs=[inside, inside],
            out_specs=(inside, inside),
            name="scale_gradient",
            compiler_params=pltpu.CompilerParams(vmem_limit_bytes=1024 * 1024),
        )(grad, rms)
        return grad.reshape(8, 8, 128), rms.reshape(())

    return jax.shard_map(
        body,
        mesh=mesh,
        in_specs=(
            P(None, "gx", "gy", "gz"),
            P("gx", "gy", "gz"),
            P("gx", "gy", "gz"),
            P(None, "gx", "gy", "gz"),
        ),
        out_specs=(P("gx", "gy", "gz"), P()),
        check_vma=False,
    )
```

```python
import functools

import jax
import jax.numpy as jnp
from jax import lax
from jax.experimental import pallas as pl
from jax.experimental.pallas import tpu as pltpu
from jax.sharding import PartitionSpec as P

MESH = pl.DeviceIdType.MESH
F32 = jnp.float32
BF16 = jnp.bfloat16

velocities = [
    (0, 0, 0),
    (1, 0, 0),
    (-1, 0, 0),
    (0, 1, 0),
    (0, -1, 0),
    (0, 0, 1),
    (0, 0, -1),
    (1, 1, 0),
    (-1, -1, 0),
    (1, -1, 0),
    (-1, 1, 0),
    (1, 0, 1),
    (-1, 0, -1),
    (1, 0, -1),
    (-1, 0, 1),
    (0, 1, 1),
    (0, -1, -1),
    (0, 1, -1),
    (0, -1, 1),
]
opposite = [0, 2, 1, 4, 3, 6, 5, 8, 7, 10, 9, 12, 11, 14, 13, 16, 15, 18, 17]
pair_weights = [1.0 / 18.0] * 3 + [1.0 / 36.0] * 6
relax_rate = 1.6
inlet_speed = 0.05
norm_eps = 1e-06
FAR = 4096.0

crossing = {
    (0, 1): [1, 7, 9, 11, 13],
    (0, -1): [2, 8, 10, 12, 14],
    (1, 1): [3, 7, 10, 15, 17],
    (1, -1): [4, 8, 9, 16, 18],
    (2, 1): [5, 11, 14, 15, 18],
    (2, -1): [6, 12, 13, 16, 17],
}
side = {1: 0, -1: 1}
kind = {0: 0, 1: 1, -1: 2}

regions = {(0, 0): (0, 64)}
for order, where_ in enumerate([(-1, 0), (1, 0), (0, -1), (0, 1), (-1, -1), (-1, 1), (1, -1), (1, 1)]):
    regions[where_] = (64 + 40 * order, 40) if order < 4 else (96 + 32 * order, 32)

flows = [
    (a, b, c) for a in (1, -1, 0) for b in (1, -1, 0) for c in (1, -1, 0) if a or b or c
]
flow_index = {flow: number for number, flow in enumerate(flows)}


def outer_cells():
    r = lax.broadcasted_iota(jnp.int32, (1, 384), 1)
    low = jnp.bitwise_and(r, 7)
    tile = lax.shift_right_logical(r, 3)
    x = jnp.where(r < 64, tile, jnp.where(r < 104, tile - 13, jnp.where(r < 144, tile - 5, low)))
    y = jnp.where(r < 144, low, jnp.where(r < 184, tile - 23, tile - 15))
    k = jnp.bitwise_and(r, 31)
    edge = lax.shift_right_logical(r, 5) - 7
    part_y = lax.shift_right_logical(k * 13, 6)
    part_x = k - 5 * part_y
    edge_x = jnp.where(edge < 2, part_x - 5, part_x + 8)
    edge_y = jnp.where(jnp.bitwise_and(edge, 1) == 0, part_y - 5, part_y + 8)
    used = jnp.logical_and(k < 25, edge < 4)
    x = jnp.where(r < 224, x, jnp.where(used, edge_x, 12288))
    y = jnp.where(r < 224, y, jnp.where(used, edge_y, 12288))
    return x.astype(F32), y.astype(F32)


def split(value):
    high = value.astype(BF16)
    return high, (value - high.astype(F32)).astype(BF16)


def left_dot(matrix, value):
    both = jnp.dot(
        matrix, jnp.concatenate(split(value), axis=1), preferred_element_type=F32
    )
    width = value.shape[1]
    return both[:, :width] + both[:, width:]


def right_dot(value, matrix):
    high, low = split(value)
    return jnp.dot(high, matrix, preferred_element_type=F32) + jnp.dot(
        low, matrix, preferred_element_type=F32
    )


def right_dot_t(value, matrix):
    high, low = split(value)
    dims = (((1,), (1,)), ((), ()))
    return lax.dot_general(high, matrix, dims, preferred_element_type=F32) + lax.dot_general(
        low, matrix, dims, preferred_element_type=F32
    )


def triangle(n):
    return 0.5 * n * (n + 1.0)


def weight_total(position, count):
    position = jnp.where(position < 0, position + count, position)
    position = jnp.where(position > count - 1, position - count, position)
    return (
        25.0
        - triangle(jnp.maximum(0.0, 4.0 - position))
        - triangle(jnp.maximum(0.0, position - (count - 5.0)))
    )


def cut(value, last, low, high):
    return (
        value
        - jnp.where(value < 0, FAR, 0.0) * low
        + jnp.where(value > last, FAR, 0.0) * high
    )


def hat(difference):
    return jnp.maximum(0.0, 5.0 - jnp.abs(difference))


def add_all(terms):
    terms = list(terms)
    while len(terms) > 1:
        terms = [
            terms[n] + terms[n + 1] if n + 1 < len(terms) else terms[n]
            for n in range(0, len(terms), 2)
        ]
    return terms[0]


def project(c, vector):
    total = None
    for component, value in zip(c, vector):
        if component == 1:
            total = value if total is None else total + value
        elif component == -1:
            total = -value if total is None else total - value
    return total


def momentum(t):
    return (
        add_all([t[0], t[3] + t[4], t[5] + t[6]]),
        add_all([t[1], t[3] - t[4], t[7] + t[8]]),
        add_all([t[2], t[5] - t[6], t[7] - t[8]]),
    )


def cell_kinds(flags):
    omega = jnp.where(flags == 3, 1.0, relax_rate)
    solid = flags == 1
    inlet = flags == 2
    blocked = jnp.logical_or(solid, inlet)
    keep = 1.0 - omega
    even = jnp.where(solid, 1.0, jnp.where(inlet, 0.0, keep))
    odd = jnp.where(solid, -1.0, jnp.where(inlet, 0.0, keep))
    fluid_omega = jnp.where(blocked, 0.0, omega)
    return omega, keep, solid, inlet, blocked, even, odd, fluid_omega


def first_collision(f, flags):
    omega, keep, solid, inlet, blocked, even, odd, fluid_omega = cell_kinds(flags)
    rate = jnp.where(inlet, 1.0, fluid_omega)
    s = [f[2 * p + 1] + f[2 * p + 2] for p in range(9)]
    t = [f[2 * p + 1] - f[2 * p + 2] for p in range(9)]
    rho = jnp.where(inlet, 1.0, add_all([f[0]] + s))
    mx, my, mz = momentum(t)
    mx = jnp.where(inlet, inlet_speed, mx)
    my = jnp.where(inlet, 0.0, my)
    mz = jnp.where(inlet, 0.0, mz)
    inverse = 1.0 / rho
    base = rho - 1.5 * (mx * mx + my * my + mz * mz) * inverse
    bend = 4.5 * inverse
    half_even, half_odd = 0.5 * even, 0.5 * odd
    base_a, base_b = rate * pair_weights[0], rate * pair_weights[3]
    first = [even * f[0] + rate * (1.0 / 3.0) * base]
    slope = []
    for p in range(9):
        along = project(velocities[2 * p + 1], (mx, my, mz))
        weight = base_a if p < 3 else base_b
        symmetric = half_even * s[p] + weight * (base + bend * (along * along))
        skew = half_odd * t[p] + (3.0 * weight) * along
        first += [symmetric + skew, symmetric - skew]
        slope.append(jnp.where(blocked, 0.0, -2.0 * skew))
    return first, slope


def adjoint_collision(f, a, kappa, flags):
    omega, keep, solid, inlet, blocked, even, odd, fluid_omega = cell_kinds(flags)
    pass_back = 1.0 - 2.0 * kappa
    s = [f[2 * p + 1] + f[2 * p + 2] for p in range(9)]
    t = [f[2 * p + 1] - f[2 * p + 2] for p in range(9)]
    rho = add_all([f[0]] + s)
    mx, my, mz = momentum(t)
    inverse = 1.0 / rho
    ux, uy, uz = mx * inverse, my * inverse, mz * inverse
    even_a = [a[2 * p + 1] + a[2 * p + 2] for p in range(9)]
    odd_a = [a[2 * p + 1] - a[2 * p + 2] for p in range(9)]
    ws = [pair_weights[p] * even_a[p] for p in range(9)]
    wt = [pair_weights[p] * odd_a[p] for p in range(9)]
    b0 = add_all([(1.0 / 3.0) * a[0]] + ws)
    b1x, b1y, b1z = momentum(wt)
    bxx = add_all([ws[0], ws[3] + ws[4], ws[5] + ws[6]])
    byy = add_all([ws[1], ws[3] + ws[4], ws[7] + ws[8]])
    bzz = add_all([ws[2], ws[5] + ws[6], ws[7] + ws[8]])
    bxy, bxz, byz = ws[3] - ws[4], ws[5] - ws[6], ws[7] - ws[8]
    vx = bxx * ux + bxy * uy + bxz * uz
    vy = bxy * ux + byy * uy + byz * uz
    vz = bxz * ux + byz * uy + bzz * uz
    moved = 3.0 * (mx * b1x + my * b1y + mz * b1z)
    kept = add_all([odd_a[p] * t[p] for p in range(9)])
    slope = jnp.where(blocked, 0.0, -(keep * kept + 2.0 * omega * moved))
    usq = ux * ux + uy * uy + uz * uz
    to_rho = fluid_omega * (b0 * (1.0 + 1.5 * usq) - 4.5 * (ux * vx + uy * vy + uz * vz))
    back = 3.0 * pass_back
    gx = fluid_omega * (back * b1x + 9.0 * vx - 3.0 * ux * b0)
    gy = fluid_omega * (back * b1y + 9.0 * vy - 3.0 * uy * b0)
    gz = fluid_omega * (back * b1z + 9.0 * vz - 3.0 * uz * b0)
    half_even = 0.5 * even
    half_odd = 0.5 * jnp.where(blocked, odd, odd * pass_back)
    result = [even * a[0] + to_rho]
    for p in range(9):
        along = project(velocities[2 * p + 1], (gx, gy, gz))
        symmetric = half_even * even_a[p] + to_rho
        skew = half_odd * odd_a[p] + along
        result += [symmetric + skew, symmetric - skew]
    return result, slope


def aligned(index):
    return pl.multiple_of(index * 8, 8)


def kernel(
    sizes,
    pop_in,
    design_in,
    flags_in,
    seed_in,
    out_ref,
    rms_ref,
    pops,
    flags_v,
    first_v,
    slope_v,
    seed_v,
    field,
    x_send,
    x_recv,
    y_field,
    y_send,
    y_rows,
    xy_send,
    mixed_send,
    z_send,
    z_recv,
    z_pack,
    kappa_v,
    grad_v,
    spread,
    spread_recv,
    q_out,
    q_recv,
    ring_a,
    ring_b,
    big_l,
    big_l_wide,
    big_lt,
    rep_l,
    rep_l_wide,
    rep_lt,
    cross_x,
    cross_z,
    cross_xt,
    cross_zt,
    wide_x_v,
    wide_z_v,
    block_mask,
    row_scale,
    local_sem,
    send_sem,
    recv_sem,
):
    nx, ny, nz = sizes
    gx, gy, gz = lax.axis_index("gx"), lax.axis_index("gy"), lax.axis_index("gz")

    def around(start, length):
        if length & (length - 1) == 0:
            return [jnp.bitwise_and(start + n, length - 1) for n in range(length)]
        return [lax.rem(start + n, length) for n in range(length)]

    place_x, place_y, place_z = around(gx, nx), around(gy, ny), around(gz, nz)

    def device(move):
        return place_x[move[0] % nx], place_y[move[1] % ny], place_z[move[2] % nz]

    slab_moves = [(0, b, c) for b in range(ny) for c in range(nz) if b or c]
    slab_moves.sort(key=lambda m: -(min(m[1], ny - m[1]) + min(m[2], nz - m[2])))
    line_moves = [(a, 0, 2 * (a % 2)) for a in range(1, nx)]
    line_moves.sort(key=lambda m: -(min(m[0], nx - m[0]) + 2 * (m[0] % 2)))

    def key(move):
        return (move[0] % nx, move[1] % ny, move[2] % nz)

    partners = []
    for move in line_moves + flows + slab_moves:
        if key(move) not in partners:
            partners.append(key(move))
    barrier = pltpu.get_barrier_semaphore()
    for move in partners:
        pl.semaphore_signal(barrier, inc=1, device_id=device(move), device_id_type=MESH)

    loads = [
        pltpu.make_async_copy(pop_in, pops, local_sem.at[1]),
        pltpu.make_async_copy(flags_in, flags_v, local_sem.at[2]),
        pltpu.make_async_copy(seed_in, seed_v.at[:, pl.ds(8, 64), :], local_sem.at[3]),
        pltpu.make_async_copy(design_in, field.at[pl.ds(0, 64)], local_sem.at[4]),
    ]
    for load in loads:
        load.start()
    for load in loads:
        load.wait()

    lane = lax.broadcasted_iota(jnp.int32, (8, 128), 1)
    row = lax.broadcasted_iota(jnp.int32, (8, 128), 0)

    def own(k, j, rows):
        if k == 0:
            return first_v[j, rows, :]
        if k == 1:
            return slope_v[(j - 1) // 2, rows, :]
        return seed_v[opposite[j], rows, :]

    def start_step(x, carry):
        rows = pl.ds(aligned(x), 8)
        inner = pl.ds(aligned(x + 1), 8)
        first, slope = first_collision([pops[i, rows, :] for i in range(19)], flags_v[rows, :])
        for i in range(19):
            first_v[i, inner, :] = first[i]
        for p in range(9):
            slope_v[p, inner, :] = slope[p]
        packs = list(carry[:2])
        for n, sign in enumerate((1, -1)):
            edge = 127 if sign == 1 else 0
            for k in range(3):
                for s, j in enumerate(crossing[2, sign]):
                    tile = (
                        first[j]
                        if k == 0
                        else slope[(j - 1) // 2]
                        if k == 1
                        else seed_v[opposite[j], inner, :]
                    )
                    place = k * 40 + s * 8 + x
                    moved = pltpu.roll(tile, jnp.bitwise_and(place + 128 - edge, 127), 1)
                    packs[n] = jnp.where(lane == place, moved, packs[n])
        tile = field[rows, :]
        quad = carry[2]
        here = lax.shift_right_logical(lane, 4) == x
        part = jnp.bitwise_and(lane, 15)
        high = pltpu.roll(tile, jnp.bitwise_and(16 * x + 5, 127), 1)
        low = pltpu.roll(tile, jnp.bitwise_and(16 * x + 8, 127), 1)
        quad = jnp.where(jnp.logical_and(here, part < 5), high, quad)
        quad = jnp.where(
            jnp.logical_and(here, jnp.logical_and(part >= 8, part < 13)), low, quad
        )
        return packs[0], packs[1], quad

    blank = jnp.zeros((8, 128), F32)
    pack_up, pack_down, quad = lax.fori_loop(0, 8, start_step, (blank, blank, blank), unroll=2)
    z_send[0, 0] = quad
    z_send[1, 0] = quad
    z_send[0, 1] = pack_up
    z_send[1, 1] = pack_down
    for sign in (1, -1):
        n = side[sign]
        edge = 7 if sign == 1 else 0
        for k in range(3):
            for s, j in enumerate(crossing[0, sign]):
                x_send[n, 5 * k + s] = own(k, j, pl.ds(8 * (edge + 1), 8))
            for s, j in enumerate(crossing[1, sign]):
                y_send[n, 5 * k + s] = own(k, j, pl.ds(8 + edge, 8, stride=8))
        for r in range(5):
            y_field[n, pl.ds(8 * r, 8), :] = field[
                pl.ds(3 + r if sign == 1 else r, 8, stride=8), :
            ]
    packs = {1: pack_up, -1: pack_down}
    mixed = [flow for flow in flows if flow[2] and (flow[0] == 0) != (flow[1] == 0)]
    for n, (a, b, c) in enumerate(mixed):
        if a:
            s = crossing[2, c].index(velocities.index((a, b, c)))
            tile = quad
            for k in range(3):
                free = k if a == 1 else 112 + k
                place = 40 * k + 8 * s + (7 if a == 1 else 0)
                tile = jnp.where(
                    lane == free, pltpu.roll(packs[c], (free - place) % 128, 1), tile
                )
        elif b == 1:
            tile = jnp.where(row == 0, pltpu.roll(packs[c], 1, 0), quad)
        else:
            tile = jnp.where(row == 7, pltpu.roll(packs[c], 7, 0), quad)
        mixed_send[n] = tile
    diagonals = [(a, b) for a in (1, -1) for b in (1, -1)]
    for n, (a, b) in enumerate(diagonals):
        j = velocities.index((a, b, 0))
        for r in range(5):
            at = (24 if a == 1 else 0) + (3 + r if b == 1 else r)
            xy_send[n, pl.ds(5 * r, 5), :] = field[pl.ds(at, 5, stride=8), :]
        for k in range(3):
            at = (8 if a == 1 else 1) * 8 + (7 if b == 1 else 0)
            xy_send[n, pl.ds(25 + k, 1), :] = own(k, j, pl.ds(at, 1))
        xy_send[n, pl.ds(28, 4), :] = jnp.zeros((4, 128), F32)

    pl.semaphore_wait(barrier, len(partners))
    count = [0]
    started = []

    def send(source, target, move):
        n = count[0]
        count[0] += 1
        copy = pltpu.make_async_remote_copy(
            src_ref=source,
            dst_ref=target,
            send_sem=send_sem.at[n],
            recv_sem=recv_sem.at[n],
            device_id=device(move),
            device_id_type=MESH,
        )
        copy.start()
        started.append(copy)
        return copy

    def region(a, b):
        start, rows = regions[a, b]
        return pl.ds(start, rows)

    field_copies, fill_copies = [], []
    for n, (a, b) in enumerate(diagonals):
        field_copies.append(send(xy_send.at[n], field.at[region(-a, -b)], (a, b, 0)))
    for a in (1, -1):
        source = pl.ds(24, 40) if a == 1 else pl.ds(0, 40)
        field_copies.append(send(field.at[source], field.at[region(-a, 0)], (a, 0, 0)))
    for flow in flows:
        if flow[2] != 0:
            n = flow_index[flow]
            if flow[0] != 0 and flow[1] != 0:
                source, target = z_send.at[side[flow[2]], 0], z_recv.at[n, 0]
            elif flow in mixed:
                source, target = mixed_send.at[mixed.index(flow)], z_recv.at[n, 0]
            else:
                source, target = z_send.at[side[flow[2]]], z_recv.at[n]
            field_copies.append(send(source, target, flow))
    for b in (1, -1):
        field_copies.append(send(y_field.at[side[b]], field.at[region(0, -b)], (0, b, 0)))
    def one_if(condition):
        return jnp.where(condition, 1.0, 0.0).astype(F32)

    x_low, x_high = one_if(gx == 0), one_if(gx == nx - 1)
    y_low, y_high = one_if(gy == 0), one_if(gy == ny - 1)
    z_low, z_high = one_if(gz == 0), one_if(gz == nz - 1)
    lanes_x, lanes_y = outer_cells()
    lanes_x = cut(lanes_x, 7.0, x_low, x_high)
    lanes_y = cut(lanes_y, 7.0, y_low, y_high)
    wide = lax.broadcasted_iota(jnp.int32, (1, 384), 1)
    plain_z = jnp.where(wide < 128, wide, jnp.where(wide < 256, wide - 129, wide - 255)).astype(F32)
    lanes_z = cut(plain_z, 127.0, z_low, z_high)
    line = lax.broadcasted_iota(jnp.int32, (1, 128), 1)
    tenth = lax.shift_right_logical(line * 205, 11)
    part_ten = line - 10 * tenth
    blocks_x = cut(jnp.where(tenth < 10, tenth - 1, 12288).astype(F32), 7.0, x_low, x_high)
    blocks_part = jnp.where(part_ten < 5, part_ten, part_ten + 3)
    stack_y = cut(jnp.where(line < 24, line - 8, 12288).astype(F32), 7.0, y_low, y_high)
    lane_scale = 1.0 / weight_total(plain_z + (gz * 128).astype(F32), 128.0 * nz)

    def build_rows(t, carry):
        rows = pl.ds(pl.multiple_of(t * 16, 16), 16)
        index = lax.broadcasted_iota(jnp.int32, (16, 128), 0) + t * 16
        tile = lax.shift_right_logical(index, 3)
        late = jnp.where(tile >= 20, 2, jnp.where(tile >= 10, 1, 0))
        plane = tile - 10 * late
        x = (plane - 1).astype(F32)
        y = (jnp.bitwise_and(index, 7) - jnp.where(late == 1, 1, jnp.where(late == 2, -1, 0))).astype(F32)
        row_scale[rows, :] = 1.0 / (
            weight_total(x + (gx * 8).astype(F32), 8.0 * nx)
            * weight_total(y + (gy * 8).astype(F32), 8.0 * ny)
        )
        cut_x = cut(x, 7.0, x_low, x_high)
        cut_y = cut(y, 7.0, y_low, y_high)
        wide_x = jnp.concatenate([cut_x] * 3, axis=1)
        wide_y = jnp.concatenate([cut_y] * 3, axis=1)
        weights = hat(wide_x - lanes_x) * hat(wide_y - lanes_y)
        big_l_wide[rows, :] = weights
        big_l[rows, :] = weights.astype(BF16)
        repeated = hat(cut_y - stack_y)
        rep_l_wide[rows, :] = repeated
        rep_l[rows, :] = repeated.astype(BF16)
        block_mask[rows, :] = jnp.where(tenth == plane, 1.0, 0.0)
        return carry

    lax.fori_loop(0, 16, build_rows, 0)
    for a in (1, -1):
        fill_copies.append(send(x_send.at[side[a]], x_recv.at[side[a]], (a, 0, 0)))
    for b in (1, -1):
        fill_copies.append(
            send(y_send.at[side[b]], y_rows.at[side[b], :, pl.ds(8, 8), :], (0, b, 0))
        )

    big_lt[...] = big_l_wide[...].T.astype(BF16)
    rep_lt[...] = rep_l_wide[...].T[0:32, :].astype(BF16)

    def build_cross(t, carry):
        rows = pl.ds(pl.multiple_of(t * 16, 16), 16)
        x = cut((t - 8).astype(F32), 7.0, x_low, x_high)
        same = lax.broadcasted_iota(jnp.int32, (16, 128), 0) == blocks_part
        weights = jnp.where(same, hat(x - blocks_x), 0.0)
        wide_x_v[rows, :] = weights
        cross_x[rows, :] = weights.astype(BF16)
        return carry

    lax.fori_loop(0, 24, build_cross, 0)

    def build_z(t, carry):
        rows = pl.ds(pl.multiple_of(t * 16, 16), 16)
        index = lax.broadcasted_iota(jnp.int32, (16, 384), 0) + t * 16
        halo = index - 128
        halo = halo - 10 * lax.shift_right_logical(halo * 205, 11)
        halo = jnp.where(halo < 5, halo - 5, halo + 123)
        z = cut(jnp.where(index < 128, index, halo).astype(F32), 127.0, z_low, z_high)
        weights = hat(z - lanes_z)
        wide_z_v[rows, :] = weights
        cross_z[rows, :] = weights.astype(BF16)
        return carry

    lax.fori_loop(0, 16, build_z, 0)
    cross_xt[...] = wide_x_v[...].T.astype(BF16)
    cross_zt[...] = wide_z_v[...].T.astype(BF16)
    grad_v[...] = jnp.zeros_like(grad_v)

    for copy in field_copies[:6] + field_copies[-2:]:
        copy.wait_recv()
    inner_xy = left_dot(big_l[...], field[...])
    for copy in field_copies[6:-2]:
        copy.wait_recv()
    part = jnp.bitwise_and(lane, 15)
    stacked = []
    for b in (-1, 0, 1):
        tiles = []
        for a in (-1, 0, 1):
            below = z_recv[flow_index[-a, -b, 1], 0]
            above = z_recv[flow_index[-a, -b, -1], 0]
            tiles.append(jnp.where(part < 8, below, above))
        stacked.append(jnp.concatenate(tiles, axis=1))
    stacked.append(jnp.zeros((8, 384), F32))
    halo_x = right_dot(jnp.concatenate(stacked, axis=0), cross_x[...])
    halo_x = jnp.concatenate([halo_x, jnp.zeros((96, 128), F32)], axis=0)
    halo_xy = left_dot(rep_l[...], halo_x) * block_mask[...]
    summed = right_dot(jnp.concatenate([inner_xy, halo_xy], axis=1), cross_z[...])
    scale_rows = jnp.concatenate([row_scale[...]] * 3, axis=1)
    scale_all = scale_rows * (-0.5 * lane_scale)
    kappa_v[...] = 0.5 + summed * scale_all

    for copy in fill_copies[2:]:
        copy.wait_recv()
    eighth = lax.shift_right_logical(lane, 3)
    slot = eighth - jnp.where(eighth >= 10, 10, jnp.where(eighth >= 5, 5, 0))
    for sign in (1, -1):
        base = z_recv[flow_index[0, 0, sign], 1]
        total = base
        for s, j in enumerate(crossing[2, sign]):
            a, b, _ = velocities[j]
            if a != 0:
                corner = z_recv[flow_index[a, 0, sign], 0]
                moved = pltpu.roll(base, a % 128, 1)
                for k in range(3):
                    free = k if a == 1 else 112 + k
                    place = 40 * k + 8 * s + (0 if a == 1 else 7)
                    moved = jnp.where(
                        lane == place, pltpu.roll(corner, (place - free) % 128, 1), moved
                    )
            elif b != 0:
                corner = z_recv[flow_index[0, b, sign], 0]
                moved = jnp.where(row == (0 if b == 1 else 7), corner, pltpu.roll(base, b % 8, 0))
            else:
                continue
            total = jnp.where(slot == s, moved, total)
        z_pack[side[sign]] = total

    def plane_step(x, carry):
        def stream(k, j):
            a, b, c = velocities[j]
            tile = own(k, j, pl.ds(aligned(x + 1 - a), 8))
            if b != 0:
                s = crossing[1, b].index(j)
                line = y_rows[side[b], 5 * k + s, pl.ds(8 + x - a, 1), :]
                tile = jnp.where(
                    row == (0 if b == 1 else 7), line, pltpu.roll(tile, b % 8, 0)
                )
            if c != 0:
                s = crossing[2, c].index(j)
                edge = 0 if c == 1 else 127
                place = k * 40 + s * 8 + x
                column = pltpu.roll(
                    z_pack[side[c]], jnp.bitwise_and(256 + edge - place, 127), 1
                )
                tile = jnp.where(lane == edge, column, pltpu.roll(tile, c % 128, 1))
            return tile

        def spot(j):
            a, b, c = velocities[j]
            return (
                pl.ds(aligned(kind[b] * 10 + x + 1 - a), 8),
                pl.ds(128 * kind[c], 128),
            )

        center = pl.ds(aligned(x + 1), 8)
        flags = flags_v[pl.ds(aligned(x), 8), :]
        state, slopes = [first_v[0, center, :]], [None]
        weights = [seed_v[0, center, :]] + [None] * 18
        for j in range(1, 19):
            slope = stream(1, j)
            rows, lanes = spot(j)
            change = kappa_v[rows, lanes] * slope
            before = stream(0, j)
            state.append(before + change if j % 2 == 1 else before - change)
            slopes.append(slope)
            weights[opposite[j]] = stream(2, j)
        kappa = kappa_v[center, 0:128]
        back, here = adjoint_collision(state, weights, kappa, flags)
        grad_v[center, 0:128] += here
        for j in range(1, 19):
            rows, lanes = spot(j)
            if j % 2 == 1:
                grad_v[rows, lanes] += slopes[j] * back[j]
            else:
                grad_v[rows, lanes] -= slopes[j] * back[j]
        return carry

    lax.fori_loop(1, 7, plane_step, 0, unroll=6)
    for copy in fill_copies[:2]:
        copy.wait_recv()
    for sign in (1, -1):
        n = side[sign]
        rows = pl.ds(0, 8) if sign == 1 else pl.ds(72, 8)
        for s, j in enumerate(crossing[0, sign]):
            first_v[j, rows, :] = x_recv[n, s]
            slope_v[(j - 1) // 2, rows, :] = x_recv[n, 5 + s]
            seed_v[opposite[j], rows, :] = x_recv[n, 10 + s]
    for a, b in diagonals:
        j = velocities.index((a, b, 0))
        s = crossing[1, b].index(j)
        start = regions[-a, -b][0]
        for k in range(3):
            y_rows[side[b], 5 * k + s, pl.ds(7 if a == 1 else 16, 1), :] = field[
                pl.ds(start + 25 + k, 1), :
            ]
    lax.fori_loop(0, 2, lambda n, carry: plane_step(7 * n, carry), 0, unroll=2)

    scaled = grad_v[...] * scale_all
    summed = right_dot(scaled, cross_zt[...])
    spread[pl.ds(64, 320), :] = left_dot(big_lt[pl.ds(64, 320), :], summed[:, 0:128])
    spread_copies = []
    for flow in flows:
        a, b, c = flow
        if c == 0:
            spread_copies.append(
                send(spread.at[region(a, b)], spread_recv.at[region(a, b)], flow)
            )
    halo_x = left_dot(rep_lt[...], summed[:, 128:256] * block_mask[...])
    halo = right_dot(halo_x, cross_xt[...])
    for b in range(3):
        for a in range(3):
            q_out[3 * b + a] = halo[8 * b : 8 * b + 8, 128 * a : 128 * a + 128]
    for flow in flows:
        a, b, c = flow
        if c != 0:
            spread_copies.append(
                send(q_out.at[3 * (b + 1) + a + 1], q_recv.at[flow_index[flow]], flow)
            )
    spread[pl.ds(0, 64), :] = left_dot(big_lt[pl.ds(0, 64), :], summed[:, 0:128])
    arrived = dict(zip([f for f in flows if f[2] == 0] + [f for f in flows if f[2] != 0], spread_copies))
    for b in (1, -1):
        arrived[0, b, 0].wait_recv()
        for r in range(5):
            y = r if b == 1 else 3 + r
            spread[pl.ds(y, 8, stride=8), :] += spread_recv[
                pl.ds(regions[0, b][0] + 8 * r, 8), :
            ]
    for flow in reversed(flows):
        if flow[2] != 0:
            arrived[flow].wait_recv()
    up = add_all([q_recv[flow_index[a, b, 1]] for a in (-1, 0, 1) for b in (-1, 0, 1)])
    down = add_all([q_recv[flow_index[a, b, -1]] for a in (-1, 0, 1) for b in (-1, 0, 1)])
    for x in range(8):
        first = pltpu.roll(up, (128 - 16 * x - 8) % 128, 1)
        last = pltpu.roll(down, (123 - 16 * x) % 128, 1)
        spread[pl.ds(8 * x, 8), :] += jnp.where(
            lane < 5, first, jnp.where(lane >= 123, last, 0.0)
        )
    arrived[-1, 0, 0].wait_recv()
    spread[pl.ds(24, 40), :] += spread_recv[region(-1, 0), :]
    arrived[1, 0, 0].wait_recv()
    spread[pl.ds(0, 40), :] += spread_recv[region(1, 0), :]
    for a, b in diagonals:
        arrived[a, b, 0].wait_recv()
        for r in range(5):
            y = r if b == 1 else 3 + r
            spread[pl.ds(y + (0 if a == 1 else 24), 5, stride=8), :] += spread_recv[
                pl.ds(regions[a, b][0] + 5 * r, 5), :
            ]
    squares = blank
    for x in range(8):
        tile = spread[pl.ds(8 * x, 8), :]
        squares = squares + tile * tile

    result_copy = pltpu.make_async_copy(spread.at[pl.ds(0, 64)], out_ref, local_sem.at[0])
    result_copy.start()

    mine = gy * nz + gz
    ring_a[mine] = jnp.sum(squares, axis=0, keepdims=True)
    before = list(started)
    ring_copies = [send(ring_a.at[mine], ring_a.at[mine], move) for move in slab_moves]
    for copy in before:
        copy.wait_send()
    for copy in reversed(ring_copies):
        copy.wait_recv()
    ring_b[gx] = jnp.sum(ring_a[...], axis=0)
    before = ring_copies
    ring_copies = [send(ring_b.at[gx], ring_b.at[gx], move) for move in line_moves]
    for copy in before:
        copy.wait_send()
    result_copy.wait()
    for copy in ring_copies:
        copy.wait_send()
    for copy in reversed(ring_copies):
        copy.wait_recv()
    total = jnp.sum(jnp.sum(ring_b[...], axis=0), axis=1, keepdims=True)
    mean_square = total / (8192.0 * nx * ny * nz)
    rms_ref[...] = jnp.broadcast_to(mean_square, (8, 128))


def finish(raw_ref, mean_ref, out_ref, rms_ref):
    mean_square = mean_ref[0:1, 0:1]
    out_ref[...] = raw_ref[...] * lax.rsqrt(mean_square + norm_eps)
    rms_ref[...] = jnp.sqrt(mean_square)


def solution(mesh):
    sizes = tuple(mesh.shape[name] for name in ("gx", "gy", "gz"))
    copies = 4 + 2 + 18 + 2 + 2 + 2 + 26 + (sizes[1] * sizes[2] - 1) + (sizes[0] - 1)

    def body(populations, design, flags, adjoint_seed):
        anywhere = pl.BlockSpec(memory_space=pl.ANY)
        inside = pl.BlockSpec(memory_space=pltpu.VMEM)
        scratch = [
            pltpu.VMEM((19, 64, 128), F32),
            pltpu.VMEM((64, 128), jnp.int32),
            pltpu.VMEM((19, 80, 128), F32),
            pltpu.VMEM((9, 80, 128), F32),
            pltpu.VMEM((19, 80, 128), F32),
            pltpu.VMEM((384, 128), F32),
            pltpu.VMEM((2, 15, 8, 128), F32),
            pltpu.VMEM((2, 15, 8, 128), F32),
            pltpu.VMEM((2, 40, 128), F32),
            pltpu.VMEM((2, 15, 8, 128), F32),
            pltpu.VMEM((2, 15, 24, 128), F32),
            pltpu.VMEM((4, 32, 128), F32),
            pltpu.VMEM((8, 8, 128), F32),
            pltpu.VMEM((2, 2, 8, 128), F32),
            pltpu.VMEM((26, 2, 8, 128), F32),
            pltpu.VMEM((2, 8, 128), F32),
            pltpu.VMEM((256, 384), F32),
            pltpu.VMEM((256, 384), F32),
            pltpu.VMEM((384, 128), F32),
            pltpu.VMEM((384, 128), F32),
            pltpu.VMEM((9, 8, 128), F32),
            pltpu.VMEM((26, 8, 128), F32),
            pltpu.VMEM((sizes[1] * sizes[2], 1, 128), F32),
            pltpu.VMEM((sizes[0], 1, 128), F32),
            pltpu.VMEM((256, 384), BF16),
            pltpu.VMEM((256, 384), F32),
            pltpu.VMEM((384, 256), BF16),
            pltpu.VMEM((256, 128), BF16),
            pltpu.VMEM((256, 128), F32),
            pltpu.VMEM((32, 256), BF16),
            pltpu.VMEM((384, 128), BF16),
            pltpu.VMEM((256, 384), BF16),
            pltpu.VMEM((128, 384), BF16),
            pltpu.VMEM((384, 256), BF16),
            pltpu.VMEM((384, 128), F32),
            pltpu.VMEM((256, 384), F32),
            pltpu.VMEM((256, 128), F32),
            pltpu.VMEM((256, 128), F32),
            pltpu.SemaphoreType.DMA((5,)),
            pltpu.SemaphoreType.DMA((copies,)),
            pltpu.SemaphoreType.DMA((copies,)),
        ]
        grad, rms = pl.pallas_call(
            functools.partial(kernel, sizes),
            out_shape=(
                jax.ShapeDtypeStruct((64, 128), F32),
                jax.ShapeDtypeStruct((8, 128), F32),
            ),
            in_specs=[anywhere] * 4,
            out_specs=(anywhere, inside),
            scratch_shapes=scratch,
            compiler_params=pltpu.CompilerParams(
                collective_id=0, has_side_effects=True, vmem_limit_bytes=56491008
            ),
        )(
            populations.reshape(19, 64, 128),
            design.reshape(64, 128),
            flags.reshape(64, 128),
            adjoint_seed.reshape(19, 64, 128),
        )
        grad, rms = pl.pallas_call(
            finish,
            out_shape=(
                jax.ShapeDtypeStruct((64, 128), F32),
                jax.ShapeDtypeStruct((1, 1), F32),
            ),
            in_specs=[inside, inside],
            out_specs=(inside, inside),
            name="scale_gradient",
            compiler_params=pltpu.CompilerParams(vmem_limit_bytes=1024 * 1024),
        )(grad, rms)
        return grad.reshape(8, 8, 128), rms.reshape(())

    return jax.shard_map(
        body,
        mesh=mesh,
        in_specs=(
            P(None, "gx", "gy", "gz"),
            P("gx", "gy", "gz"),
            P("gx", "gy", "gz"),
            P(None, "gx", "gy", "gz"),
        ),
        out_specs=(P("gx", "gy", "gz"), P()),
        check_vma=False,
    )
```

```python
import functools

import jax
import jax.numpy as jnp
from jax import lax
from jax.experimental import pallas as pl
from jax.experimental.pallas import tpu as pltpu
from jax.sharding import PartitionSpec as P

MESH = pl.DeviceIdType.MESH
F32 = jnp.float32
BF16 = jnp.bfloat16

velocities = [
    (0, 0, 0),
    (1, 0, 0),
    (-1, 0, 0),
    (0, 1, 0),
    (0, -1, 0),
    (0, 0, 1),
    (0, 0, -1),
    (1, 1, 0),
    (-1, -1, 0),
    (1, -1, 0),
    (-1, 1, 0),
    (1, 0, 1),
    (-1, 0, -1),
    (1, 0, -1),
    (-1, 0, 1),
    (0, 1, 1),
    (0, -1, -1),
    (0, 1, -1),
    (0, -1, 1),
]
opposite = [0, 2, 1, 4, 3, 6, 5, 8, 7, 10, 9, 12, 11, 14, 13, 16, 15, 18, 17]
pair_weights = [1.0 / 18.0] * 3 + [1.0 / 36.0] * 6
relax_rate = 1.6
inlet_speed = 0.05
norm_eps = 1e-06
FAR = 4096.0

crossing = {
    (0, 1): [1, 7, 9, 11, 13],
    (0, -1): [2, 8, 10, 12, 14],
    (1, 1): [3, 7, 10, 15, 17],
    (1, -1): [4, 8, 9, 16, 18],
    (2, 1): [5, 11, 14, 15, 18],
    (2, -1): [6, 12, 13, 16, 17],
}
side = {1: 0, -1: 1}
kind = {0: 0, 1: 1, -1: 2}

regions = {(0, 0): (0, 64)}
for order, where_ in enumerate([(-1, 0), (1, 0), (0, -1), (0, 1), (-1, -1), (-1, 1), (1, -1), (1, 1)]):
    regions[where_] = (64 + 40 * order, 40) if order < 4 else (96 + 32 * order, 32)

flows = [
    (a, b, c) for a in (1, -1, 0) for b in (1, -1, 0) for c in (1, -1, 0) if a or b or c
]
flow_index = {flow: number for number, flow in enumerate(flows)}


def outer_cells():
    r = lax.broadcasted_iota(jnp.int32, (1, 384), 1)
    low = jnp.bitwise_and(r, 7)
    tile = lax.shift_right_logical(r, 3)
    x = jnp.where(r < 64, tile, jnp.where(r < 104, tile - 13, jnp.where(r < 144, tile - 5, low)))
    y = jnp.where(r < 144, low, jnp.where(r < 184, tile - 23, tile - 15))
    k = jnp.bitwise_and(r, 31)
    edge = lax.shift_right_logical(r, 5) - 7
    part_y = lax.shift_right_logical(k * 13, 6)
    part_x = k - 5 * part_y
    edge_x = jnp.where(edge < 2, part_x - 5, part_x + 8)
    edge_y = jnp.where(jnp.bitwise_and(edge, 1) == 0, part_y - 5, part_y + 8)
    used = jnp.logical_and(k < 25, edge < 4)
    x = jnp.where(r < 224, x, jnp.where(used, edge_x, 12288))
    y = jnp.where(r < 224, y, jnp.where(used, edge_y, 12288))
    return x.astype(F32), y.astype(F32)


def split(value):
    high = value.astype(BF16)
    return high, (value - high.astype(F32)).astype(BF16)


def left_dot(matrix, value):
    both = jnp.dot(
        matrix, jnp.concatenate(split(value), axis=1), preferred_element_type=F32
    )
    width = value.shape[1]
    return both[:, :width] + both[:, width:]


def right_dot(value, matrix):
    high, low = split(value)
    return jnp.dot(high, matrix, preferred_element_type=F32) + jnp.dot(
        low, matrix, preferred_element_type=F32
    )


def right_dot_t(value, matrix):
    high, low = split(value)
    dims = (((1,), (1,)), ((), ()))
    return lax.dot_general(high, matrix, dims, preferred_element_type=F32) + lax.dot_general(
        low, matrix, dims, preferred_element_type=F32
    )


def triangle(n):
    return 0.5 * n * (n + 1.0)


def weight_total(position, count):
    position = jnp.where(position < 0, position + count, position)
    position = jnp.where(position > count - 1, position - count, position)
    return (
        25.0
        - triangle(jnp.maximum(0.0, 4.0 - position))
        - triangle(jnp.maximum(0.0, position - (count - 5.0)))
    )


def cut(value, last, low, high):
    return (
        value
        - jnp.where(value < 0, FAR, 0.0) * low
        + jnp.where(value > last, FAR, 0.0) * high
    )


def hat(difference):
    return jnp.maximum(0.0, 5.0 - jnp.abs(difference))


def add_all(terms):
    terms = list(terms)
    while len(terms) > 1:
        terms = [
            terms[n] + terms[n + 1] if n + 1 < len(terms) else terms[n]
            for n in range(0, len(terms), 2)
        ]
    return terms[0]


def project(c, vector):
    total = None
    for component, value in zip(c, vector):
        if component == 1:
            total = value if total is None else total + value
        elif component == -1:
            total = -value if total is None else total - value
    return total


def momentum(t):
    return (
        add_all([t[0], t[3] + t[4], t[5] + t[6]]),
        add_all([t[1], t[3] - t[4], t[7] + t[8]]),
        add_all([t[2], t[5] - t[6], t[7] - t[8]]),
    )


def cell_kinds(flags):
    omega = jnp.where(flags == 3, 1.0, relax_rate)
    solid = flags == 1
    inlet = flags == 2
    blocked = jnp.logical_or(solid, inlet)
    keep = 1.0 - omega
    even = jnp.where(solid, 1.0, jnp.where(inlet, 0.0, keep))
    odd = jnp.where(solid, -1.0, jnp.where(inlet, 0.0, keep))
    fluid_omega = jnp.where(blocked, 0.0, omega)
    return omega, keep, solid, inlet, blocked, even, odd, fluid_omega


def first_collision(f, flags):
    omega, keep, solid, inlet, blocked, even, odd, fluid_omega = cell_kinds(flags)
    rate = jnp.where(inlet, 1.0, fluid_omega)
    s = [f[2 * p + 1] + f[2 * p + 2] for p in range(9)]
    t = [f[2 * p + 1] - f[2 * p + 2] for p in range(9)]
    rho = jnp.where(inlet, 1.0, add_all([f[0]] + s))
    mx, my, mz = momentum(t)
    mx = jnp.where(inlet, inlet_speed, mx)
    my = jnp.where(inlet, 0.0, my)
    mz = jnp.where(inlet, 0.0, mz)
    inverse = 1.0 / rho
    base = rho - 1.5 * (mx * mx + my * my + mz * mz) * inverse
    bend = 4.5 * inverse
    half_even, half_odd = 0.5 * even, 0.5 * odd
    base_a, base_b = rate * pair_weights[0], rate * pair_weights[3]
    first = [even * f[0] + rate * (1.0 / 3.0) * base]
    slope = []
    for p in range(9):
        along = project(velocities[2 * p + 1], (mx, my, mz))
        weight = base_a if p < 3 else base_b
        symmetric = half_even * s[p] + weight * (base + bend * (along * along))
        skew = half_odd * t[p] + (3.0 * weight) * along
        first += [symmetric + skew, symmetric - skew]
        slope.append(jnp.where(blocked, 0.0, -2.0 * skew))
    return first, slope


def adjoint_collision(f, a, kappa, flags):
    omega, keep, solid, inlet, blocked, even, odd, fluid_omega = cell_kinds(flags)
    pass_back = 1.0 - 2.0 * kappa
    s = [f[2 * p + 1] + f[2 * p + 2] for p in range(9)]
    t = [f[2 * p + 1] - f[2 * p + 2] for p in range(9)]
    rho = add_all([f[0]] + s)
    mx, my, mz = momentum(t)
    inverse = 1.0 / rho
    ux, uy, uz = mx * inverse, my * inverse, mz * inverse
    even_a = [a[2 * p + 1] + a[2 * p + 2] for p in range(9)]
    odd_a = [a[2 * p + 1] - a[2 * p + 2] for p in range(9)]
    ws = [pair_weights[p] * even_a[p] for p in range(9)]
    wt = [pair_weights[p] * odd_a[p] for p in range(9)]
    b0 = add_all([(1.0 / 3.0) * a[0]] + ws)
    b1x, b1y, b1z = momentum(wt)
    bxx = add_all([ws[0], ws[3] + ws[4], ws[5] + ws[6]])
    byy = add_all([ws[1], ws[3] + ws[4], ws[7] + ws[8]])
    bzz = add_all([ws[2], ws[5] + ws[6], ws[7] + ws[8]])
    bxy, bxz, byz = ws[3] - ws[4], ws[5] - ws[6], ws[7] - ws[8]
    vx = bxx * ux + bxy * uy + bxz * uz
    vy = bxy * ux + byy * uy + byz * uz
    vz = bxz * ux + byz * uy + bzz * uz
    moved = 3.0 * (mx * b1x + my * b1y + mz * b1z)
    kept = add_all([odd_a[p] * t[p] for p in range(9)])
    slope = jnp.where(blocked, 0.0, -(keep * kept + 2.0 * omega * moved))
    usq = ux * ux + uy * uy + uz * uz
    to_rho = fluid_omega * (b0 * (1.0 + 1.5 * usq) - 4.5 * (ux * vx + uy * vy + uz * vz))
    back = 3.0 * pass_back
    gx = fluid_omega * (back * b1x + 9.0 * vx - 3.0 * ux * b0)
    gy = fluid_omega * (back * b1y + 9.0 * vy - 3.0 * uy * b0)
    gz = fluid_omega * (back * b1z + 9.0 * vz - 3.0 * uz * b0)
    half_even = 0.5 * even
    half_odd = 0.5 * jnp.where(blocked, odd, odd * pass_back)
    result = [even * a[0] + to_rho]
    for p in range(9):
        along = project(velocities[2 * p + 1], (gx, gy, gz))
        symmetric = half_even * even_a[p] + to_rho
        skew = half_odd * odd_a[p] + along
        result += [symmetric + skew, symmetric - skew]
    return result, slope


def aligned(index):
    return pl.multiple_of(index * 8, 8)


def kernel(
    sizes,
    pop_in,
    design_in,
    flags_in,
    seed_in,
    out_ref,
    rms_ref,
    pops,
    flags_v,
    first_v,
    slope_v,
    seed_v,
    turned,
    field,
    x_send,
    x_recv,
    y_field,
    y_send,
    y_rows,
    xy_send,
    mixed_send,
    z_send,
    z_recv,
    z_pack,
    kappa_v,
    grad_v,
    spread,
    spread_recv,
    q_out,
    q_recv,
    ring_a,
    ring_b,
    big_l,
    big_l_wide,
    big_lt,
    rep_l,
    rep_l_wide,
    rep_lt,
    cross_x,
    cross_z,
    cross_xt,
    cross_zt,
    wide_x_v,
    wide_z_v,
    block_mask,
    row_scale,
    local_sem,
    send_sem,
    recv_sem,
):
    nx, ny, nz = sizes
    gx, gy, gz = lax.axis_index("gx"), lax.axis_index("gy"), lax.axis_index("gz")

    def around(start, length):
        if length & (length - 1) == 0:
            return [jnp.bitwise_and(start + n, length - 1) for n in range(length)]
        return [lax.rem(start + n, length) for n in range(length)]

    place_x, place_y, place_z = around(gx, nx), around(gy, ny), around(gz, nz)

    def device(move):
        return place_x[move[0] % nx], place_y[move[1] % ny], place_z[move[2] % nz]

    slab_moves = [(0, b, c) for b in range(ny) for c in range(nz) if b or c]
    slab_moves.sort(key=lambda m: -(min(m[1], ny - m[1]) + min(m[2], nz - m[2])))
    line_moves = [(a, 0, 2 * (a % 2)) for a in range(1, nx)]
    line_moves.sort(key=lambda m: -(min(m[0], nx - m[0]) + 2 * (m[0] % 2)))

    def key(move):
        return (move[0] % nx, move[1] % ny, move[2] % nz)

    partners = []
    for move in line_moves + flows + slab_moves:
        if key(move) not in partners:
            partners.append(key(move))
    barrier = pltpu.get_barrier_semaphore()
    for move in partners:
        pl.semaphore_signal(barrier, inc=1, device_id=device(move), device_id_type=MESH)

    loads = [
        pltpu.make_async_copy(pop_in, pops, local_sem.at[1]),
        pltpu.make_async_copy(flags_in, flags_v, local_sem.at[2]),
        pltpu.make_async_copy(seed_in, seed_v.at[:, pl.ds(8, 64), :], local_sem.at[3]),
        pltpu.make_async_copy(design_in, field.at[pl.ds(0, 64)], local_sem.at[4]),
    ]
    for load in loads:
        load.start()
    for load in loads:
        load.wait()

    lane = lax.broadcasted_iota(jnp.int32, (8, 128), 1)
    row = lax.broadcasted_iota(jnp.int32, (8, 128), 0)

    def own(k, j, rows):
        if k == 0:
            return first_v[j, rows, :]
        if k == 1:
            return slope_v[(j - 1) // 2, rows, :]
        return seed_v[opposite[j], rows, :]

    def start_step(x, carry):
        rows = pl.ds(aligned(x), 8)
        inner = pl.ds(aligned(x + 1), 8)
        first, slope = first_collision([pops[i, rows, :] for i in range(19)], flags_v[rows, :])
        for i in range(19):
            first_v[i, inner, :] = first[i]
        for p in range(9):
            slope_v[p, inner, :] = slope[p]
        packs = list(carry[:2])
        for n, sign in enumerate((1, -1)):
            edge = 127 if sign == 1 else 0
            for k in range(3):
                for s, j in enumerate(crossing[2, sign]):
                    tile = (
                        first[j]
                        if k == 0
                        else slope[(j - 1) // 2]
                        if k == 1
                        else seed_v[opposite[j], inner, :]
                    )
                    place = k * 40 + s * 8 + x
                    moved = pltpu.roll(tile, jnp.bitwise_and(place + 128 - edge, 127), 1)
                    packs[n] = jnp.where(lane == place, moved, packs[n])
        tile = field[rows, :]
        quad = carry[2]
        here = lax.shift_right_logical(lane, 4) == x
        part = jnp.bitwise_and(lane, 15)
        high = pltpu.roll(tile, jnp.bitwise_and(16 * x + 5, 127), 1)
        low = pltpu.roll(tile, jnp.bitwise_and(16 * x + 8, 127), 1)
        quad = jnp.where(jnp.logical_and(here, part < 5), high, quad)
        quad = jnp.where(
            jnp.logical_and(here, jnp.logical_and(part >= 8, part < 13)), low, quad
        )
        return packs[0], packs[1], quad

    blank = jnp.zeros((8, 128), F32)
    pack_up, pack_down, quad = lax.fori_loop(0, 8, start_step, (blank, blank, blank), unroll=2)
    z_send[0, 0] = quad
    z_send[1, 0] = quad
    z_send[0, 1] = pack_up
    z_send[1, 1] = pack_down
    for sign in (1, -1):
        n = side[sign]
        edge = 7 if sign == 1 else 0
        for k in range(3):
            for s, j in enumerate(crossing[0, sign]):
                x_send[n, 5 * k + s] = own(k, j, pl.ds(8 * (edge + 1), 8))
            for s, j in enumerate(crossing[1, sign]):
                y_send[n, 5 * k + s] = own(k, j, pl.ds(8 + edge, 8, stride=8))
        for r in range(5):
            y_field[n, pl.ds(8 * r, 8), :] = field[
                pl.ds(3 + r if sign == 1 else r, 8, stride=8), :
            ]
    packs = {1: pack_up, -1: pack_down}
    mixed = [flow for flow in flows if flow[2] and (flow[0] == 0) != (flow[1] == 0)]
    for n, (a, b, c) in enumerate(mixed):
        if a:
            s = crossing[2, c].index(velocities.index((a, b, c)))
            tile = quad
            for k in range(3):
                free = k if a == 1 else 112 + k
                place = 40 * k + 8 * s + (7 if a == 1 else 0)
                tile = jnp.where(
                    lane == free, pltpu.roll(packs[c], (free - place) % 128, 1), tile
                )
        elif b == 1:
            tile = jnp.where(row == 0, pltpu.roll(packs[c], 1, 0), quad)
        else:
            tile = jnp.where(row == 7, pltpu.roll(packs[c], 7, 0), quad)
        mixed_send[n] = tile
    diagonals = [(a, b) for a in (1, -1) for b in (1, -1)]
    for n, (a, b) in enumerate(diagonals):
        j = velocities.index((a, b, 0))
        for r in range(5):
            at = (24 if a == 1 else 0) + (3 + r if b == 1 else r)
            xy_send[n, pl.ds(5 * r, 5), :] = field[pl.ds(at, 5, stride=8), :]
        for k in range(3):
            at = (8 if a == 1 else 1) * 8 + (7 if b == 1 else 0)
            xy_send[n, pl.ds(25 + k, 1), :] = own(k, j, pl.ds(at, 1))
        xy_send[n, pl.ds(28, 4), :] = jnp.zeros((4, 128), F32)

    pl.semaphore_wait(barrier, len(partners))
    count = [0]
    started = []

    def send(source, target, move):
        n = count[0]
        count[0] += 1
        copy = pltpu.make_async_remote_copy(
            src_ref=source,
            dst_ref=target,
            send_sem=send_sem.at[n],
            recv_sem=recv_sem.at[n],
            device_id=device(move),
            device_id_type=MESH,
        )
        copy.start()
        started.append(copy)
        return copy

    def region(a, b):
        start, rows = regions[a, b]
        return pl.ds(start, rows)

    field_copies, fill_copies = [], []
    for n, (a, b) in enumerate(diagonals):
        field_copies.append(send(xy_send.at[n], field.at[region(-a, -b)], (a, b, 0)))
    for a in (1, -1):
        source = pl.ds(24, 40) if a == 1 else pl.ds(0, 40)
        field_copies.append(send(field.at[source], field.at[region(-a, 0)], (a, 0, 0)))
    for flow in flows:
        if flow[2] != 0:
            n = flow_index[flow]
            if flow[0] != 0 and flow[1] != 0:
                source, target = z_send.at[side[flow[2]], 0], z_recv.at[n, 0]
            elif flow in mixed:
                source, target = mixed_send.at[mixed.index(flow)], z_recv.at[n, 0]
            else:
                source, target = z_send.at[side[flow[2]]], z_recv.at[n]
            field_copies.append(send(source, target, flow))
    for b in (1, -1):
        field_copies.append(send(y_field.at[side[b]], field.at[region(0, -b)], (0, b, 0)))
    for a in (1, -1):
        fill_copies.append(send(x_send.at[side[a]], x_recv.at[side[a]], (a, 0, 0)))
    for b in (1, -1):
        fill_copies.append(
            send(y_send.at[side[b]], y_rows.at[side[b], :, pl.ds(8, 8), :], (0, b, 0))
        )

    def one_if(condition):
        return jnp.where(condition, 1.0, 0.0).astype(F32)

    x_low, x_high = one_if(gx == 0), one_if(gx == nx - 1)
    y_low, y_high = one_if(gy == 0), one_if(gy == ny - 1)
    z_low, z_high = one_if(gz == 0), one_if(gz == nz - 1)
    lanes_x, lanes_y = outer_cells()
    lanes_x = cut(lanes_x, 7.0, x_low, x_high)
    lanes_y = cut(lanes_y, 7.0, y_low, y_high)
    wide = lax.broadcasted_iota(jnp.int32, (1, 384), 1)
    plain_z = jnp.where(wide < 128, wide, jnp.where(wide < 256, wide - 129, wide - 255)).astype(F32)
    lanes_z = cut(plain_z, 127.0, z_low, z_high)
    line = lax.broadcasted_iota(jnp.int32, (1, 128), 1)
    tenth = lax.shift_right_logical(line * 205, 11)
    part_ten = line - 10 * tenth
    blocks_x = cut(jnp.where(tenth < 10, tenth - 1, 12288).astype(F32), 7.0, x_low, x_high)
    blocks_part = jnp.where(part_ten < 5, part_ten, part_ten + 3)
    stack_y = cut(jnp.where(line < 24, line - 8, 12288).astype(F32), 7.0, y_low, y_high)
    lane_scale = 1.0 / weight_total(plain_z + (gz * 128).astype(F32), 128.0 * nz)

    def build_rows(t, carry):
        rows = pl.ds(pl.multiple_of(t * 16, 16), 16)
        index = lax.broadcasted_iota(jnp.int32, (16, 128), 0) + t * 16
        tile = lax.shift_right_logical(index, 3)
        late = jnp.where(tile >= 20, 2, jnp.where(tile >= 10, 1, 0))
        plane = tile - 10 * late
        x = (plane - 1).astype(F32)
        y = (jnp.bitwise_and(index, 7) - jnp.where(late == 1, 1, jnp.where(late == 2, -1, 0))).astype(F32)
        row_scale[rows, :] = 1.0 / (
            weight_total(x + (gx * 8).astype(F32), 8.0 * nx)
            * weight_total(y + (gy * 8).astype(F32), 8.0 * ny)
        )
        cut_x = cut(x, 7.0, x_low, x_high)
        cut_y = cut(y, 7.0, y_low, y_high)
        wide_x = jnp.concatenate([cut_x] * 3, axis=1)
        wide_y = jnp.concatenate([cut_y] * 3, axis=1)
        weights = hat(wide_x - lanes_x) * hat(wide_y - lanes_y)
        big_l_wide[rows, :] = weights
        big_l[rows, :] = weights.astype(BF16)
        repeated = hat(cut_y - stack_y)
        rep_l_wide[rows, :] = repeated
        rep_l[rows, :] = repeated.astype(BF16)
        block_mask[rows, :] = jnp.where(tenth == plane, 1.0, 0.0)
        return carry

    lax.fori_loop(0, 16, build_rows, 0)

    def turn(tile, j):
        _, b, c = velocities[j]
        if b != 0:
            tile = pltpu.roll(tile, b % 8, 0)
        if c != 0:
            tile = pltpu.roll(tile, c % 128, 1)
        return tile

    def turn_step(x, carry):
        inner = pl.ds(aligned(x + 1), 8)
        for k in range(3):
            for j in range(1, 19):
                turned[k, j - 1, inner, :] = turn(own(k, j, inner), j)
        return carry

    lax.fori_loop(0, 8, turn_step, 0, unroll=2)
    big_lt[...] = big_l_wide[...].T.astype(BF16)
    rep_lt[...] = rep_l_wide[...].T[0:32, :].astype(BF16)

    def build_cross(t, carry):
        rows = pl.ds(pl.multiple_of(t * 16, 16), 16)
        x = cut((t - 8).astype(F32), 7.0, x_low, x_high)
        same = lax.broadcasted_iota(jnp.int32, (16, 128), 0) == blocks_part
        weights = jnp.where(same, hat(x - blocks_x), 0.0)
        wide_x_v[rows, :] = weights
        cross_x[rows, :] = weights.astype(BF16)
        return carry

    lax.fori_loop(0, 24, build_cross, 0)

    def build_z(t, carry):
        rows = pl.ds(pl.multiple_of(t * 16, 16), 16)
        index = lax.broadcasted_iota(jnp.int32, (16, 384), 0) + t * 16
        halo = index - 128
        halo = halo - 10 * lax.shift_right_logical(halo * 205, 11)
        halo = jnp.where(halo < 5, halo - 5, halo + 123)
        z = cut(jnp.where(index < 128, index, halo).astype(F32), 127.0, z_low, z_high)
        weights = hat(z - lanes_z)
        wide_z_v[rows, :] = weights
        cross_z[rows, :] = weights.astype(BF16)
        return carry

    lax.fori_loop(0, 16, build_z, 0)
    cross_xt[...] = wide_x_v[...].T.astype(BF16)
    cross_zt[...] = wide_z_v[...].T.astype(BF16)
    grad_v[...] = jnp.zeros_like(grad_v)

    for copy in field_copies[:6] + field_copies[-2:]:
        copy.wait_recv()
    inner_xy = left_dot(big_l[...], field[...])
    for copy in field_copies[6:-2]:
        copy.wait_recv()
    part = jnp.bitwise_and(lane, 15)
    stacked = []
    for b in (-1, 0, 1):
        tiles = []
        for a in (-1, 0, 1):
            below = z_recv[flow_index[-a, -b, 1], 0]
            above = z_recv[flow_index[-a, -b, -1], 0]
            tiles.append(jnp.where(part < 8, below, above))
        stacked.append(jnp.concatenate(tiles, axis=1))
    stacked.append(jnp.zeros((8, 384), F32))
    halo_x = right_dot(jnp.concatenate(stacked, axis=0), cross_x[...])
    halo_x = jnp.concatenate([halo_x, jnp.zeros((96, 128), F32)], axis=0)
    halo_xy = left_dot(rep_l[...], halo_x) * block_mask[...]
    summed = right_dot(jnp.concatenate([inner_xy, halo_xy], axis=1), cross_z[...])
    scale_rows = jnp.concatenate([row_scale[...]] * 3, axis=1)
    kappa_v[...] = 0.5 * (1.0 - summed * scale_rows * lane_scale)

    for copy in fill_copies[2:]:
        copy.wait_recv()
    for b in (1, -1):
        for s, j in enumerate(crossing[1, b]):
            c = velocities[j][2]
            for k in range(3):
                if c != 0:
                    lines = y_rows[side[b], 5 * k + s, pl.ds(8, 8), :]
                    y_rows[side[b], 5 * k + s, pl.ds(8, 8), :] = pltpu.roll(lines, c % 128, 1)
    eighth = lax.shift_right_logical(lane, 3)
    slot = eighth - jnp.where(eighth >= 10, 10, jnp.where(eighth >= 5, 5, 0))
    for sign in (1, -1):
        base = z_recv[flow_index[0, 0, sign], 1]
        total = base
        for s, j in enumerate(crossing[2, sign]):
            a, b, _ = velocities[j]
            if a != 0:
                corner = z_recv[flow_index[a, 0, sign], 0]
                moved = pltpu.roll(base, a % 128, 1)
                for k in range(3):
                    free = k if a == 1 else 112 + k
                    place = 40 * k + 8 * s + (0 if a == 1 else 7)
                    moved = jnp.where(
                        lane == place, pltpu.roll(corner, (place - free) % 128, 1), moved
                    )
            elif b != 0:
                corner = z_recv[flow_index[0, b, sign], 0]
                moved = jnp.where(row == (0 if b == 1 else 7), corner, pltpu.roll(base, b % 8, 0))
            else:
                continue
            total = jnp.where(slot == s, moved, total)
        z_pack[side[sign]] = total

    def plane_step(x, carry):
        def stream(k, j):
            a, b, c = velocities[j]
            tile = turned[k, j - 1, pl.ds(aligned(x + 1 - a), 8), :]
            if b != 0:
                s = crossing[1, b].index(j)
                line = y_rows[side[b], 5 * k + s, pl.ds(8 + x - a, 1), :]
                tile = jnp.where(row == (0 if b == 1 else 7), line, tile)
            if c != 0:
                s = crossing[2, c].index(j)
                edge = 0 if c == 1 else 127
                place = k * 40 + s * 8 + x
                column = pltpu.roll(
                    z_pack[side[c]], jnp.bitwise_and(256 + edge - place, 127), 1
                )
                tile = jnp.where(lane == edge, column, tile)
            return tile

        def spot(j):
            a, b, c = velocities[j]
            return (
                pl.ds(aligned(kind[b] * 10 + x + 1 - a), 8),
                pl.ds(128 * kind[c], 128),
            )

        center = pl.ds(aligned(x + 1), 8)
        flags = flags_v[pl.ds(aligned(x), 8), :]
        state, slopes = [first_v[0, center, :]], [None]
        weights = [seed_v[0, center, :]] + [None] * 18
        for j in range(1, 19):
            slope = stream(1, j)
            rows, lanes = spot(j)
            change = kappa_v[rows, lanes] * slope
            before = stream(0, j)
            state.append(before + change if j % 2 == 1 else before - change)
            slopes.append(slope)
            weights[opposite[j]] = stream(2, j)
        kappa = kappa_v[center, 0:128]
        back, here = adjoint_collision(state, weights, kappa, flags)
        grad_v[center, 0:128] += here
        for j in range(1, 19):
            rows, lanes = spot(j)
            if j % 2 == 1:
                grad_v[rows, lanes] += slopes[j] * back[j]
            else:
                grad_v[rows, lanes] -= slopes[j] * back[j]
        return carry

    lax.fori_loop(1, 7, plane_step, 0, unroll=6)
    for copy in fill_copies[:2]:
        copy.wait_recv()
    for sign in (1, -1):
        n = side[sign]
        rows = pl.ds(0, 8) if sign == 1 else pl.ds(72, 8)
        for s, j in enumerate(crossing[0, sign]):
            for k in range(3):
                turned[k, j - 1, rows, :] = turn(x_recv[n, 5 * k + s], j)
    for a, b in diagonals:
        j = velocities.index((a, b, 0))
        s = crossing[1, b].index(j)
        start = regions[-a, -b][0]
        for k in range(3):
            y_rows[side[b], 5 * k + s, pl.ds(7 if a == 1 else 16, 1), :] = field[
                pl.ds(start + 25 + k, 1), :
            ]
    lax.fori_loop(0, 2, lambda n, carry: plane_step(7 * n, carry), 0, unroll=2)

    scaled = grad_v[...] * (scale_rows * (-0.5 * lane_scale))
    summed = right_dot(scaled, cross_zt[...])
    spread[...] = left_dot(big_lt[...], summed[:, 0:128])
    spread_copies = []
    for flow in flows:
        a, b, c = flow
        if c == 0:
            spread_copies.append(
                send(spread.at[region(a, b)], spread_recv.at[region(a, b)], flow)
            )
    halo_x = left_dot(rep_lt[...], summed[:, 128:256] * block_mask[...])
    halo = right_dot(halo_x, cross_xt[...])
    for b in range(3):
        for a in range(3):
            q_out[3 * b + a] = halo[8 * b : 8 * b + 8, 128 * a : 128 * a + 128]
    for flow in flows:
        a, b, c = flow
        if c != 0:
            spread_copies.append(
                send(q_out.at[3 * (b + 1) + a + 1], q_recv.at[flow_index[flow]], flow)
            )
    arrived = dict(zip([f for f in flows if f[2] == 0] + [f for f in flows if f[2] != 0], spread_copies))
    for b in (1, -1):
        arrived[0, b, 0].wait_recv()
        for r in range(5):
            y = r if b == 1 else 3 + r
            spread[pl.ds(y, 8, stride=8), :] += spread_recv[
                pl.ds(regions[0, b][0] + 8 * r, 8), :
            ]
    for flow in reversed(flows):
        if flow[2] != 0:
            arrived[flow].wait_recv()
    up = add_all([q_recv[flow_index[a, b, 1]] for a in (-1, 0, 1) for b in (-1, 0, 1)])
    down = add_all([q_recv[flow_index[a, b, -1]] for a in (-1, 0, 1) for b in (-1, 0, 1)])
    for x in range(8):
        first = pltpu.roll(up, (128 - 16 * x - 8) % 128, 1)
        last = pltpu.roll(down, (123 - 16 * x) % 128, 1)
        spread[pl.ds(8 * x, 8), :] += jnp.where(
            lane < 5, first, jnp.where(lane >= 123, last, 0.0)
        )
    arrived[-1, 0, 0].wait_recv()
    spread[pl.ds(24, 40), :] += spread_recv[region(-1, 0), :]
    arrived[1, 0, 0].wait_recv()
    spread[pl.ds(0, 40), :] += spread_recv[region(1, 0), :]
    for a, b in diagonals:
        arrived[a, b, 0].wait_recv()
        for r in range(5):
            y = r if b == 1 else 3 + r
            spread[pl.ds(y + (0 if a == 1 else 24), 5, stride=8), :] += spread_recv[
                pl.ds(regions[a, b][0] + 5 * r, 5), :
            ]
    squares = blank
    for x in range(8):
        tile = spread[pl.ds(8 * x, 8), :]
        squares = squares + tile * tile

    mine = gy * nz + gz
    ring_a[mine] = jnp.sum(squares, axis=0, keepdims=True)
    ring_copies = [send(ring_a.at[mine], ring_a.at[mine], move) for move in slab_moves]
    for copy in reversed(ring_copies):
        copy.wait_recv()
    ring_b[gx] = jnp.sum(ring_a[...], axis=0)
    ring_copies = [send(ring_b.at[gx], ring_b.at[gx], move) for move in line_moves]
    for copy in reversed(ring_copies):
        copy.wait_recv()
    total = jnp.sum(jnp.sum(ring_b[...], axis=0), axis=1, keepdims=True)
    mean_square = total / (8192.0 * nx * ny * nz)
    out_ref[...] = spread[pl.ds(0, 64), :]
    rms_ref[...] = jnp.broadcast_to(mean_square, (8, 128))
    for copy in started:
        copy.wait_send()


def finish(raw_ref, mean_ref, out_ref, rms_ref):
    mean_square = mean_ref[0:1, 0:1]
    out_ref[...] = raw_ref[...] * lax.rsqrt(mean_square + norm_eps)
    rms_ref[...] = jnp.sqrt(mean_square)


def solution(mesh):
    sizes = tuple(mesh.shape[name] for name in ("gx", "gy", "gz"))
    copies = 4 + 2 + 18 + 2 + 2 + 2 + 26 + (sizes[1] * sizes[2] - 1) + (sizes[0] - 1)

    def body(populations, design, flags, adjoint_seed):
        anywhere = pl.BlockSpec(memory_space=pl.ANY)
        inside = pl.BlockSpec(memory_space=pltpu.VMEM)
        scratch = [
            pltpu.VMEM((19, 64, 128), F32),
            pltpu.VMEM((64, 128), jnp.int32),
            pltpu.VMEM((19, 80, 128), F32),
            pltpu.VMEM((9, 80, 128), F32),
            pltpu.VMEM((19, 80, 128), F32),
            pltpu.VMEM((3, 18, 80, 128), F32),
            pltpu.VMEM((384, 128), F32),
            pltpu.VMEM((2, 15, 8, 128), F32),
            pltpu.VMEM((2, 15, 8, 128), F32),
            pltpu.VMEM((2, 40, 128), F32),
            pltpu.VMEM((2, 15, 8, 128), F32),
            pltpu.VMEM((2, 15, 24, 128), F32),
            pltpu.VMEM((4, 32, 128), F32),
            pltpu.VMEM((8, 8, 128), F32),
            pltpu.VMEM((2, 2, 8, 128), F32),
            pltpu.VMEM((26, 2, 8, 128), F32),
            pltpu.VMEM((2, 8, 128), F32),
            pltpu.VMEM((256, 384), F32),
            pltpu.VMEM((256, 384), F32),
            pltpu.VMEM((384, 128), F32),
            pltpu.VMEM((384, 128), F32),
            pltpu.VMEM((9, 8, 128), F32),
            pltpu.VMEM((26, 8, 128), F32),
            pltpu.VMEM((sizes[1] * sizes[2], 1, 128), F32),
            pltpu.VMEM((sizes[0], 1, 128), F32),
            pltpu.VMEM((256, 384), BF16),
            pltpu.VMEM((256, 384), F32),
            pltpu.VMEM((384, 256), BF16),
            pltpu.VMEM((256, 128), BF16),
            pltpu.VMEM((256, 128), F32),
            pltpu.VMEM((32, 256), BF16),
            pltpu.VMEM((384, 128), BF16),
            pltpu.VMEM((256, 384), BF16),
            pltpu.VMEM((128, 384), BF16),
            pltpu.VMEM((384, 256), BF16),
            pltpu.VMEM((384, 128), F32),
            pltpu.VMEM((256, 384), F32),
            pltpu.VMEM((256, 128), F32),
            pltpu.VMEM((256, 128), F32),
            pltpu.SemaphoreType.DMA((5,)),
            pltpu.SemaphoreType.DMA((copies,)),
            pltpu.SemaphoreType.DMA((copies,)),
        ]
        grad, rms = pl.pallas_call(
            functools.partial(kernel, sizes),
            out_shape=(
                jax.ShapeDtypeStruct((64, 128), F32),
                jax.ShapeDtypeStruct((8, 128), F32),
            ),
            in_specs=[anywhere] * 4,
            out_specs=(inside, inside),
            scratch_shapes=scratch,
            compiler_params=pltpu.CompilerParams(
                collective_id=0, has_side_effects=True, vmem_limit_bytes=56491008
            ),
        )(
            populations.reshape(19, 64, 128),
            design.reshape(64, 128),
            flags.reshape(64, 128),
            adjoint_seed.reshape(19, 64, 128),
        )
        grad, rms = pl.pallas_call(
            finish,
            out_shape=(
                jax.ShapeDtypeStruct((64, 128), F32),
                jax.ShapeDtypeStruct((1, 1), F32),
            ),
            in_specs=[inside, inside],
            out_specs=(inside, inside),
            name="scale_gradient",
            compiler_params=pltpu.CompilerParams(vmem_limit_bytes=1024 * 1024),
        )(grad, rms)
        return grad.reshape(8, 8, 128), rms.reshape(())

    return jax.shard_map(
        body,
        mesh=mesh,
        in_specs=(
            P(None, "gx", "gy", "gz"),
            P("gx", "gy", "gz"),
            P("gx", "gy", "gz"),
            P(None, "gx", "gy", "gz"),
        ),
        out_specs=(P("gx", "gy", "gz"), P()),
        check_vma=False,
    )
```
